32 devices in a mesh: grp: 4 (over y, x), batch: 8 (over z, core).
Axes of the slice: x: 2, y: 2, z: 4, core: 2. Of those that a mesh axis runs over, the one named last changes fastest.
Arguments:
- features: bfloat16 [25088, 2048], P('batch', 'grp'), may hold values from -40 to 40
- pixel_mask: int32 [25088], P('batch'), may hold values from 0 to 1, as said below
- out_cotangent: bfloat16 [25088, 2048], P('batch', 'grp'), may hold values from -40 to 40
- reduce_master: float32 [2048, 1024], P(('grp', 'batch')), may hold values from -0.125 to 0.125
- group_master: float32 [288, 1024], P(None, ('grp', 'batch')), may hold values from -0.375 to 0.375
- expand_master: float32 [1024, 2048], P('batch', 'grp'), may hold values from -0.1875 to 0.1875
- norm_params: float32 [4, 1024], P(None, 'grp'), may hold values from -1.5 to 1.5, as said below
- out_params: float32 [2, 2048], P(None, 'grp'), may hold values from -1.5 to 1.5, as said below
- reduce_first: float32 [2048, 1024], P(('grp', 'batch')), may hold values from -0.0007324219 to 0.0007324219
- reduce_second: float32 [2048, 1024], P(('grp', 'batch')), may hold values from 2.2235029e-10 to 8.8940116e-10
- group_first: float32 [288, 1024], P(None, ('grp', 'batch')), may hold values from -0.0007324219 to 0.0007324219
- group_second: float32 [288, 1024], P(None, ('grp', 'batch')), may hold values from 2.2235029e-10 to 8.8940116e-10
- expand_first: float32 [1024, 2048], P('batch', 'grp'), may hold values from -0.0007324219 to 0.0007324219
- expand_second: float32 [1024, 2048], P('batch', 'grp'), may hold values from 2.2235029e-10 to 8.8940116e-10
- norm_first: float32 [4, 1024], P(None, 'grp'), may hold values from -0.0009765625 to 0.0009765625
- norm_second: float32 [4, 1024], P(None, 'grp'), may hold values from 4.4470058e-10 to 1.7788023e-09
- out_first: float32 [2, 2048], P(None, 'grp'), may hold values from -0.0009765625 to 0.0009765625
- out_second: float32 [2, 2048], P(None, 'grp'), may hold values from 4.4470058e-10 to 1.7788023e-09
Outputs:
- block_out: bfloat16 [25088, 2048], P('batch', 'grp')
- input_grad: bfloat16 [25088, 2048], P('batch', 'grp')
- grad_norm: float32 [], replicated
- weight_trust: float32 [3], replicated
- norm_trust: float32 [2], replicated
- reduce_grad: float32 [2048, 1024], P(('grp', 'batch'))
- reduce_first_new: float32 [2048, 1024], P(('grp', 'batch'))
- reduce_second_new: float32 [2048, 1024], P(('grp', 'batch'))
- reduce_new: float32 [2048, 1024], P(('grp', 'batch'))
- reduce_low: bfloat16 [2048, 1024], P(('grp', 'batch'))
- group_grad: float32 [288, 1024], P(None, ('grp', 'batch'))
- group_first_new: float32 [288, 1024], P(None, ('grp', 'batch'))
- group_second_new: float32 [288, 1024], P(None, ('grp', 'batch'))
- group_new: float32 [288, 1024], P(None, ('grp', 'batch'))
- group_low: bfloat16 [288, 1024], P(None, ('grp', 'batch'))
- expand_grad: float32 [1024, 2048], P('batch', 'grp')
- expand_first_new: float32 [1024, 2048], P('batch', 'grp')
- expand_second_new: float32 [1024, 2048], P('batch', 'grp')
- expand_new: float32 [1024, 2048], P('batch', 'grp')
- expand_low: bfloat16 [1024, 2048], P('batch', 'grp')
- norm_grad: float32 [4, 1024], P(None, 'grp')
- norm_first_new: float32 [4, 1024], P(None, 'grp')
- norm_second_new: float32 [4, 1024], P(None, 'grp')
- norm_new: float32 [4, 1024], P(None, 'grp')
- out_grad: float32 [2, 2048], P(None, 'grp')
- out_first_new: float32 [2, 2048], P(None, 'grp')
- out_second_new: float32 [2, 2048], P(None, 'grp')
- out_new: float32 [2, 2048], P(None, 'grp')
The draws below stay inside these ranges and needn't reach their ends.
Inputs may be any that keep to these rules, and one draw needn't show every extreme that they name: `pixel_mask`: each image's valid pixels form the top-left rectangle of its 7 x 7 frame; one side of the rectangle has 7 pixels, the other 3 to 7. `norm_params`: rows 0 and 2 lie in 0.6 to 1.4. `out_params`: row 0 lies in 0.6 to 1.4.
All inputs are finite; a program needn't handle non-finite values.
Results may differ from the reference program's by a relative error of at most 0.025.
Values may be sent and summed in bfloat16 or wider, within the bound.
A program may use at most 192 MiB of HBM per device.

```python
import math
import jax
import jax.numpy as jnp
from jax import lax

C = 2048
W = 1024
GROUPS = 32
GW = 32
SIDE = 7
IMAGES = 512
PIXELS = 25088
NPARAM = 4497408
N_BATCH = 8


def scaled_field(key, width):
    first_key, second_key, third_key = jax.random.split(key, 3)
    image_index = jnp.arange(PIXELS) // (SIDE * SIDE)
    position = image_index.astype(jnp.float32) / IMAGES
    column_place = jnp.arange(width).astype(jnp.float32) / width
    base = jnp.clip(jax.random.normal(first_key, (PIXELS, width), jnp.float32), -5.0, 5.0)
    rising = jnp.exp(1.1 * position)
    ramp = 1.1
    per_image = jnp.exp(jax.random.uniform(second_key, (IMAGES,), jnp.float32, -0.5, 0.5))
    per_column = jnp.exp(jax.random.uniform(third_key, (width,), jnp.float32, -0.3, 0.3)) * jnp.exp(ramp * (column_place - 0.5))
    row_factor = 0.6 * rising * per_image[image_index]
    return base * row_factor[:, None] * per_column[None, :]


def draw_features(key, part):
    return scaled_field(jax.random.fold_in(key, 1), C).astype(jnp.bfloat16)


def draw_out_cotangent(key, part):
    return scaled_field(jax.random.fold_in(key, 2), C).astype(jnp.bfloat16)


def draw_pixel_mask(key, part):
    first_key, second_key = jax.random.split(jax.random.fold_in(key, 3))
    upright = jax.random.randint(first_key, (IMAGES,), 0, 2)
    shorter = jax.random.randint(second_key, (IMAGES,), 3, SIDE + 1)
    row_count = jnp.where(upright == 1, SIDE, shorter)
    col_count = jnp.where(upright == 1, shorter, SIDE)
    places = jnp.arange(SIDE * SIDE)
    valid = (places[None, :] // SIDE < row_count[:, None]) & (places[None, :] % SIDE < col_count[:, None])
    return valid.astype(jnp.int32).reshape(PIXELS)


def gains_biases(key, rows, width):
    first_key, second_key = jax.random.split(key)
    column_place = jnp.arange(width).astype(jnp.float32) / width
    jitter = jax.random.uniform(first_key, (rows, width), jnp.float32, 0.0, 0.1)
    gains = 0.6 + 0.7 * column_place[None, :] + jitter
    biases = jnp.clip(0.3 * jax.random.normal(second_key, (rows, width), jnp.float32), -1.5, 1.5)
    return (gains, biases)


def draw_norm_params(key, part):
    gains, biases = gains_biases(jax.random.fold_in(key, 4), 2, W)
    return jnp.stack([gains[0], biases[0], gains[1], biases[1]])


def draw_out_params(key, part):
    gains, biases = gains_biases(jax.random.fold_in(key, 5), 1, C)
    return jnp.stack([gains[0], biases[0]])


def block_scale(key, extent, cuts, smallest, high):
    loudness, own = 1.0, jax.random.fold_in(key, 6)
    for axis_at, parts in cuts:
        draws = jnp.exp(jax.random.uniform(jax.random.fold_in(own, axis_at), (parts,), jnp.float32, smallest / len(cuts), high / len(cuts)))
        loudness = loudness * jnp.repeat(draws, extent[axis_at] // parts).reshape([-1 if axis == axis_at else 1 for axis in range(len(extent))])
    return loudness


def scatter_about(stream_key, extent, spread, bound, cuts=(), kind=jnp.bfloat16):
    entries = spread * jax.random.normal(stream_key, extent, jnp.float32)
    if cuts:
        entries = entries * block_scale(stream_key, extent, cuts, -0.22, 0.18)
    return jnp.clip(entries, -bound, bound).astype(kind)


def setup_inputs(seed: int = 0) -> dict:
    arg_keys = jax.random.split(jax.random.key(seed), 19)
    return {
        "features": draw_features(jax.random.fold_in(arg_keys[18], 71), 0),
        "pixel_mask": draw_pixel_mask(jax.random.fold_in(arg_keys[18], 71), 0),
        "out_cotangent": draw_out_cotangent(jax.random.fold_in(arg_keys[18], 71), 0),
        "reduce_master": scatter_about(arg_keys[3], (C, W), C ** -0.5, 0.125, ((0, 32),), jnp.float32),
        "group_master": scatter_about(arg_keys[4], (9 * GW, W), (9 * GW) ** -0.5, 0.375, ((1, 32),), jnp.float32),
        "expand_master": scatter_about(arg_keys[5], (W, C), W ** -0.5, 0.1875, ((0, 8), (1, 4)), jnp.float32),
        "norm_params": draw_norm_params(jax.random.fold_in(arg_keys[18], 71), 0),
        "out_params": draw_out_params(jax.random.fold_in(arg_keys[18], 71), 0),
        "reduce_first": scatter_about(arg_keys[8], (C, W), (0.11 / NPARAM ** 0.5), 0.0007324219, ((0, 32),), jnp.float32),
        "reduce_second": jnp.clip(jnp.exp(math.log(8.894011638282961e-10) - 1.3862944 * jax.random.uniform(arg_keys[9], (C, W), jnp.float32) ** block_scale(arg_keys[9], (C, W), ((0, 32),), -0.2, 0.2)), 2.2235029095707404e-10, 8.894011638282961e-10),
        "group_first": scatter_about(arg_keys[10], (9 * GW, W), (0.11 / NPARAM ** 0.5), 0.0007324219, ((1, 32),), jnp.float32),
        "group_second": jnp.clip(jnp.exp(math.log(8.894011638282961e-10) - 1.3862944 * jax.random.uniform(arg_keys[11], (9 * GW, W), jnp.float32) ** block_scale(arg_keys[11], (9 * GW, W), ((1, 32),), -0.2, 0.2)), 2.2235029095707404e-10, 8.894011638282961e-10),
        "expand_first": scatter_about(arg_keys[12], (W, C), (0.11 / NPARAM ** 0.5), 0.0007324219, ((0, 8), (1, 4)), jnp.float32),
        "expand_second": jnp.clip(jnp.exp(math.log(8.894011638282961e-10) - 1.3862944 * jax.random.uniform(arg_keys[13], (W, C), jnp.float32) ** block_scale(arg_keys[13], (W, C), ((0, 8), (1, 4)), -0.2, 0.2)), 2.2235029095707404e-10, 8.894011638282961e-10),
        "norm_first": scatter_about(arg_keys[14], (4, W), (0.16 / NPARAM ** 0.5), 0.0009765625, ((1, 4),), jnp.float32),
        "norm_second": jnp.clip(jnp.exp(math.log(1.7788023276565923e-09) - 1.3862944 * jax.random.uniform(arg_keys[15], (4, W), jnp.float32) ** block_scale(arg_keys[15], (4, W), ((1, 4),), -0.2, 0.2)), 4.447005819141481e-10, 1.7788023276565923e-09),
        "out_first": scatter_about(arg_keys[16], (2, C), (0.16 / NPARAM ** 0.5), 0.0009765625, ((1, 4),), jnp.float32),
        "out_second": jnp.clip(jnp.exp(math.log(1.7788023276565923e-09) - 1.3862944 * jax.random.uniform(arg_keys[17], (2, C), jnp.float32) ** block_scale(arg_keys[17], (2, C), ((1, 4),), -0.2, 0.2)), 4.447005819141481e-10, 1.7788023276565923e-09),
    }


@jax.custom_vjp
def low(v):
    return lax.optimization_barrier(v.astype(jnp.bfloat16)).astype(jnp.float32)

@jax.custom_vjp
def low_back(v):
    return v

def low_keep(v):
    return (low(v), None)

def low_pass(kept, grad):
    return (grad,)

def back_keep(v):
    return (v, None)

def back_low(kept, grad):
    return (low(grad),)
low.defvjp(low_keep, low_pass)
low_back.defvjp(back_keep, back_low)
eps_norm = 1e-05
beta_one = 0.9
beta_two = 0.999
adam_eps = 1e-08
learn_rate = 0.25
step_count = 10.0
clip_norm = 1.0
highest = lax.Precision.HIGHEST

def smooth_act(values):
    return values * jax.nn.sigmoid(values)

def masked_norm(values, validity, gain_row, bias_row, counted):
    centre = lax.optimization_barrier(jnp.sum(values * validity[:, None], axis=0)) / counted
    centred = values - centre
    variance = lax.optimization_barrier(jnp.sum(centred * centred * validity[:, None], axis=0)) / counted
    return centred * lax.rsqrt(variance + eps_norm) * gain_row + bias_row

def group_conv(values, weight):
    tap_rows = weight.reshape(9, GW, GROUPS, GW)
    blocks = values.reshape(N_BATCH, IMAGES // N_BATCH, SIDE, SIDE, GROUPS, GW)

    def one_block(images):
        padded = jnp.pad(images, ((0, 0), (1, 1), (1, 1), (0, 0), (0, 0)))
        totals = jnp.zeros(images.shape, jnp.float32)
        for tap_row in range(3):
            for tap_col in range(3):
                pieces = padded[:, tap_row:tap_row + SIDE, tap_col:tap_col + SIDE]
                totals = totals + jnp.einsum('nhwgi,igo->nhwgo', pieces, tap_rows[3 * tap_row + tap_col], precision=highest)
        return totals
    return lax.map(jax.checkpoint(one_block), blocks).reshape(values.shape)

def forward(source, validity, reduce_w, group_w, expand_w, norm_rows, out_rows):
    counted = jnp.sum(validity)
    columns = validity[:, None]
    z_reduce = low_back(jnp.dot(source, low(reduce_w), precision=highest))
    pre_one = masked_norm(z_reduce, validity, norm_rows[0], norm_rows[1], counted)
    act_one = low(smooth_act(pre_one) * columns)
    z_group = low_back(group_conv(act_one, low(group_w)))
    pre_two = masked_norm(z_group, validity, norm_rows[2], norm_rows[3], counted)
    act_two = low(smooth_act(pre_two) * columns)
    z_expand = low_back(jnp.dot(act_two, low(expand_w), precision=highest))
    summed = masked_norm(z_expand, validity, out_rows[0], out_rows[1], counted) + source
    return smooth_act(summed) * columns

def adam_direction(tensor, clipped, moment_one, moment_two, decay_rate):
    new_first = beta_one * moment_one + (1.0 - beta_one) * clipped
    new_second = beta_two * moment_two + (1.0 - beta_two) * clipped * clipped
    first_hat = new_first / (1.0 - beta_one ** step_count)
    second_hat = new_second / (1.0 - beta_two ** step_count)
    direction = first_hat / (jnp.sqrt(second_hat) + adam_eps) + decay_rate * tensor
    return (new_first, new_second, direction)

def reference(features, pixel_mask, out_cotangent, reduce_master, group_master, expand_master, norm_params, out_params, reduce_first, reduce_second, group_first, group_second, expand_first, expand_second, norm_first, norm_second, out_first, out_second):
    source = features.astype(jnp.float32)
    validity = pixel_mask.astype(jnp.float32)

    def wrapped(source_in, reduce_w, group_w, expand_w, norm_rows, out_rows):
        return forward(source_in, validity, reduce_w, group_w, expand_w, norm_rows, out_rows)
    block_value, pullback = jax.vjp(wrapped, source, reduce_master, group_master, expand_master, norm_params, out_params)
    gradients = pullback(out_cotangent.astype(jnp.float32))
    block_out = block_value.astype(jnp.bfloat16)
    input_grad = gradients[0].astype(jnp.bfloat16)
    raw_grads = gradients[1:]
    square_total = jnp.zeros((), jnp.float32)
    for raw_grad in raw_grads:
        square_total = square_total + jnp.sum(raw_grad * raw_grad)
    grad_norm = jnp.sqrt(square_total)
    factor = jnp.minimum(1.0, clip_norm / grad_norm)
    tensors = (reduce_master, group_master, expand_master, norm_params, out_params)
    moments_one = (reduce_first, group_first, expand_first, norm_first, out_first)
    moments_two = (reduce_second, group_second, expand_second, norm_second, out_second)
    decays = (0.01, 0.01, 0.01, 0.0, 0.0)
    results = []
    weight_sq = []
    step_sq = []
    for tensor, raw_grad, moment_one, moment_two, decay_rate in zip(tensors, raw_grads, moments_one, moments_two, decays):
        clipped = factor * raw_grad
        new_first, new_second, direction = adam_direction(tensor, clipped, moment_one, moment_two, decay_rate)
        results.append((clipped, new_first, new_second, direction))
        weight_sq.append(jnp.sum(tensor * tensor))
        step_sq.append(jnp.sum(direction * direction))
    trust_ratios = jnp.sqrt(jnp.stack(weight_sq)) * lax.rsqrt(jnp.stack(step_sq) + 1e-06)
    updated = []
    for number in range(5):
        updated.append(tensors[number] - learn_rate * trust_ratios[number] * results[number][3])
    return (block_out, input_grad, grad_norm, trust_ratios[:3], trust_ratios[3:], results[0][0], results[0][1], results[0][2], updated[0], updated[0].astype(jnp.bfloat16), results[1][0], results[1][1], results[1][2], updated[1], updated[1].astype(jnp.bfloat16), results[2][0], results[2][1], results[2][2], updated[2], updated[2].astype(jnp.bfloat16), results[3][0], results[3][1], results[3][2], updated[3], results[4][0], results[4][1], results[4][2], updated[4])
```

```python
import functools

import jax
import jax.numpy as jnp
from jax import lax
from jax.experimental import pallas as pl
from jax.experimental.pallas import tpu as pltpu
from jax.sharding import PartitionSpec as P

GW = 32
SIDE = 7
HW = SIDE * SIDE
BLK = 256

eps_norm = 1e-05
beta_one = 0.9
beta_two = 0.999
adam_eps = 1e-08
learn_rate = 0.25
step_count = 10.0
clip_norm = 1.0

MESH = pl.DeviceIdType.MESH
F32 = jnp.float32
BF16 = jnp.bfloat16
VMEM_LIMIT = 60 * 1024 * 1024


def params(**more):
    return pltpu.CompilerParams(vmem_limit_bytes=VMEM_LIMIT, **more)


def dot(a, b):
    return jnp.dot(a, b, preferred_element_type=F32)


def dot_left(a, b):
    return lax.dot_general(a, b, (((0,), (0,)), ((), ())), preferred_element_type=F32)


def dot_right(a, b):
    return lax.dot_general(a, b, (((1,), (1,)), ((), ())), preferred_element_type=F32)


def sigmoid(v):
    return 0.5 + 0.5 * jnp.tanh(0.5 * v)


def to_inner(rows, images):
    to = lax.broadcasted_iota(jnp.int32, (rows, rows), 0)
    source = (to % images) * HW + to // images
    at = lax.broadcasted_iota(jnp.int32, (rows, rows), 1)
    return jnp.where(at == source, 1.0, 0.0).astype(BF16)


def to_outer(rows, images):
    to = lax.broadcasted_iota(jnp.int32, (rows, rows), 0)
    source = (to % HW) * images + to // HW
    at = lax.broadcasted_iota(jnp.int32, (rows, rows), 1)
    return jnp.where(at == source, 1.0, 0.0).astype(BF16)


def wide(mask, columns):
    return jnp.concatenate([mask] * (columns // 128), axis=1)


def peers(axis):
    size = lax.axis_size(axis)
    mine = lax.axis_index(axis)
    return [{axis: lax.rem(mine + other, size)} for other in range(1, size)]


def greet(groups):
    barrier = pltpu.get_barrier_semaphore()
    for peer in groups:
        pl.semaphore_signal(barrier, inc=1, device_id=peer, device_id_type=MESH)


def greeted(groups):
    pl.semaphore_wait(pltpu.get_barrier_semaphore(), len(groups))


def everyone():
    return peers("grp") + peers("batch")


def sums_scratch(rows, columns):
    grp, batch = lax.axis_size("grp"), lax.axis_size("batch")
    return [
        pltpu.VMEM((grp - 1, rows, columns), F32),
        pltpu.VMEM((batch - 1, rows, columns), F32),
        pltpu.VMEM((rows, columns), F32),
        pltpu.SemaphoreType.DMA((grp - 1,)),
        pltpu.SemaphoreType.DMA((grp - 1,)),
        pltpu.SemaphoreType.DMA((batch - 1,)),
        pltpu.SemaphoreType.DMA((batch - 1,)),
    ]


def add_rows(parts):
    return functools.reduce(jnp.add, parts)


def merge_stats(parts):
    count = add_rows([part[2:3] for part in parts])
    total = add_rows([part[0:1] for part in parts])
    centre = total / count
    spread = add_rows([part[1:2] + part[2:3] * (part[0:1] / part[2:3] - centre) ** 2 for part in parts])
    return jnp.concatenate([total, spread, count], axis=0)


def over_devices(source, scratch, merge):
    first, second, mid, *sems = scratch
    copies = []
    for axis, slots, send, recv in (("grp", first, sems[0], sems[1]), ("batch", second, sems[2], sems[3])):
        here = []
        for number, peer in enumerate(peers(axis)):
            copy = pltpu.make_async_remote_copy(
                source, slots.at[number], send.at[number], recv.at[number], device_id=peer, device_id_type=MESH
            )
            copy.start()
            here.append(copy)
        for copy in here:
            copy.wait_recv()
        copies += here
        merged = merge([source[...]] + [slots[number] for number in range(len(here))])
        if axis == "grp":
            mid[...] = merged
            source = mid
    for copy in copies:
        copy.wait_send()
    return merged


def norm_rows(merged):
    total, spread, count = merged[0:1], merged[1:2], merged[2:3]
    return jnp.concatenate([total / count, lax.rsqrt(spread / count + eps_norm), count], axis=0)


def clear_edges(col, images, reverse):
    for tap_row in range(3):
        for tap_col in range(3):
            tap = 3 * tap_row + tap_col
            dy, dx = (1 - tap_row, 1 - tap_col) if reverse else (tap_row - 1, tap_col - 1)
            for row in range(SIDE):
                for column in range(SIDE):
                    inside = 0 <= row + dy < SIDE and 0 <= column + dx < SIDE
                    if not inside:
                        at = (row * SIDE + column) * images
                        col[at : at + images, tap * BLK : (tap + 1) * BLK] = jnp.zeros((images, BLK), BF16)


def spread_row(col, value, row, images, reverse):
    for tap_row in range(3):
        for tap_col in range(3):
            tap = 3 * tap_row + tap_col
            dy, dx = (1 - tap_row, 1 - tap_col) if reverse else (tap_row - 1, tap_col - 1)
            to_row = row - dy
            if not 0 <= to_row < SIDE:
                continue
            first = max(0, dx)
            last = min(SIDE, SIDE + dx)
            at = (to_row * SIDE + first - dx) * images
            col[at : at + (last - first) * images, tap * BLK : (tap + 1) * BLK] = value[first * images : last * images]


class Links:
    def __init__(self, send, recv, local):
        self.send_sems, self.recv_sems, self.local_sems = send, recv, local
        self.sent = self.moved = 0
        self.open_sends, self.open_moves = [], []

    def send(self, source, target, peer):
        at = self.sent
        self.sent += 1
        copy = pltpu.make_async_remote_copy(
            source, target, self.send_sems.at[at], self.recv_sems.at[at], device_id=peer, device_id_type=MESH
        )
        copy.start()
        self.open_sends.append(copy)
        return copy

    def move(self, source, target, keep=True):
        copy = pltpu.make_async_copy(source, target, self.local_sems.at[self.moved])
        self.moved += 1
        copy.start()
        if keep:
            self.open_moves.append(copy)
        return copy

    def close(self):
        for copy in self.open_sends:
            copy.wait_send()
        for copy in self.open_moves:
            copy.wait()


def arrived(copies):
    for copy in copies:
        copy.wait_recv()


class Place:
    def __init__(self):
        grp, batch = lax.axis_size("grp"), lax.axis_size("batch")
        self.grp, self.lines = grp, batch // 2
        self.me, self.mine = lax.axis_index("grp"), lax.axis_index("batch")
        self.core, self.line = lax.rem(self.mine, 2), self.mine // 2
        self.sibling = {"batch": self.mine + 1 - 2 * self.core}
        self.across = peers("grp")
        self.along = [{"batch": self.next_line(k) * 2 + self.core} for k in range(1, self.lines)]
        self.far = {"batch": (self.line + 2 - 4 * (self.line // 2)) * 2 + self.core}
        self.near = {"batch": (self.line + 1 - 2 * lax.rem(self.line, 2)) * 2 + self.core}

    def next_grp(self, k):
        return lax.rem(self.me + k, self.grp)

    def next_line(self, k):
        return lax.rem(self.line + k, self.lines)


def aligned(at, size):
    return pl.ds(pl.multiple_of(at, size), size)


def block_weights(wg_ref, number, blocks):
    lanes = lax.broadcasted_iota(jnp.int32, (GW, 128), 1) // GW
    zero = jnp.zeros((GW, 128), BF16)
    for group in range(BLK // GW):
        for tap in range(9):
            piece = wg_ref[number, group // 2, group % 2, (tap // 4) * GW : (tap // 4 + 1) * GW].astype(F32)
            turn = ((group - tap) % 4) * GW
            if turn:
                piece = pltpu.roll(piece, turn, 1)
            piece = jnp.where(lanes == group % 4, piece, 0.0).astype(BF16)
            row = tap * BLK + group * GW
            left = (group // 4) * 128
            blocks[row : row + GW, left : left + 128] = piece
            blocks[row : row + GW, 128 - left : 256 - left] = zero


def block_stats(z_ref, left, columns, m_ref, st_ref, step):
    rows = z_ref.shape[0]
    for part in range(0, columns, BLK):
        span = pl.ds(pl.multiple_of(left + part, BLK), BLK)
        total = jnp.zeros((1, BLK), F32)
        count = jnp.zeros((1, 128), F32)
        for at in range(0, rows, step):
            mask = m_ref[at : at + step]
            total += jnp.sum(z_ref[at : at + step, span] * wide(mask, BLK), axis=0, keepdims=True)
            count += jnp.sum(mask, axis=0, keepdims=True)
        count = wide(count, BLK)
        centre = total / count
        spread = jnp.zeros((1, BLK), F32)
        for at in range(0, rows, step):
            off = (z_ref[at : at + step, span] - centre) * wide(m_ref[at : at + step], BLK)
            spread += jnp.sum(off * off, axis=0, keepdims=True)
        st_ref[0:1, span] = total
        st_ref[1:2, span] = spread
        st_ref[2:3, span] = count


def smooth(pre, mask):
    sigma = sigmoid(pre)
    masked = sigma * mask
    return pre * masked, masked * (1.0 + pre * (1.0 - sigma))


FWD_OUTS = ("inner", "x1", "act1", "slope1", "x2", "act2", "slope2", "x3", "grads", "outs", "wr", "we", "wg")


def forward_kernel(*refs, images, gather):
    (feat, cotg, m_ref, np_ref, op_ref, wr_in, we_in, wg_in) = refs[:8]
    big = dict(zip(FWD_OUTS, refs[8:21]))
    n1, n2, n3, norm_all, out_all, sums3 = refs[21:27]
    (inner, x1, act1, slope1, x2, act2, slope2, x3, grads, land_f, wr, we, wg) = refs[27:40]
    (land_c, cot, perm, back, z1, ze, col, blocks, st1, st2, st3, st4, send, recv, moves) = refs[40:55]
    ex1, ex2, ex3, ex4 = (refs[55 + 7 * k : 62 + 7 * k] for k in range(4))
    held = dict(zip(FWD_OUTS, (inner, x1, act1, slope1, x2, act2, slope2, x3, grads, land_f, wr, we, wg)))
    here = Place()
    grp = here.grp
    rows, own_in = land_f.shape[1:]
    width, channels = z1.shape[1], ze.shape[1]
    own_width = np_ref.shape[1]
    step = SIDE * images
    links = Links(send, recv, moves)

    greet(everyone())
    own_rows = aligned(here.me * rows, rows)
    own_f = links.move(feat.at[own_rows], land_f.at[0], keep=False)
    if gather:
        wr[here.me, here.line, here.core] = wr_in[...]
        we[here.me, here.line, here.core] = we_in[...]
        wg[here.me, here.line, here.core] = wg_in[...]
        loads = []
    else:
        loads = [links.move(wr_in, wr, keep=False), links.move(we_in, we, keep=False), links.move(wg_in, wg, keep=False)]
    norm_all[:, aligned(here.me * own_width, own_width)] = np_ref[...]
    out_all[:, aligned(here.me * own_in, own_in)] = op_ref[...]
    greeted(everyone())

    def spread_out(buffer, targets, rows=slice(None)):
        place = buffer.at[here.me, here.line, here.core, rows]
        return [links.send(place, place, peer) for peer in targets]

    if gather:
        wr_a = spread_out(wr, here.across)
        wg_a = spread_out(wg, here.across)
    small = []
    for k in range(1, grp):
        peer = here.across[k - 1]
        span = aligned(here.me * own_width, own_width)
        small.append(links.send(np_ref, norm_all.at[:, span], peer))
        span = aligned(here.me * own_in, own_in)
        small.append(links.send(op_ref, out_all.at[:, span], peer))
    from_f = {}
    for k in range(1, grp):
        source = feat.at[aligned(here.next_grp(k) * rows, rows)]
        from_f[grp - k] = links.send(source, land_f.at[grp - k], here.across[k - 1])
    own_c = links.move(cotg.at[own_rows], land_c.at[0], keep=False)
    if gather:
        arrived(wr_a)
        wr_b = [links.send(wr.at[:, here.line, here.core], wr.at[:, here.line, here.core], here.sibling)]
        wr_l = [links.send(wr.at[:, here.line, here.core], wr.at[:, here.line, here.core], peer) for peer in here.along]
        arrived(wg_a)
        wg_b = [links.send(wg.at[:, here.line, here.core], wg.at[:, here.line, here.core], peer) for peer in here.along]
    perm[...] = to_inner(rows, images)
    back[...] = to_outer(rows, images)
    own_f.wait()
    for number in range(grp):
        if number:
            from_f[number].wait_recv()
        span = aligned(here.next_grp(number) * own_in, own_in)
        inner[:, span] = dot(perm[...], land_f[number]).astype(BF16)
    if gather:
        for k in range(1, here.lines):
            wr_l[k - 1].wait_recv()
            line = here.next_line(here.lines - k)
            wr_b.append(links.send(wr.at[:, line, here.core], wr.at[:, line, here.core], here.sibling))
        arrived(wg_b)
        wg_c = [links.send(wg.at[:, :, here.core], wg.at[:, :, here.core], here.sibling)]
        arrived(wr_b)
    for copy in loads:
        copy.wait()
    links.move(inner, big["inner"])

    if gather:
        half = we.shape[3] // 2
        lower, upper = pl.ds(0, half), pl.ds(half, half)
        we_a0 = spread_out(we, here.across, lower)
        we_a1 = spread_out(we, here.along, upper)
    from_c = {}
    for k in range(1, grp):
        source = cotg.at[aligned(here.next_grp(k) * rows, rows)]
        from_c[grp - k] = links.send(source, land_c.at[grp - k], here.across[k - 1])

    steps = width // BLK

    @pl.loop(0, steps)
    def _(number):
        span = aligned(number * BLK, BLK)
        z1[:, span] = dot(inner[...], wr[:, :, :, :, span].reshape(channels, BLK))
        block_stats(z1, number * BLK, BLK, m_ref, st1, step)

    links.move(wr, big["wr"])
    if gather:
        arrived(we_a0)
        arrived(we_a1)
        we_b = [
            links.send(we.at[:, here.line, here.core, lower], we.at[:, here.line, here.core, lower], peer)
            for peer in here.along
        ] + [
            links.send(we.at[here.me, :, here.core, upper], we.at[here.me, :, here.core, upper], peer)
            for peer in here.across
        ]
        arrived(wg_c)
    arrived(small)
    n1[...] = norm_rows(over_devices(st1, ex1, merge_stats))

    clear_edges(col, images, False)

    @pl.loop(0, steps)
    def _(number):
        span = aligned(number * BLK, BLK)
        block_weights(wg, number, blocks)
        centre, scale = n1[0:1, span], n1[1:2, span]
        gain, bias = norm_all[0:1, span], norm_all[1:2, span]
        for row in range(SIDE):
            at = row * step
            mask = wide(m_ref[at : at + step], BLK)
            normed = (z1[at : at + step, span] - centre) * scale
            value, slope = smooth(normed * gain + bias, mask)
            act = value.astype(BF16)
            x1[at : at + step, span] = normed.astype(BF16)
            act1[at : at + step, span] = act
            slope1[at : at + step, span] = slope.astype(BF16)
            spread_row(col, act, row, images, False)
        z1[:, span] = dot(col[...], blocks[...])
        block_stats(z1, number * BLK, BLK, m_ref, st2, step)

    for name in ("x1", "act1", "slope1", "wg"):
        links.move(held[name], big[name])
    if gather:
        arrived(we_b)
        we_c = [links.send(we.at[:, :, here.core], we.at[:, :, here.core], here.sibling)]
    n2[...] = norm_rows(over_devices(st2, ex2, merge_stats))

    @pl.loop(0, steps)
    def _(number):
        span = aligned(number * BLK, BLK)
        for at in range(0, rows, step):
            mask = wide(m_ref[at : at + step], BLK)
            normed = (z1[at : at + step, span] - n2[0:1, span]) * n2[1:2, span]
            value, slope = smooth(normed * norm_all[2:3, span] + norm_all[3:4, span], mask)
            x2[at : at + step, span] = normed.astype(BF16)
            act2[at : at + step, span] = value.astype(BF16)
            slope2[at : at + step, span] = slope.astype(BF16)

    for name in ("x2", "act2", "slope2"):
        links.move(held[name], big[name])
    if gather:
        arrived(we_c)
    links.move(we, big["we"])

    @pl.loop(0, grp)
    def _(number):
        for part in range(0, own_in, BLK):
            span = pl.ds(pl.multiple_of(number * own_in + part, BLK), BLK)
            ze[:, span] = dot(act2[...], we[number, :, :, :, part : part + BLK].reshape(width, BLK))
        block_stats(ze, number * own_in, own_in, m_ref, st3, step)

    n3[...] = norm_rows(over_devices(st3, ex3, merge_stats))
    own_c.wait()
    arrived([from_c[number] for number in range(1, grp)])

    @pl.loop(0, grp)
    def _(number):
        slot = lax.rem(number + grp - here.me, grp)
        cot[...] = dot(perm[...], land_c[slot])
        for part in range(0, own_in, BLK):
            span = pl.ds(pl.multiple_of(number * own_in + part, BLK), BLK)
            local = slice(part, part + BLK)
            bias_grad = jnp.zeros((1, BLK), F32)
            gain_grad = jnp.zeros((1, BLK), F32)
            for at in range(0, rows, step):
                mask = wide(m_ref[at : at + step], BLK)
                normed = (ze[at : at + step, span] - n3[0:1, span]) * n3[1:2, span]
                summed = normed * out_all[0:1, span] + out_all[1:2, span] + inner[at : at + step, span].astype(F32)
                value, slope = smooth(summed, mask)
                grad = cot[at : at + step, local] * slope
                x3[at : at + step, span] = normed.astype(BF16)
                col[at : at + step, local] = value.astype(BF16)
                grads[at : at + step, span] = grad.astype(BF16)
                bias_grad += jnp.sum(grad, axis=0, keepdims=True)
                gain_grad += jnp.sum(grad * normed, axis=0, keepdims=True)
            st4[0:1, span] = bias_grad
            st4[1:2, span] = gain_grad
        land_f[slot] = dot(back[...], col[:, 0:own_in]).astype(BF16)

    for name in ("x3", "grads", "outs"):
        links.move(held[name], big[name])
    sums3[...] = over_devices(st4, ex4, add_rows)
    links.close()


def forward(features, out_cotangent, mask, norm_params, out_params, reduce_w, expand_w, group_w, gather):
    grp = lax.axis_size("grp")
    rows = features.shape[0] // grp
    own_in = features.shape[1]
    channels = own_in * grp
    width = norm_params.shape[1] * grp
    lines, cores = (lax.axis_size("batch") // 2, 2) if gather else (1, 1)
    r_shape = (grp, lines, cores, own_in // (lines * cores), width)
    e_shape = (grp, lines, cores, width // (lines * cores), own_in)
    g_shape = (width // BLK, BLK // GW // 2, 2, 3 * GW, 128)
    across = (rows, width)
    shapes = {
        "inner": (rows, channels),
        "x1": across,
        "act1": across,
        "slope1": across,
        "x2": across,
        "act2": across,
        "slope2": across,
        "x3": (rows, channels),
        "grads": (rows, channels),
        "outs": (grp, rows, own_in),
        "wr": r_shape,
        "we": e_shape,
        "wg": g_shape,
    }
    small = [(3, width), (3, width), (3, channels), (4, width), (2, channels), (2, channels)]
    vmem = pl.BlockSpec(memory_space=pltpu.VMEM)
    hbm = pl.BlockSpec(memory_space=pl.ANY)
    if gather:
        weights = (reduce_w, expand_w, group_w)
    else:
        weights = (reduce_w.reshape(r_shape), expand_w.reshape(e_shape), group_w.reshape(g_shape))
    results = pl.pallas_call(
        functools.partial(forward_kernel, images=rows // HW, gather=gather),
        out_shape=[jax.ShapeDtypeStruct(shapes[name], BF16) for name in FWD_OUTS]
        + [jax.ShapeDtypeStruct(shape, F32) for shape in small],
        in_specs=[hbm, hbm, vmem, vmem, vmem] + [vmem if gather else hbm] * 3,
        out_specs=[hbm] * len(FWD_OUTS) + [vmem] * len(small),
        scratch_shapes=[pltpu.VMEM(shapes[name], BF16) for name in FWD_OUTS]
        + [
            pltpu.VMEM((grp, rows, own_in), BF16),
            pltpu.VMEM((rows, own_in), F32),
            pltpu.VMEM((rows, rows), BF16),
            pltpu.VMEM((rows, rows), BF16),
            pltpu.VMEM(across, F32),
            pltpu.VMEM((rows, channels), F32),
            pltpu.VMEM((rows, 9 * BLK), BF16),
            pltpu.VMEM((9 * BLK, BLK), BF16),
            pltpu.VMEM((3, width), F32),
            pltpu.VMEM((3, width), F32),
            pltpu.VMEM((3, channels), F32),
            pltpu.VMEM((2, channels), F32),
            pltpu.SemaphoreType.DMA((64,)),
            pltpu.SemaphoreType.DMA((64,)),
            pltpu.SemaphoreType.DMA((20,)),
        ]
        + sums_scratch(3, width)
        + sums_scratch(3, width)
        + sums_scratch(3, channels)
        + sums_scratch(2, channels),
        compiler_params=params(collective_id=1, has_side_effects=True),
    )(features, out_cotangent, mask, norm_params, out_params, *weights)
    return dict(zip(FWD_OUTS, results)), results[len(FWD_OUTS) :]


def packed_groups(weight):
    groups = weight.shape[1] // GW
    taps = jnp.pad(weight.reshape(9, GW, groups, GW), ((0, 3), (0, 0), (0, 0), (0, 0)))
    return taps.reshape(3, 4, GW, groups, GW).transpose(3, 0, 2, 1, 4).reshape(groups, 3 * GW, 4 * GW)


BWD_INS = ("grads", "x3", "we", "act2", "slope2", "x2", "act1", "slope1", "x1", "wg", "wr")


def backward_kernel(*refs, images, owners):
    outs_in, inner_in = refs[:2]
    given = dict(zip(BWD_INS, refs[2:13]))
    m_ref, n1, n2, n3, norm_all, out_all, sums3 = refs[13:20]
    block_out, input_grad, reduce_out, expand_out, group_out, sums1, sums2 = refs[20:27]
    (grads, x3, we, act2, slope2, x2, act1, slope1, x1, wg, wr) = refs[27:38]
    held = dict(zip(BWD_INS, (grads, x3, we, act2, slope2, x2, act1, slope1, x1, wg, wr)))
    (ge, dp, col, blocks, turned, grad_in, back, st1, st2, raw_e, raw_r, raw_g, send, recv, moves) = refs[38:53]
    ex1, ex2 = refs[53:60], refs[60:67]
    here = Place()
    me, grp, core, line, lines = here.me, here.grp, here.core, here.line, here.lines
    rows, width = dp.shape
    channels = grads.shape[1]
    own_in = channels // grp
    step = SIDE * images
    steps = width // BLK
    links = Links(send, recv, moves)
    if owners:
        (e1, e2, e3, r1, r2, r3, g1, g2, g3, g4, gs1, gs2, gs3) = refs[67:]

    greet(everyone())
    loads = {name: links.move(given[name], held[name], keep=False) for name in BWD_INS}
    own_rows = aligned(me * rows, rows)
    links.move(outs_in.at[0], block_out.at[own_rows])
    back[...] = to_outer(rows, images)
    greeted(everyone())
    out_sends = [
        links.send(outs_in.at[k], block_out.at[own_rows], here.across[k - 1]) for k in range(1, grp)
    ]

    def core_swap(raw, slot):
        return links.send(raw.at[:, :, 1 - core], slot, here.sibling)

    def add_core(raw, slot):
        @pl.loop(0, grp * lines)
        def _(at):
            a, b = at // lines, lax.rem(at, lines)
            slot[a, b] = (raw[a, b, core].astype(F32) + slot[a, b].astype(F32)).astype(BF16)

    def over_grp(summed, slots):
        return [links.send(summed.at[here.next_grp(k)], slots.at[k - 1], here.across[k - 1]) for k in range(1, grp)]

    def add_grp(summed, slots):
        @pl.loop(0, lines)
        def _(b):
            piece = summed[me, b].astype(F32)
            for k in range(grp - 1):
                piece += slots[k, b].astype(F32)
            slots[0, b] = piece.astype(BF16)

    def over_line(slots, last):
        return [
            links.send(slots.at[0, here.next_line(k)], last.at[k - 1], here.along[k - 1]) for k in range(1, lines)
        ]

    def add_line(slots, last, out):
        piece = slots[0, line].astype(F32)
        for k in range(lines - 1):
            piece += last[k].astype(F32)
        out[...] = piece

    for name in ("grads", "x3", "we", "act2"):
        loads[name].wait()

    @pl.loop(0, grp)
    def _(number):
        for part in range(0, own_in, BLK):
            span = pl.ds(pl.multiple_of(number * own_in + part, BLK), BLK)
            inverse = 1.0 / n3[2:3, span]
            factor = out_all[0:1, span] * n3[1:2, span]
            for at in range(0, rows, step):
                mask = wide(m_ref[at : at + step], BLK)
                normed = x3[at : at + step, span].astype(F32)
                shift = (sums3[0:1, span] + normed * sums3[1:2, span]) * inverse
                value = mask * factor * (grads[at : at + step, span].astype(F32) - shift)
                ge[at : at + step, part : part + BLK] = value.astype(BF16)
        per = we.shape[3]
        taken = BLK // per if per < BLK else 1
        for left in range(0, width, BLK):
            if per < BLK:
                slots = [divmod(left // per + k, we.shape[2]) for k in range(taken)]
                weights = jnp.concatenate([we[number, b, c] for b, c in slots], axis=0)
            else:
                weights = we[number, 0, 0, left : left + BLK]
            part_sum = dot_right(ge[...], weights)
            block = dot_left(act2[:, left : left + BLK], ge[...]).astype(BF16)
            if per < BLK:
                for k, (b, c) in enumerate(slots):
                    raw_e[number, b, c] = block[k * per : (k + 1) * per]
            else:
                raw_e[number, 0, 0, left : left + BLK] = block

            @pl.when(number == 0)
            def _():
                dp[:, left : left + BLK] = part_sum

            @pl.when(number > 0)
            def _():
                dp[:, left : left + BLK] += part_sum

    if owners:
        e_core = core_swap(raw_e, e1)
    else:
        links.move(raw_e, expand_out)
    for name in ("slope2", "x2"):
        loads[name].wait()

    def norm_sums(slope, normed, sums):
        @pl.loop(0, steps)
        def _(number):
            span = aligned(number * BLK, BLK)
            bias_grad = jnp.zeros((1, BLK), F32)
            gain_grad = jnp.zeros((1, BLK), F32)
            for at in range(0, rows, step):
                grad = dp[at : at + step, span] * slope[at : at + step, span].astype(F32)
                dp[at : at + step, span] = grad
                bias_grad += jnp.sum(grad, axis=0, keepdims=True)
                gain_grad += jnp.sum(grad * normed[at : at + step, span].astype(F32), axis=0, keepdims=True)
            sums[0:1, span] = bias_grad
            sums[1:2, span] = gain_grad

    norm_sums(slope2, x2, st2)
    sums2[...] = over_devices(st2, ex2, add_rows)
    if owners:
        e_core.wait_recv()
        add_core(raw_e, e1)
        e_grp = over_grp(e1, e2)

    for name in ("act1", "slope1", "x1", "wg"):
        loads[name].wait()
    own = (
        lax.broadcasted_iota(jnp.int32, (BLK, BLK), 0) // GW == lax.broadcasted_iota(jnp.int32, (BLK, BLK), 1) // GW
    )

    @pl.loop(0, steps)
    def _(number):
        span = aligned(number * BLK, BLK)
        inverse = 1.0 / n2[2:3, span]
        factor = norm_all[2:3, span] * n2[1:2, span]
        clear_edges(col, images, False)
        for row in range(SIDE):
            at = row * step
            mask = wide(m_ref[at : at + step], BLK)
            normed = x2[at : at + step, span].astype(F32)
            shift = (sums2[0:1, span] + normed * sums2[1:2, span]) * inverse
            grad_in[at : at + step] = (mask * factor * (dp[at : at + step, span] - shift)).astype(BF16)
            spread_row(col, act1[at : at + step, span], row, images, False)
        for tap in range(9):
            product = dot_left(col[:, tap * BLK : (tap + 1) * BLK], grad_in[...])
            product = jnp.where(own, product, 0.0)
            piece = product[0:GW]
            for group in range(1, BLK // GW):
                piece += product[group * GW : (group + 1) * GW]
            raw_g[tap * GW : (tap + 1) * GW, span] = piece.astype(BF16)
        clear_edges(col, images, True)
        for row in range(SIDE):
            at = row * step
            spread_row(col, grad_in[at : at + step], row, images, True)
        block_weights(wg, number, blocks)
        for tap in range(9):
            turned[tap * BLK : (tap + 1) * BLK] = blocks[tap * BLK : (tap + 1) * BLK].astype(F32).T.astype(BF16)
        dp[:, span] = dot(col[...], turned[...])

    norm_sums(slope1, x1, st1)
    inner = col.at[:, 0:channels]
    load_inner = links.move(inner_in, inner, keep=False)
    if owners:
        g_grp = [
            links.send(raw_g.at[:, aligned(here.next_grp(k) * BLK, BLK)], g1.at[k - 1], here.across[k - 1])
            for k in range(1, grp)
        ]
    else:
        links.move(raw_g, group_out)
    sums1[...] = over_devices(st1, ex1, add_rows)
    if owners:
        arrived(e_grp)
        add_grp(e1, e2)
        e_line = over_line(e2, e3)

    @pl.loop(0, steps)
    def _(number):
        span = aligned(number * BLK, BLK)
        inverse = 1.0 / n1[2:3, span]
        factor = norm_all[0:1, span] * n1[1:2, span]
        for at in range(0, rows, step):
            mask = wide(m_ref[at : at + step], BLK)
            normed = x1[at : at + step, span].astype(F32)
            shift = (sums1[0:1, span] + normed * sums1[1:2, span]) * inverse
            x1[at : at + step, span] = (mask * factor * (dp[at : at + step, span] - shift)).astype(BF16)

    grad_reduce = x1
    load_inner.wait()
    per_r = raw_r.shape[3]

    @pl.loop(0, grp)
    def _(number):
        for part in range(0, own_in, BLK):
            span = pl.ds(pl.multiple_of(number * own_in + part, BLK), BLK)
            block = dot_left(col[:, span], grad_reduce[...]).astype(BF16)
            if per_r < BLK:
                for k in range(BLK // per_r):
                    b, c = divmod(part // per_r + k, raw_r.shape[2])
                    raw_r[number, b, c] = block[k * per_r : (k + 1) * per_r]
            else:
                raw_r[number, 0, 0, part : part + BLK] = block

    if owners:
        r_core = core_swap(raw_r, r1)
        arrived(g_grp)
        total = raw_g[:, aligned(me * BLK, BLK)].astype(F32)
        for k in range(grp - 1):
            total += g1[k].astype(F32)
        gs1[...] = total.astype(BF16)
        high = line // 2
        g_far = links.send(gs1.at[:, aligned((1 - high) * 128, 128)], g2, here.far)
        r_core.wait_recv()
        add_core(raw_r, r1)
        r_grp = over_grp(r1, r2)
    else:
        links.move(raw_r, reduce_out)
    loads["wr"].wait()

    @pl.loop(0, grp)
    def _(number):
        for part in range(0, own_in, BLK):
            span = pl.ds(pl.multiple_of(number * own_in + part, BLK), BLK)
            per = wr.shape[3]
            if per < BLK:
                slots = [divmod(part // per + k, wr.shape[2]) for k in range(BLK // per)]
                weights = jnp.concatenate([wr[number, b, c] for b, c in slots], axis=0)
            else:
                weights = wr[number, 0, 0, part : part + BLK]
            total = grads[:, span].astype(F32) + dot_right(grad_reduce[...], weights)
            ge[:, part : part + BLK] = total.astype(BF16)
        grads[:, aligned(number * own_in, own_in)] = dot(back[...], ge[...]).astype(BF16)

    if owners:
        g_far.wait_recv()
        gs2[...] = (gs1[:, aligned(high * 128, 128)].astype(F32) + g2[...].astype(F32)).astype(BF16)
        g_near = links.send(gs2, g3, here.near)
        arrived(e_line)
        add_line(e2, e3, expand_out)
        g_near.wait_recv()
        gs3[...] = (gs2[...].astype(F32) + g3[...].astype(F32)).astype(BF16)
        g_last = links.send(gs3, g4, here.sibling)
        g_last.wait_recv()
        group_out[...] = gs3[...].astype(F32) + g4[...].astype(F32)
        arrived(r_grp)
        add_grp(r1, r2)
        r_line = over_line(r2, r3)
    in_sends = [
        links.send(grads.at[:, aligned(here.next_grp(k) * own_in, own_in)], input_grad.at[own_rows], here.across[k - 1])
        for k in range(1, grp)
    ]
    links.move(grads.at[:, aligned(me * own_in, own_in)], input_grad.at[own_rows])
    if owners:
        arrived(r_line)
        add_line(r2, r3, reduce_out)
    arrived(out_sends)
    arrived(in_sends)
    links.close()


def backward(kept, mask, n1, n2, n3, norm_all, out_all, sums3, owners):
    grp = lax.axis_size("grp")
    rows, width = kept["act1"].shape
    channels = kept["x3"].shape[1]
    own_in = channels // grp
    r_shape, e_shape = kept["wr"].shape, kept["we"].shape
    lines = r_shape[1]
    vmem = pl.BlockSpec(memory_space=pltpu.VMEM)
    hbm = pl.BlockSpec(memory_space=pl.ANY)
    if owners:
        parts = [
            jax.ShapeDtypeStruct(r_shape[3:], F32),
            jax.ShapeDtypeStruct(e_shape[3:], F32),
            jax.ShapeDtypeStruct((9 * GW, 128), F32),
        ]
    else:
        parts = [jax.ShapeDtypeStruct(shape, BF16) for shape in (r_shape, e_shape, (9 * GW, width))]
    sums = [jax.ShapeDtypeStruct((2, width), F32)] * 2
    scratch = [pltpu.VMEM(kept[name].shape, BF16) for name in BWD_INS] + [
        pltpu.VMEM((rows, own_in), BF16),
        pltpu.VMEM((rows, width), F32),
        pltpu.VMEM((rows, 9 * BLK), BF16),
        pltpu.VMEM((9 * BLK, BLK), BF16),
        pltpu.VMEM((9 * BLK, BLK), BF16),
        pltpu.VMEM((rows, BLK), BF16),
        pltpu.VMEM((rows, rows), BF16),
        pltpu.VMEM((2, width), F32),
        pltpu.VMEM((2, width), F32),
        pltpu.VMEM(e_shape, BF16),
        pltpu.VMEM(r_shape, BF16),
        pltpu.VMEM((9 * GW, width), BF16),
        pltpu.SemaphoreType.DMA((32,)),
        pltpu.SemaphoreType.DMA((32,)),
        pltpu.SemaphoreType.DMA((20,)),
    ]
    scratch += sums_scratch(2, width) + sums_scratch(2, width)
    if owners:
        for shape in (e_shape, r_shape):
            tail = shape[3:]
            scratch += [
                pltpu.VMEM((grp, lines, *tail), BF16),
                pltpu.VMEM((grp - 1, lines, *tail), BF16),
                pltpu.VMEM((lines - 1, *tail), BF16),
            ]
        narrow = pltpu.VMEM((9 * GW, 128), BF16)
        scratch += [pltpu.VMEM((grp - 1, 9 * GW, BLK), BF16), narrow, narrow, narrow]
        scratch += [pltpu.VMEM((9 * GW, BLK), BF16), narrow, narrow]
    whole = jax.ShapeDtypeStruct((grp * rows, own_in), BF16)
    return pl.pallas_call(
        functools.partial(backward_kernel, images=rows // HW, owners=owners),
        out_shape=[whole, whole, *parts, *sums],
        in_specs=[hbm] * 13 + [vmem] * 7,
        out_specs=[hbm, hbm] + [vmem if owners else hbm] * 3 + [vmem] * 2,
        scratch_shapes=scratch,
        compiler_params=params(collective_id=2, has_side_effects=True),
    )(
        kept["outs"],
        kept["inner"],
        *[kept[name] for name in BWD_INS],
        mask,
        n1,
        n2,
        n3,
        norm_all,
        out_all,
        sums3,
    )


DECAYS = (0.01, 0.01, 0.01, 0.0, 0.0)


def whole_sum(value):
    return jnp.sum(jnp.sum(value, axis=0, keepdims=True), axis=1, keepdims=True)


def adam_direction(tensor, clipped, moment_one, moment_two, decay_rate):
    new_first = beta_one * moment_one + (1.0 - beta_one) * clipped
    new_second = beta_two * moment_two + (1.0 - beta_two) * clipped * clipped
    first_hat = new_first / (1.0 - beta_one**step_count)
    second_hat = new_second / (1.0 - beta_two**step_count)
    direction = first_hat / (jnp.sqrt(second_hat) + adam_eps) + decay_rate * tensor
    return (new_first, new_second, direction)


def trust_kernel(*refs):
    raws, tensors, firsts, seconds = (refs[5 * k : 5 * k + 5] for k in range(4))
    out_ref, pay, *scratch = refs[20:]
    one, two = scratch[:7], scratch[7:]
    share = 1.0 / lax.axis_size("batch")
    shares = (1.0, 1.0, 1.0, share, share)
    greet(everyone())
    square = jnp.zeros((1, 1), F32)
    pay[...] = jnp.zeros_like(pay)
    for number in range(5):
        square += shares[number] * whole_sum(raws[number][...] ** 2)
        weight = shares[number] * whole_sum(tensors[number][...] ** 2)
        pay[0, number + 1 : number + 2] = jnp.broadcast_to(weight, (1, 128))
    pay[0, 0:1] = jnp.broadcast_to(square, (1, 128))
    greeted(everyone())
    sums = over_devices(pay.at[0], one, add_rows)
    grad_norm = jnp.sqrt(sums[0:1])
    factor = jnp.minimum(1.0, clip_norm / grad_norm)
    for number in range(5):
        direction = adam_direction(
            tensors[number][...],
            factor[0:1, 0:1] * raws[number][...],
            firsts[number][...],
            seconds[number][...],
            DECAYS[number],
        )[2]
        step = shares[number] * whole_sum(direction * direction)
        pay[1, number + 1 : number + 2] = jnp.broadcast_to(step, (1, 128))
    steps = over_devices(pay.at[1], two, add_rows)
    out_ref[...] = jnp.zeros_like(out_ref)
    out_ref[0:1] = grad_norm
    out_ref[1:2] = factor
    out_ref[2:7] = jnp.sqrt(sums[1:6]) * lax.rsqrt(steps[1:6] + 1e-06)


def update_kernel(*refs):
    scalars = refs[0]
    raws, tensors, firsts, seconds = (refs[5 * k + 1 : 5 * k + 6] for k in range(4))
    outs = refs[21:]
    at = 0
    for number in range(5):
        clipped = scalars[1:2, 0:1] * raws[number][...]
        tensor = tensors[number][...]
        new_first, new_second, direction = adam_direction(
            tensor, clipped, firsts[number][...], seconds[number][...], DECAYS[number]
        )
        updated = tensor - learn_rate * scalars[2 + number : 3 + number, 0:1] * direction
        values = [clipped, new_first, new_second, updated]
        if number < 3:
            values.append(updated.astype(BF16))
        for value in values:
            outs[at][...] = value
            at += 1


def optimizer(raws, tensors, firsts, seconds):
    vmem = pl.BlockSpec(memory_space=pltpu.VMEM)
    state = (*raws, *tensors, *firsts, *seconds)
    scalars = pl.pallas_call(
        trust_kernel,
        out_shape=jax.ShapeDtypeStruct((8, 128), F32),
        in_specs=[vmem] * 20,
        out_specs=vmem,
        scratch_shapes=[pltpu.VMEM((2, 8, 128), F32)] + sums_scratch(8, 128) + sums_scratch(8, 128),
        compiler_params=params(collective_id=8, has_side_effects=True),
    )(*state)
    shapes = []
    for number, tensor in enumerate(tensors):
        shapes += [jax.ShapeDtypeStruct(tensor.shape, F32)] * 4
        if number < 3:
            shapes.append(jax.ShapeDtypeStruct(tensor.shape, BF16))
    outs = pl.pallas_call(
        update_kernel,
        out_shape=shapes,
        in_specs=[vmem] * 21,
        out_specs=[vmem] * len(shapes),
        compiler_params=params(),
    )(scalars, *state)
    return scalars, outs


def local(
    features,
    pixel_mask,
    out_cotangent,
    reduce_master,
    group_master,
    expand_master,
    norm_params,
    out_params,
    reduce_first,
    reduce_second,
    group_first,
    group_second,
    expand_first,
    expand_second,
    norm_first,
    norm_second,
    out_first,
    out_second,
):
    grp, batch = lax.axis_size("grp"), lax.axis_size("batch")
    both = ("grp", "batch")
    me, mine = lax.axis_index("grp"), lax.axis_index("batch")
    rows = features.shape[0] // grp
    images = rows // HW
    own_in = features.shape[1]
    own_width = norm_params.shape[1]
    inside = batch == 8 and own_width == 8 * GW
    validity = lax.dynamic_slice_in_dim(pixel_mask, me * rows, rows, 0).astype(F32)
    mask = jnp.broadcast_to(validity.reshape(images, HW).T.reshape(rows, 1), (rows, 128))
    reduce_w, group_w, expand_w = (value.astype(BF16) for value in (reduce_master, group_master, expand_master))
    if inside:
        group_w = packed_groups(group_w)[0]
    else:
        reduce_w = lax.all_gather(reduce_w, both, axis=0, tiled=True)
        expand_w = lax.all_gather(expand_w, both, axis=0, tiled=True)
        group_w = packed_groups(lax.all_gather(group_w, both, axis=1, tiled=True))
    kept, (n1, n2, n3, norm_all, out_all, sums_three) = forward(
        features, out_cotangent, mask, norm_params, out_params, reduce_w, expand_w, group_w, inside
    )
    block_out, input_grad, reduce_part, expand_part, group_part, sums_one, sums_two = backward(
        kept, mask, n1, n2, n3, norm_all, out_all, sums_three, inside
    )
    if inside:
        group_part = lax.dynamic_slice_in_dim(group_part, lax.rem(mine, 4) * GW, GW, 1)
    else:
        flat = group_part.reshape(9 * GW, grp * batch, -1).transpose(1, 0, 2)
        reduce_part, expand_part, group_part = (
            lax.psum_scatter(value, both, scatter_dimension=0).astype(F32)
            for value in (
                reduce_part.reshape(grp * batch, own_in // batch, -1),
                expand_part.reshape(grp * batch, -1, own_in),
                flat,
            )
        )
    norm_sums = jnp.concatenate([sums_one[1:2], sums_one[0:1], sums_two[1:2], sums_two[0:1]], axis=0)
    norm_raw = lax.dynamic_slice_in_dim(norm_sums, me * own_width, own_width, 1)
    out_raw = lax.dynamic_slice_in_dim(
        jnp.concatenate([sums_three[1:2], sums_three[0:1]], axis=0), me * own_in, own_in, 1
    )
    scalars, updates = optimizer(
        (reduce_part, group_part, expand_part, norm_raw, out_raw),
        (reduce_master, group_master, expand_master, norm_params, out_params),
        (reduce_first, group_first, expand_first, norm_first, out_first),
        (reduce_second, group_second, expand_second, norm_second, out_second),
    )
    return (block_out, input_grad, scalars[0, 0], scalars[2:5, 0], scalars[5:7, 0], *updates)


def solution(mesh):
    in_specs = (
        P("batch", "grp"),
        P("batch"),
        P("batch", "grp"),
        P(("grp", "batch"), None),
        P(None, ("grp", "batch")),
        P("batch", "grp"),
        P(None, "grp"),
        P(None, "grp"),
        P(("grp", "batch"), None),
        P(("grp", "batch"), None),
        P(None, ("grp", "batch")),
        P(None, ("grp", "batch")),
        P("batch", "grp"),
        P("batch", "grp"),
        P(None, "grp"),
        P(None, "grp"),
        P(None, "grp"),
        P(None, "grp"),
    )
    out_specs = (
        P("batch", "grp"),
        P("batch", "grp"),
        P(),
        P(),
        P(),
        P(("grp", "batch"), None),
        P(("grp", "batch"), None),
        P(("grp", "batch"), None),
        P(("grp", "batch"), None),
        P(("grp", "batch"), None),
        P(None, ("grp", "batch")),
        P(None, ("grp", "batch")),
        P(None, ("grp", "batch")),
        P(None, ("grp", "batch")),
        P(None, ("grp", "batch")),
        P("batch", "grp"),
        P("batch", "grp"),
        P("batch", "grp"),
        P("batch", "grp"),
        P("batch", "grp"),
        P(None, "grp"),
        P(None, "grp"),
        P(None, "grp"),
        P(None, "grp"),
        P(None, "grp"),
        P(None, "grp"),
        P(None, "grp"),
        P(None, "grp"),
    )
    return jax.shard_map(local, mesh=mesh, in_specs=in_specs, out_specs=out_specs, check_vma=False)
```

```python
import functools

import jax
import jax.numpy as jnp
from jax import lax
from jax.experimental import pallas as pl
from jax.experimental.pallas import tpu as pltpu
from jax.sharding import PartitionSpec as P

GW = 32
SIDE = 7
HW = SIDE * SIDE
BLK = 256

eps_norm = 1e-05
beta_one = 0.9
beta_two = 0.999
adam_eps = 1e-08
learn_rate = 0.25
step_count = 10.0
clip_norm = 1.0

MESH = pl.DeviceIdType.MESH
F32 = jnp.float32
BF16 = jnp.bfloat16
VMEM_LIMIT = 60 * 1024 * 1024


def params(**more):
    return pltpu.CompilerParams(vmem_limit_bytes=VMEM_LIMIT, **more)


def dot(a, b):
    return jnp.dot(a, b, preferred_element_type=F32)


def dot_left(a, b):
    return lax.dot_general(a, b, (((0,), (0,)), ((), ())), preferred_element_type=F32)


def dot_right(a, b):
    return lax.dot_general(a, b, (((1,), (1,)), ((), ())), preferred_element_type=F32)


def sigmoid(v):
    return 0.5 + 0.5 * jnp.tanh(0.5 * v)


def to_inner(rows, images):
    to = lax.broadcasted_iota(jnp.int32, (rows, rows), 0)
    source = (to % images) * HW + to // images
    at = lax.broadcasted_iota(jnp.int32, (rows, rows), 1)
    return jnp.where(at == source, 1.0, 0.0).astype(BF16)


def to_outer(rows, images):
    to = lax.broadcasted_iota(jnp.int32, (rows, rows), 0)
    source = (to % HW) * images + to // HW
    at = lax.broadcasted_iota(jnp.int32, (rows, rows), 1)
    return jnp.where(at == source, 1.0, 0.0).astype(BF16)


def wide(mask, columns):
    return jnp.concatenate([mask] * (columns // 128), axis=1)


def peers(axis):
    size = lax.axis_size(axis)
    mine = lax.axis_index(axis)
    return [{axis: lax.rem(mine + other, size)} for other in range(1, size)]


def greet(groups):
    barrier = pltpu.get_barrier_semaphore()
    for peer in groups:
        pl.semaphore_signal(barrier, inc=1, device_id=peer, device_id_type=MESH)


def greeted(groups):
    pl.semaphore_wait(pltpu.get_barrier_semaphore(), len(groups))


def everyone():
    return peers("grp") + peers("batch")


def sums_scratch(rows, columns):
    grp, batch = lax.axis_size("grp"), lax.axis_size("batch")
    return [
        pltpu.VMEM((grp - 1, rows, columns), F32),
        pltpu.VMEM((batch - 1, rows, columns), F32),
        pltpu.VMEM((rows, columns), F32),
        pltpu.SemaphoreType.DMA((grp - 1,)),
        pltpu.SemaphoreType.DMA((grp - 1,)),
        pltpu.SemaphoreType.DMA((batch - 1,)),
        pltpu.SemaphoreType.DMA((batch - 1,)),
    ]


def add_rows(parts):
    return functools.reduce(jnp.add, parts)


def merge_stats(parts):
    count = add_rows([part[2:3] for part in parts])
    total = add_rows([part[0:1] for part in parts])
    centre = total / count
    spread = add_rows([part[1:2] + part[2:3] * (part[0:1] / part[2:3] - centre) ** 2 for part in parts])
    return jnp.concatenate([total, spread, count], axis=0)


def over_devices(source, scratch, merge):
    first, second, mid, *sems = scratch
    copies = []
    for axis, slots, send, recv in (("grp", first, sems[0], sems[1]), ("batch", second, sems[2], sems[3])):
        here = []
        for number, peer in enumerate(peers(axis)):
            copy = pltpu.make_async_remote_copy(
                source, slots.at[number], send.at[number], recv.at[number], device_id=peer, device_id_type=MESH
            )
            copy.start()
            here.append(copy)
        for copy in here:
            copy.wait_recv()
        copies += here
        merged = merge([source[...]] + [slots[number] for number in range(len(here))])
        if axis == "grp":
            mid[...] = merged
            source = mid
    for copy in copies:
        copy.wait_send()
    return merged


def norm_rows(merged):
    total, spread, count = merged[0:1], merged[1:2], merged[2:3]
    return jnp.concatenate([total / count, lax.rsqrt(spread / count + eps_norm), count], axis=0)


def clear_edges(col, images, reverse):
    for tap_row in range(3):
        for tap_col in range(3):
            tap = 3 * tap_row + tap_col
            dy, dx = (1 - tap_row, 1 - tap_col) if reverse else (tap_row - 1, tap_col - 1)
            for row in range(SIDE):
                for column in range(SIDE):
                    inside = 0 <= row + dy < SIDE and 0 <= column + dx < SIDE
                    if not inside:
                        at = (row * SIDE + column) * images
                        col[at : at + images, tap * BLK : (tap + 1) * BLK] = jnp.zeros((images, BLK), BF16)


def spread_row(col, value, row, images, reverse):
    for tap_row in range(3):
        for tap_col in range(3):
            tap = 3 * tap_row + tap_col
            dy, dx = (1 - tap_row, 1 - tap_col) if reverse else (tap_row - 1, tap_col - 1)
            to_row = row - dy
            if not 0 <= to_row < SIDE:
                continue
            first = max(0, dx)
            last = min(SIDE, SIDE + dx)
            at = (to_row * SIDE + first - dx) * images
            col[at : at + (last - first) * images, tap * BLK : (tap + 1) * BLK] = value[first * images : last * images]


class Links:
    def __init__(self, send, recv, local):
        self.send_sems, self.recv_sems, self.local_sems = send, recv, local
        self.sent = self.moved = 0
        self.open_sends, self.open_moves = [], []

    def send(self, source, target, peer, start=True):
        at = self.sent
        self.sent += 1
        copy = pltpu.make_async_remote_copy(
            source, target, self.send_sems.at[at], self.recv_sems.at[at], device_id=peer, device_id_type=MESH
        )
        if start:
            copy.start()
        self.open_sends.append(copy)
        return copy

    def move(self, source, target, keep=True):
        copy = pltpu.make_async_copy(source, target, self.local_sems.at[self.moved])
        self.moved += 1
        copy.start()
        if keep:
            self.open_moves.append(copy)
        return copy

    def close(self):
        for copy in self.open_sends:
            copy.wait_send()
        for copy in self.open_moves:
            copy.wait()


def arrived(copies):
    for copy in copies:
        copy.wait_recv()


class Place:
    def __init__(self):
        grp, batch = lax.axis_size("grp"), lax.axis_size("batch")
        self.grp, self.lines = grp, batch // 2
        self.me, self.mine = lax.axis_index("grp"), lax.axis_index("batch")
        self.core, self.line = lax.rem(self.mine, 2), self.mine // 2
        self.sibling = {"batch": self.mine + 1 - 2 * self.core}
        self.across = [{"grp": self.partner(k)} for k in range(1, grp)]
        self.along = [{"batch": self.next_line(k) * 2 + self.core} for k in range(1, self.lines)]
        self.far = {"batch": (self.line + 2 - 4 * (self.line // 2)) * 2 + self.core}
        self.near = {"batch": (self.line + 1 - 2 * lax.rem(self.line, 2)) * 2 + self.core}

    def partner(self, k):
        low = lax.rem(lax.rem(self.me, 2) + (k % 2 if isinstance(k, int) else lax.rem(k, 2)), 2)
        return lax.rem(self.me // 2 + k // 2, 2) * 2 + low

    def next_line(self, k):
        return lax.rem(self.line + k, self.lines)


def aligned(at, size):
    return pl.ds(pl.multiple_of(at, size), size)


def block_weights(wg_ref, number, blocks):
    lanes = lax.broadcasted_iota(jnp.int32, (GW, 128), 1) // GW
    zero = jnp.zeros((GW, 128), BF16)
    for group in range(BLK // GW):
        for tap in range(9):
            piece = wg_ref[number, group // 2, group % 2, (tap // 4) * GW : (tap // 4 + 1) * GW].astype(F32)
            turn = ((group - tap) % 4) * GW
            if turn:
                piece = pltpu.roll(piece, turn, 1)
            piece = jnp.where(lanes == group % 4, piece, 0.0).astype(BF16)
            row = tap * BLK + group * GW
            left = (group // 4) * 128
            blocks[row : row + GW, left : left + 128] = piece
            blocks[row : row + GW, 128 - left : 256 - left] = zero


def block_stats(z_ref, left, columns, m_ref, st_ref, step):
    rows = z_ref.shape[0]
    for part in range(0, columns, BLK):
        span = pl.ds(pl.multiple_of(left + part, BLK), BLK)
        total = jnp.zeros((1, BLK), F32)
        count = jnp.zeros((1, 128), F32)
        for at in range(0, rows, step):
            mask = m_ref[at : at + step]
            total += jnp.sum(z_ref[at : at + step, span] * wide(mask, BLK), axis=0, keepdims=True)
            count += jnp.sum(mask, axis=0, keepdims=True)
        count = wide(count, BLK)
        centre = total / count
        spread = jnp.zeros((1, BLK), F32)
        for at in range(0, rows, step):
            off = (z_ref[at : at + step, span] - centre) * wide(m_ref[at : at + step], BLK)
            spread += jnp.sum(off * off, axis=0, keepdims=True)
        st_ref[0:1, span] = total
        st_ref[1:2, span] = spread
        st_ref[2:3, span] = count


def smooth(pre, mask):
    sigma = sigmoid(pre)
    masked = sigma * mask
    return pre * masked, masked * (1.0 + pre * (1.0 - sigma))


FWD_OUTS = ("inner", "x1", "act1", "slope1", "x2", "act2", "slope2", "x3", "grads", "wr", "we", "wg", "far")


def forward_kernel(*refs, images, gather):
    (feat, cotg, m_ref, np_ref, op_ref, wr_in, we_in, wg_in) = refs[:8]
    big = dict(zip(FWD_OUTS, refs[8:21]))
    block_out, n1, n2, n3, norm_all, out_all, sums3 = refs[21:28]
    (inner, x1, act1, slope1, x2, act2, slope2, x3, grads, wr, we, wg) = refs[28:40]
    (land_f, land_c, cot, perm, back, z1, ze, col, blocks, st1, st2, st3, st4, send, recv, moves) = refs[40:56]
    ex1, ex2, ex3, ex4 = (refs[56 + 7 * k : 63 + 7 * k] for k in range(4))
    held = dict(zip(FWD_OUTS, (inner, x1, act1, slope1, x2, act2, slope2, x3, grads, wr, we, wg)))
    here = Place()
    grp = here.grp
    rows, own_in = land_f.shape[1:]
    width, channels = z1.shape[1], ze.shape[1]
    own_width = np_ref.shape[1]
    step = SIDE * images
    links = Links(send, recv, moves)

    greet(everyone())
    own_rows = aligned(here.me * rows, rows)
    own_f = links.move(feat.at[own_rows], land_f.at[0], keep=False)
    if gather:
        wr[here.me, here.line, here.core] = wr_in[...].astype(BF16)
        we[here.me, here.line, here.core] = we_in[...].astype(BF16)
        wg[here.me, here.line, here.core] = wg_in[...]
        loads = []
    else:
        loads = [links.move(wr_in, wr, keep=False), links.move(we_in, we, keep=False), links.move(wg_in, wg, keep=False)]
    norm_all[:, aligned(here.me * own_width, own_width)] = np_ref[...]
    out_all[:, aligned(here.me * own_in, own_in)] = op_ref[...]
    greeted(everyone())

    def spread_out(buffer, targets, rows=slice(None)):
        place = buffer.at[here.me, here.line, here.core, rows]
        return [links.send(place, place, peer) for peer in targets]

    if gather:
        quarter = wr.shape[3] // 4
        head, rest = pl.ds(0, quarter), pl.ds(quarter, 3 * quarter)
        half = we.shape[3] // 2
        lower, upper = pl.ds(0, half), pl.ds(half, half)
        wr_a = spread_out(wr, here.across, rest)
        wr_z = spread_out(wr, here.along, head)
    small = []
    for k in range(1, grp):
        peer = here.across[k - 1]
        span = aligned(here.me * own_width, own_width)
        small.append(links.send(np_ref, norm_all.at[:, span], peer))
        span = aligned(here.me * own_in, own_in)
        small.append(links.send(op_ref, out_all.at[:, span], peer))
    from_f = {}
    for k in range(1, grp):
        source = feat.at[aligned(here.partner(k) * rows, rows)]
        from_f[k] = links.send(source, land_f.at[k], here.across[k - 1])
    own_c = links.move(cotg.at[own_rows], land_c.at[0], keep=False)
    if gather:
        arrived(wr_a)
        place = wr.at[:, here.line, here.core, rest]
        wr_l = [links.send(place, place, peer) for peer in here.along]
        wr_b = [links.send(place, place, here.sibling)]
        arrived(wr_z)
        place = wr.at[here.me, :, here.core, head]
        wr_g = [links.send(place, place, peer) for peer in here.across]
        wg_a = spread_out(wg, here.along)
        we_a0 = spread_out(we, here.across, lower)
        we_a1 = spread_out(we, here.along, upper)
    perm[...] = to_inner(rows, images)
    back[...] = to_outer(rows, images)
    own_f.wait()
    for number in range(grp):
        if number:
            from_f[number].wait_recv()
        span = aligned(here.partner(number) * own_in, own_in)
        inner[:, span] = dot(perm[...], land_f[number]).astype(BF16)
    if gather:
        for k in range(1, here.lines):
            wr_l[k - 1].wait_recv()
            place = wr.at[:, here.next_line(here.lines - k), here.core, rest]
            wr_b.append(links.send(place, place, here.sibling))
        arrived(wr_g)
        place = wr.at[:, :, here.core, head]
        wr_b.append(links.send(place, place, here.sibling))
        arrived(wg_a)
        place = wg.at[here.me, :, here.core]
        wg_b = [links.send(place, place, peer) for peer in here.across]
        arrived(we_a0)
        arrived(we_a1)
        place = we.at[:, here.line, here.core, lower]
        we_b = [links.send(place, place, peer) for peer in here.along]
        place = we.at[here.me, :, here.core, upper]
        we_b += [links.send(place, place, peer) for peer in here.across]
        arrived(wr_b)
    for copy in loads:
        copy.wait()
    links.move(inner, big["inner"])

    steps = width // BLK

    @pl.loop(0, steps)
    def _(number):
        span = aligned(number * BLK, BLK)
        z1[:, span] = dot(inner[...], wr[:, :, :, :, span].reshape(channels, BLK))
        block_stats(z1, number * BLK, BLK, m_ref, st1, step)

    links.move(wr, big["wr"])
    if gather:
        arrived(wg_b)
        place = wg.at[:, :, here.core]
        wg_c = [links.send(place, place, here.sibling)]
    arrived(small)
    n1[...] = norm_rows(over_devices(st1, ex1, merge_stats))
    from_c = []
    for k in range(1, grp):
        source = cotg.at[aligned(here.partner(k) * rows, rows)]
        from_c.append(links.send(source, land_c.at[k], here.across[k - 1]))
    if gather:
        arrived(wg_c)

    clear_edges(col, images, False)

    @pl.loop(0, steps)
    def _(number):
        span = aligned(number * BLK, BLK)
        block_weights(wg, number, blocks)
        centre, scale = n1[0:1, span], n1[1:2, span]
        gain, bias = norm_all[0:1, span], norm_all[1:2, span]
        for row in range(SIDE):
            at = row * step
            mask = wide(m_ref[at : at + step], BLK)
            normed = (z1[at : at + step, span] - centre) * scale
            value, slope = smooth(normed * gain + bias, mask)
            act = value.astype(BF16)
            x1[at : at + step, span] = normed.astype(BF16)
            act1[at : at + step, span] = act
            slope1[at : at + step, span] = slope.astype(BF16)
            spread_row(col, act, row, images, False)
        z1[:, span] = dot(col[...], blocks[...])
        block_stats(z1, number * BLK, BLK, m_ref, st2, step)

    for name in ("x1", "act1", "slope1", "wg"):
        links.move(held[name], big[name])
    if gather:
        arrived(we_b)
        place = we.at[:, :, here.core]
        we_c = [links.send(place, place, here.sibling)]
    n2[...] = norm_rows(over_devices(st2, ex2, merge_stats))

    @pl.loop(0, steps)
    def _(number):
        span = aligned(number * BLK, BLK)
        for at in range(0, rows, step):
            mask = wide(m_ref[at : at + step], BLK)
            normed = (z1[at : at + step, span] - n2[0:1, span]) * n2[1:2, span]
            value, slope = smooth(normed * norm_all[2:3, span] + norm_all[3:4, span], mask)
            x2[at : at + step, span] = normed.astype(BF16)
            act2[at : at + step, span] = value.astype(BF16)
            slope2[at : at + step, span] = slope.astype(BF16)

    for name in ("x2", "act2", "slope2"):
        links.move(held[name], big[name])
    if gather:
        arrived(we_c)
    links.move(we, big["we"])

    @pl.loop(0, grp)
    def _(number):
        for part in range(0, own_in, BLK):
            span = pl.ds(pl.multiple_of(number * own_in + part, BLK), BLK)
            ze[:, span] = dot(act2[...], we[number, :, :, :, part : part + BLK].reshape(width, BLK))
        block_stats(ze, number * own_in, own_in, m_ref, st3, step)

    n3[...] = norm_rows(over_devices(st3, ex3, merge_stats))
    own_c.wait()
    arrived(from_c)
    to_near = [
        links.send(land_f.at[k], block_out.at[own_rows], here.across[k - 1], start=False) for k in range(1, grp - 1)
    ]

    @pl.loop(0, grp)
    def _(turn):
        slot = lax.rem(turn + 1, grp)
        number = here.partner(slot)
        cot[...] = dot(perm[...], land_c[slot])
        for part in range(0, own_in, BLK):
            span = pl.ds(pl.multiple_of(number * own_in + part, BLK), BLK)
            local = slice(part, part + BLK)
            bias_grad = jnp.zeros((1, BLK), F32)
            gain_grad = jnp.zeros((1, BLK), F32)
            for at in range(0, rows, step):
                mask = wide(m_ref[at : at + step], BLK)
                normed = (ze[at : at + step, span] - n3[0:1, span]) * n3[1:2, span]
                summed = normed * out_all[0:1, span] + out_all[1:2, span] + inner[at : at + step, span].astype(F32)
                value, slope = smooth(summed, mask)
                grad = cot[at : at + step, local] * slope
                x3[at : at + step, span] = normed.astype(BF16)
                col[at : at + step, local] = value.astype(BF16)
                grads[at : at + step, span] = grad.astype(BF16)
                bias_grad += jnp.sum(grad, axis=0, keepdims=True)
                gain_grad += jnp.sum(grad * normed, axis=0, keepdims=True)
            st4[0:1, span] = bias_grad
            st4[1:2, span] = gain_grad
        land_f[slot] = dot(back[...], col[:, 0:own_in]).astype(BF16)
        for k, copy in enumerate(to_near):

            @pl.when(turn == k)
            def _():
                copy.start()

    links.move(land_f.at[0], block_out.at[own_rows])
    links.move(land_f.at[grp - 1], big["far"])
    for name in ("x3", "grads"):
        links.move(held[name], big[name])
    sums3[...] = over_devices(st4, ex4, add_rows)
    arrived(to_near)
    links.close()


def forward(features, out_cotangent, mask, norm_params, out_params, reduce_w, expand_w, group_w, gather):
    grp = lax.axis_size("grp")
    rows = features.shape[0] // grp
    own_in = features.shape[1]
    channels = own_in * grp
    width = norm_params.shape[1] * grp
    lines, cores = (lax.axis_size("batch") // 2, 2) if gather else (1, 1)
    r_shape = (grp, lines, cores, own_in // (lines * cores), width)
    e_shape = (grp, lines, cores, width // (lines * cores), own_in)
    g_shape = (width // BLK, BLK // GW // 2, 2, 3 * GW, 128)
    across = (rows, width)
    shapes = {
        "inner": (rows, channels),
        "x1": across,
        "act1": across,
        "slope1": across,
        "x2": across,
        "act2": across,
        "slope2": across,
        "x3": (rows, channels),
        "grads": (rows, channels),
        "far": (rows, own_in),
        "wr": r_shape,
        "we": e_shape,
        "wg": g_shape,
    }
    small = [(3, width), (3, width), (3, channels), (4, width), (2, channels), (2, channels)]
    vmem = pl.BlockSpec(memory_space=pltpu.VMEM)
    hbm = pl.BlockSpec(memory_space=pl.ANY)
    if gather:
        weights = (reduce_w, expand_w, group_w)
    else:
        weights = (reduce_w.reshape(r_shape), expand_w.reshape(e_shape), group_w.reshape(g_shape))
    results = pl.pallas_call(
        functools.partial(forward_kernel, images=rows // HW, gather=gather),
        out_shape=[jax.ShapeDtypeStruct(shapes[name], BF16) for name in FWD_OUTS]
        + [jax.ShapeDtypeStruct(features.shape, BF16)]
        + [jax.ShapeDtypeStruct(shape, F32) for shape in small],
        in_specs=[hbm, hbm, vmem, vmem, vmem] + [vmem if gather else hbm] * 3,
        out_specs=[hbm] * (len(FWD_OUTS) + 1) + [vmem] * len(small),
        scratch_shapes=[pltpu.VMEM(shapes[name], BF16) for name in FWD_OUTS[:-1]]
        + [
            pltpu.VMEM((grp, rows, own_in), BF16),
            pltpu.VMEM((grp, rows, own_in), BF16),
            pltpu.VMEM((rows, own_in), F32),
            pltpu.VMEM((rows, rows), BF16),
            pltpu.VMEM((rows, rows), BF16),
            pltpu.VMEM(across, F32),
            pltpu.VMEM((rows, channels), F32),
            pltpu.VMEM((rows, 9 * BLK), BF16),
            pltpu.VMEM((9 * BLK, BLK), BF16),
            pltpu.VMEM((3, width), F32),
            pltpu.VMEM((3, width), F32),
            pltpu.VMEM((3, channels), F32),
            pltpu.VMEM((2, channels), F32),
            pltpu.SemaphoreType.DMA((64,)),
            pltpu.SemaphoreType.DMA((64,)),
            pltpu.SemaphoreType.DMA((20,)),
        ]
        + sums_scratch(3, width)
        + sums_scratch(3, width)
        + sums_scratch(3, channels)
        + sums_scratch(2, channels),
        compiler_params=params(collective_id=1, has_side_effects=True),
    )(features, out_cotangent, mask, norm_params, out_params, *weights)
    return dict(zip(FWD_OUTS, results)), results[len(FWD_OUTS)], results[len(FWD_OUTS) + 1 :]


def packed_groups(weight):
    groups = weight.shape[1] // GW
    taps = jnp.pad(weight.reshape(9, GW, groups, GW), ((0, 3), (0, 0), (0, 0), (0, 0)))
    return taps.reshape(3, 4, GW, groups, GW).transpose(3, 0, 2, 1, 4).reshape(groups, 3 * GW, 4 * GW)


BWD_INS = ("grads", "x3", "we", "act2", "slope2", "x2", "act1", "slope1", "x1", "wg", "wr")


def backward_kernel(*refs, images, owners):
    _, far_in, inner_in = refs[:3]
    given = dict(zip(BWD_INS, refs[3:14]))
    m_ref, n1, n2, n3, norm_all, out_all, sums3 = refs[14:21]
    refs = refs[21:]
    state, refs = (refs[:15], refs[15:]) if owners else ((), refs)
    block_out, input_grad, reduce_out, expand_out, group_out, sums1, sums2 = refs[:7]
    raws, refs = ((reduce_out, group_out, expand_out, *refs[7:9]), refs[9:]) if owners else ((), refs[7:])
    scalars, refs = (refs[0], refs[1:]) if owners else (None, refs)
    (grads, x3, we, act2, slope2, x2, act1, slope1, x1, wg, wr) = refs[:11]
    held = dict(zip(BWD_INS, (grads, x3, we, act2, slope2, x2, act1, slope1, x1, wg, wr)))
    (ge, dp, col, blocks, turned, grad_in, back, st1, st2, raw_e, raw_r, raw_g, send, recv, moves) = refs[11:26]
    ex1, ex2 = refs[26:33], refs[33:40]
    here = Place()
    me, grp, core, line, lines = here.me, here.grp, here.core, here.line, here.lines
    rows, width = dp.shape
    channels = grads.shape[1]
    own_in = channels // grp
    step = SIDE * images
    steps = width // BLK
    links = Links(send, recv, moves)
    if owners:
        e_slots, r_slots = refs[40:45], refs[45:50]
        (g1, g2, g3, g4, gs1, gs2, gs3) = refs[50:57]
        trust_scratch = refs[57:]

    greet(everyone())
    loads = {name: links.move(given[name], held[name], keep=False) for name in BWD_INS}
    own_rows = aligned(me * rows, rows)
    back[...] = to_outer(rows, images)
    greeted(everyone())
    out_sends = [links.send(far_in, block_out.at[own_rows], here.across[grp - 2])]

    def core_swap(raw, slots):
        return links.send(raw.at[:, :, 1 - core], slots[0], here.sibling)

    def add_core(raw, slots):
        @pl.loop(0, grp * lines)
        def _(at):
            a, b = at // lines, lax.rem(at, lines)
            slots[0][a, b] = (raw[a, b, core].astype(F32) + slots[0][a, b].astype(F32)).astype(BF16)

    def halves(slots):
        half = slots[0].shape[2] // 2
        return half, pl.ds(0, half), pl.ds(half, half)

    def spread_sums(slots):
        one, grp_slots, line_slots = slots[:3]
        _, lower, upper = halves(slots)
        over = [
            links.send(one.at[here.partner(k), :, lower], grp_slots.at[k - 1], here.across[k - 1])
            for k in range(1, grp)
        ]
        along = [
            links.send(one.at[:, here.next_line(k), upper], line_slots.at[k - 1], here.along[k - 1])
            for k in range(1, lines)
        ]
        return over, along

    def add_over(slots):
        one, grp_slots = slots[:2]
        half = halves(slots)[0]

        @pl.loop(0, lines)
        def _(b):
            piece = one[me, b, 0:half].astype(F32)
            for k in range(grp - 1):
                piece += grp_slots[k, b].astype(F32)
            grp_slots[0, b] = piece.astype(BF16)

        return [
            links.send(grp_slots.at[0, here.next_line(k)], slots[3].at[k - 1], here.along[k - 1])
            for k in range(1, lines)
        ]

    def add_along(slots):
        one, line_slots = slots[0], slots[2]
        half = halves(slots)[0]

        @pl.loop(0, grp)
        def _(a):
            piece = one[a, line, half : 2 * half].astype(F32)
            for k in range(lines - 1):
                piece += line_slots[k, a].astype(F32)
            line_slots[0, a] = piece.astype(BF16)

        return [
            links.send(line_slots.at[0, here.partner(k)], slots[4].at[k - 1], here.across[k - 1])
            for k in range(1, grp)
        ]

    def add_last(slots, out):
        half, lower, upper = halves(slots)
        piece = slots[1][0, line].astype(F32)
        for k in range(lines - 1):
            piece += slots[3][k].astype(F32)
        out[0:half] = piece
        piece = slots[2][0, me].astype(F32)
        for k in range(grp - 1):
            piece += slots[4][k].astype(F32)
        out[half : 2 * half] = piece

    for name in ("grads", "x3", "we", "act2"):
        loads[name].wait()

    @pl.loop(0, grp)
    def _(number):
        for part in range(0, own_in, BLK):
            span = pl.ds(pl.multiple_of(number * own_in + part, BLK), BLK)
            inverse = 1.0 / n3[2:3, span]
            factor = out_all[0:1, span] * n3[1:2, span]
            for at in range(0, rows, step):
                mask = wide(m_ref[at : at + step], BLK)
                normed = x3[at : at + step, span].astype(F32)
                shift = (sums3[0:1, span] + normed * sums3[1:2, span]) * inverse
                value = mask * factor * (grads[at : at + step, span].astype(F32) - shift)
                ge[at : at + step, part : part + BLK] = value.astype(BF16)
        per = we.shape[3]
        taken = BLK // per if per < BLK else 1
        for left in range(0, width, BLK):
            if per < BLK:
                slots = [divmod(left // per + k, we.shape[2]) for k in range(taken)]
                weights = jnp.concatenate([we[number, b, c] for b, c in slots], axis=0)
            else:
                weights = we[number, 0, 0, left : left + BLK]
            part_sum = dot_right(ge[...], weights)
            block = dot_left(act2[:, left : left + BLK], ge[...]).astype(BF16)
            if per < BLK:
                for k, (b, c) in enumerate(slots):
                    raw_e[number, b, c] = block[k * per : (k + 1) * per]
            else:
                raw_e[number, 0, 0, left : left + BLK] = block

            @pl.when(number == 0)
            def _():
                dp[:, left : left + BLK] = part_sum

            @pl.when(number > 0)
            def _():
                dp[:, left : left + BLK] += part_sum

    if owners:
        e_core = core_swap(raw_e, e_slots)
    else:
        links.move(raw_e, expand_out)
    for name in ("slope2", "x2"):
        loads[name].wait()

    def norm_sums(slope, normed, sums):
        @pl.loop(0, steps)
        def _(number):
            span = aligned(number * BLK, BLK)
            bias_grad = jnp.zeros((1, BLK), F32)
            gain_grad = jnp.zeros((1, BLK), F32)
            for at in range(0, rows, step):
                grad = dp[at : at + step, span] * slope[at : at + step, span].astype(F32)
                dp[at : at + step, span] = grad
                bias_grad += jnp.sum(grad, axis=0, keepdims=True)
                gain_grad += jnp.sum(grad * normed[at : at + step, span].astype(F32), axis=0, keepdims=True)
            sums[0:1, span] = bias_grad
            sums[1:2, span] = gain_grad

    norm_sums(slope2, x2, st2)
    sums2[...] = over_devices(st2, ex2, add_rows)
    if owners:
        e_core.wait_recv()
        add_core(raw_e, e_slots)
        e_over, e_along = spread_sums(e_slots)

    for name in ("act1", "slope1", "x1", "wg"):
        loads[name].wait()
    own = (
        lax.broadcasted_iota(jnp.int32, (BLK, BLK), 0) // GW == lax.broadcasted_iota(jnp.int32, (BLK, BLK), 1) // GW
    )

    @pl.loop(0, steps)
    def _(number):
        span = aligned(number * BLK, BLK)
        inverse = 1.0 / n2[2:3, span]
        factor = norm_all[2:3, span] * n2[1:2, span]
        clear_edges(col, images, False)
        for row in range(SIDE):
            at = row * step
            mask = wide(m_ref[at : at + step], BLK)
            normed = x2[at : at + step, span].astype(F32)
            shift = (sums2[0:1, span] + normed * sums2[1:2, span]) * inverse
            grad_in[at : at + step] = (mask * factor * (dp[at : at + step, span] - shift)).astype(BF16)
            spread_row(col, act1[at : at + step, span], row, images, False)
        for tap in range(9):
            product = dot_left(col[:, tap * BLK : (tap + 1) * BLK], grad_in[...])
            product = jnp.where(own, product, 0.0)
            piece = product[0:GW]
            for group in range(1, BLK // GW):
                piece += product[group * GW : (group + 1) * GW]
            raw_g[tap * GW : (tap + 1) * GW, span] = piece.astype(BF16)
        clear_edges(col, images, True)
        for row in range(SIDE):
            at = row * step
            spread_row(col, grad_in[at : at + step], row, images, True)
        block_weights(wg, number, blocks)
        for tap in range(9):
            turned[tap * BLK : (tap + 1) * BLK] = blocks[tap * BLK : (tap + 1) * BLK].astype(F32).T.astype(BF16)
        dp[:, span] = dot(col[...], turned[...])

    norm_sums(slope1, x1, st1)
    inner = col.at[:, 0:channels]
    load_inner = links.move(inner_in, inner, keep=False)
    if owners:
        g_grp = [
            links.send(raw_g.at[:, aligned(here.partner(k) * BLK, BLK)], g1.at[k - 1], here.across[k - 1])
            for k in range(1, grp)
        ]
    else:
        links.move(raw_g, group_out)
    sums1[...] = over_devices(st1, ex1, add_rows)
    if owners:
        arrived(e_over)
        e_last = add_over(e_slots)
        arrived(e_along)
        e_last += add_along(e_slots)

    @pl.loop(0, steps)
    def _(number):
        span = aligned(number * BLK, BLK)
        inverse = 1.0 / n1[2:3, span]
        factor = norm_all[0:1, span] * n1[1:2, span]
        for at in range(0, rows, step):
            mask = wide(m_ref[at : at + step], BLK)
            normed = x1[at : at + step, span].astype(F32)
            shift = (sums1[0:1, span] + normed * sums1[1:2, span]) * inverse
            x1[at : at + step, span] = (mask * factor * (dp[at : at + step, span] - shift)).astype(BF16)

    grad_reduce = x1
    load_inner.wait()
    per_r = raw_r.shape[3]

    @pl.loop(0, grp)
    def _(number):
        for part in range(0, own_in, BLK):
            span = pl.ds(pl.multiple_of(number * own_in + part, BLK), BLK)
            block = dot_left(col[:, span], grad_reduce[...]).astype(BF16)
            if per_r < BLK:
                for k in range(BLK // per_r):
                    b, c = divmod(part // per_r + k, raw_r.shape[2])
                    raw_r[number, b, c] = block[k * per_r : (k + 1) * per_r]
            else:
                raw_r[number, 0, 0, part : part + BLK] = block

    if owners:
        r_core = core_swap(raw_r, r_slots)
        arrived(g_grp)
        total = raw_g[:, aligned(me * BLK, BLK)].astype(F32)
        for k in range(grp - 1):
            total += g1[k].astype(F32)
        gs1[...] = total.astype(BF16)
        high = line // 2
        g_far = links.send(gs1.at[:, aligned((1 - high) * 128, 128)], g2, here.far)
        r_core.wait_recv()
        add_core(raw_r, r_slots)
        r_over, r_along = spread_sums(r_slots)
    else:
        links.move(raw_r, reduce_out)
    loads["wr"].wait()

    @pl.loop(0, grp)
    def _(number):
        for part in range(0, own_in, BLK):
            span = pl.ds(pl.multiple_of(number * own_in + part, BLK), BLK)
            per = wr.shape[3]
            if per < BLK:
                slots = [divmod(part // per + k, wr.shape[2]) for k in range(BLK // per)]
                weights = jnp.concatenate([wr[number, b, c] for b, c in slots], axis=0)
            else:
                weights = wr[number, 0, 0, part : part + BLK]
            total = grads[:, span].astype(F32) + dot_right(grad_reduce[...], weights)
            ge[:, part : part + BLK] = total.astype(BF16)
        grads[:, aligned(number * own_in, own_in)] = dot(back[...], ge[...]).astype(BF16)

    if owners:
        g_far.wait_recv()
        gs2[...] = (gs1[:, aligned(high * 128, 128)].astype(F32) + g2[...].astype(F32)).astype(BF16)
        g_near = links.send(gs2, g3, here.near)
        arrived(e_last)
        add_last(e_slots, expand_out)
        g_near.wait_recv()
        gs3[...] = (gs2[...].astype(F32) + g3[...].astype(F32)).astype(BF16)
        g_last = links.send(gs3, g4, here.sibling)
        arrived(r_over)
        r_last = add_over(r_slots)
    in_sends = [
        links.send(grads.at[:, aligned(here.partner(k) * own_in, own_in)], input_grad.at[own_rows], here.across[k - 1])
        for k in range(1, grp)
    ]
    links.move(grads.at[:, aligned(me * own_in, own_in)], input_grad.at[own_rows])
    if owners:
        g_last.wait_recv()
        turned_sum = (gs3[...].astype(F32) + g4[...].astype(F32)).T
        quarter = lax.rem(here.mine, 4)
        piece = turned_sum[0:GW]
        for k in range(1, 4):
            piece = jnp.where(quarter == k, turned_sum[k * GW : (k + 1) * GW], piece)
        group_out[...] = piece
        own_width = width // grp
        span = aligned(me * own_width, own_width)
        raws[3][0:1], raws[3][1:2] = sums1[1:2, span], sums1[0:1, span]
        raws[3][2:3], raws[3][3:4] = sums2[1:2, span], sums2[0:1, span]
        span = aligned(me * own_in, own_in)
        raws[4][0:1], raws[4][1:2] = sums3[1:2, span], sums3[0:1, span]
        arrived(r_along)
        r_last += add_along(r_slots)
        arrived(r_last)
        add_last(r_slots, reduce_out)
        trust(raws, state[:5], state[5:10], state[10:], scalars, trust_scratch[0], trust_scratch[1:8], trust_scratch[8:])
    arrived(out_sends)
    arrived(in_sends)
    links.close()


def backward(kept, block_out, mask, n1, n2, n3, norm_all, out_all, sums3, state, owners):
    grp = lax.axis_size("grp")
    rows, width = kept["act1"].shape
    channels = kept["x3"].shape[1]
    own_in = channels // grp
    r_shape, e_shape = kept["wr"].shape, kept["we"].shape
    lines = r_shape[1]
    vmem = pl.BlockSpec(memory_space=pltpu.VMEM)
    hbm = pl.BlockSpec(memory_space=pl.ANY)
    if owners:
        parts = [
            jax.ShapeDtypeStruct(r_shape[3:], F32),
            jax.ShapeDtypeStruct(e_shape[3:], F32),
            jax.ShapeDtypeStruct((GW, 9 * GW), F32),
        ]
        last = [
            jax.ShapeDtypeStruct((4, width // grp), F32),
            jax.ShapeDtypeStruct((2, own_in), F32),
            jax.ShapeDtypeStruct((8, 128), F32),
        ]
    else:
        last = []
        parts = [jax.ShapeDtypeStruct(shape, BF16) for shape in (r_shape, e_shape, (9 * GW, width))]
    sums = [jax.ShapeDtypeStruct((2, width), F32)] * 2
    scratch = [pltpu.VMEM(kept[name].shape, BF16) for name in BWD_INS] + [
        pltpu.VMEM((rows, own_in), BF16),
        pltpu.VMEM((rows, width), F32),
        pltpu.VMEM((rows, 9 * BLK), BF16),
        pltpu.VMEM((9 * BLK, BLK), BF16),
        pltpu.VMEM((9 * BLK, BLK), BF16),
        pltpu.VMEM((rows, BLK), BF16),
        pltpu.VMEM((rows, rows), BF16),
        pltpu.VMEM((2, width), F32),
        pltpu.VMEM((2, width), F32),
        pltpu.VMEM(e_shape, BF16),
        pltpu.VMEM(r_shape, BF16),
        pltpu.VMEM((9 * GW, width), BF16),
        pltpu.SemaphoreType.DMA((48,)),
        pltpu.SemaphoreType.DMA((48,)),
        pltpu.SemaphoreType.DMA((20,)),
    ]
    scratch += sums_scratch(2, width) + sums_scratch(2, width)
    if owners:
        for shape in (e_shape, r_shape):
            half = (shape[3] // 2, shape[4])
            scratch += [
                pltpu.VMEM((grp, lines, *shape[3:]), BF16),
                pltpu.VMEM((grp - 1, lines, *half), BF16),
                pltpu.VMEM((lines - 1, grp, *half), BF16),
                pltpu.VMEM((lines - 1, *half), BF16),
                pltpu.VMEM((grp - 1, *half), BF16),
            ]
        narrow = pltpu.VMEM((9 * GW, 128), BF16)
        scratch += [pltpu.VMEM((grp - 1, 9 * GW, BLK), BF16), narrow, narrow, narrow]
        scratch += [pltpu.VMEM((9 * GW, BLK), BF16), narrow, narrow]
        scratch += [pltpu.VMEM((2, 8, 128), F32)] + sums_scratch(8, 128) + sums_scratch(8, 128)
    whole = jax.ShapeDtypeStruct((grp * rows, own_in), BF16)
    return pl.pallas_call(
        functools.partial(backward_kernel, images=rows // HW, owners=owners),
        out_shape=[whole, whole, *parts, *sums, *last],
        in_specs=[hbm] * 14 + [vmem] * (7 + len(state)),
        out_specs=[hbm, hbm] + [vmem if owners else hbm] * 3 + [vmem] * (2 + len(last)),
        scratch_shapes=scratch,
        input_output_aliases={0: 0},
        compiler_params=params(collective_id=2, has_side_effects=True),
    )(
        block_out,
        kept["far"],
        kept["inner"],
        *[kept[name] for name in BWD_INS],
        mask,
        n1,
        n2,
        n3,
        norm_all,
        out_all,
        sums3,
        *state,
    )


DECAYS = (0.01, 0.01, 0.01, 0.0, 0.0)


def whole_sum(value):
    return jnp.sum(jnp.sum(value, axis=0, keepdims=True), axis=1, keepdims=True)


def adam_direction(tensor, clipped, moment_one, moment_two, decay_rate):
    new_first = beta_one * moment_one + (1.0 - beta_one) * clipped
    new_second = beta_two * moment_two + (1.0 - beta_two) * clipped * clipped
    first_hat = new_first / (1.0 - beta_one**step_count)
    second_hat = new_second / (1.0 - beta_two**step_count)
    direction = first_hat / (jnp.sqrt(second_hat) + adam_eps) + decay_rate * tensor
    return (new_first, new_second, direction)


def trust(raws, tensors, firsts, seconds, out_ref, pay, one, two):
    share = 1.0 / lax.axis_size("batch")
    shares = (1.0, 1.0, 1.0, share, share)
    square = jnp.zeros((1, 1), F32)
    pay[...] = jnp.zeros_like(pay)
    for number in range(5):
        square += shares[number] * whole_sum(raws[number][...] ** 2)
        weight = shares[number] * whole_sum(tensors[number][...] ** 2)
        pay[0, number + 1 : number + 2] = jnp.broadcast_to(weight, (1, 128))
    pay[0, 0:1] = jnp.broadcast_to(square, (1, 128))
    sums = over_devices(pay.at[0], one, add_rows)
    grad_norm = jnp.sqrt(sums[0:1])
    factor = jnp.minimum(1.0, clip_norm / grad_norm)
    for number in range(5):
        direction = adam_direction(
            tensors[number][...],
            factor[0:1, 0:1] * raws[number][...],
            firsts[number][...],
            seconds[number][...],
            DECAYS[number],
        )[2]
        step = shares[number] * whole_sum(direction * direction)
        pay[1, number + 1 : number + 2] = jnp.broadcast_to(step, (1, 128))
    steps = over_devices(pay.at[1], two, add_rows)
    out_ref[...] = jnp.zeros_like(out_ref)
    out_ref[0:1] = grad_norm
    out_ref[1:2] = factor
    out_ref[2:7] = jnp.sqrt(sums[1:6]) * lax.rsqrt(steps[1:6] + 1e-06)


def trust_kernel(*refs):
    raws, tensors, firsts, seconds = (refs[5 * k : 5 * k + 5] for k in range(4))
    greet(everyone())
    greeted(everyone())
    trust(raws, tensors, firsts, seconds, refs[20], refs[21], refs[22:29], refs[29:])


def update_kernel(*refs):
    scalars = refs[0]
    raws, tensors, firsts, seconds = (refs[5 * k + 1 : 5 * k + 6] for k in range(4))
    outs = refs[21:]
    at = 0
    for number in range(5):
        clipped = scalars[1:2, 0:1] * raws[number][...]
        tensor = tensors[number][...]
        new_first, new_second, direction = adam_direction(
            tensor, clipped, firsts[number][...], seconds[number][...], DECAYS[number]
        )
        updated = tensor - learn_rate * scalars[2 + number : 3 + number, 0:1] * direction
        values = [clipped, new_first, new_second, updated]
        if number < 3:
            values.append(updated.astype(BF16))
        for value in values:
            outs[at][...] = value
            at += 1


def trust_alone(raws, state):
    vmem = pl.BlockSpec(memory_space=pltpu.VMEM)
    return pl.pallas_call(
        trust_kernel,
        out_shape=jax.ShapeDtypeStruct((8, 128), F32),
        in_specs=[vmem] * 20,
        out_specs=vmem,
        scratch_shapes=[pltpu.VMEM((2, 8, 128), F32)] + sums_scratch(8, 128) + sums_scratch(8, 128),
        compiler_params=params(collective_id=3, has_side_effects=True),
    )(*raws, *state)


def update(scalars, raws, state):
    vmem = pl.BlockSpec(memory_space=pltpu.VMEM)
    shapes = []
    for number, tensor in enumerate(state[:5]):
        shapes += [jax.ShapeDtypeStruct(tensor.shape, F32)] * 4
        if number < 3:
            shapes.append(jax.ShapeDtypeStruct(tensor.shape, BF16))
    return pl.pallas_call(
        update_kernel,
        out_shape=shapes,
        in_specs=[vmem] * 21,
        out_specs=[vmem] * len(shapes),
        compiler_params=params(),
    )(scalars, *raws, *state)


def local(
    features,
    pixel_mask,
    out_cotangent,
    reduce_master,
    group_master,
    expand_master,
    norm_params,
    out_params,
    reduce_first,
    reduce_second,
    group_first,
    group_second,
    expand_first,
    expand_second,
    norm_first,
    norm_second,
    out_first,
    out_second,
):
    grp, batch = lax.axis_size("grp"), lax.axis_size("batch")
    both = ("grp", "batch")
    me = lax.axis_index("grp")
    rows = features.shape[0] // grp
    images = rows // HW
    own_in = features.shape[1]
    own_width = norm_params.shape[1]
    inside = batch == 8 and own_width == 8 * GW
    validity = lax.dynamic_slice_in_dim(pixel_mask, me * rows, rows, 0).astype(F32)
    mask = jnp.broadcast_to(validity.reshape(images, HW).T.reshape(rows, 1), (rows, 128))
    state = (
        *(reduce_master, group_master.T, expand_master, norm_params, out_params),
        *(reduce_first, group_first.T, expand_first, norm_first, out_first),
        *(reduce_second, group_second.T, expand_second, norm_second, out_second),
    )
    group_w = group_master.astype(BF16)
    if inside:
        reduce_w, expand_w = reduce_master, expand_master
        group_w = packed_groups(group_w)[0]
    else:
        reduce_w = lax.all_gather(reduce_master.astype(BF16), both, axis=0, tiled=True)
        expand_w = lax.all_gather(expand_master.astype(BF16), both, axis=0, tiled=True)
        group_w = packed_groups(lax.all_gather(group_w, both, axis=1, tiled=True))
    kept, block_out, (n1, n2, n3, norm_all, out_all, sums_three) = forward(
        features, out_cotangent, mask, norm_params, out_params, reduce_w, expand_w, group_w, inside
    )
    block_out, input_grad, reduce_part, expand_part, group_part, sums_one, sums_two, *last = backward(
        kept, block_out, mask, n1, n2, n3, norm_all, out_all, sums_three, state if inside else (), inside
    )
    if inside:
        norm_raw, out_raw, scalars = last
        raws = (reduce_part, group_part, expand_part, norm_raw, out_raw)
    else:
        flat = group_part.reshape(9 * GW, grp * batch, -1).transpose(1, 2, 0)
        reduce_part, expand_part, group_part = (
            lax.psum_scatter(value, both, scatter_dimension=0).astype(F32)
            for value in (
                reduce_part.reshape(grp * batch, own_in // batch, -1),
                expand_part.reshape(grp * batch, -1, own_in),
                flat,
            )
        )
        norm_sums = jnp.concatenate([sums_one[1:2], sums_one[0:1], sums_two[1:2], sums_two[0:1]], axis=0)
        norm_raw = lax.dynamic_slice_in_dim(norm_sums, me * own_width, own_width, 1)
        out_sums = jnp.concatenate([sums_three[1:2], sums_three[0:1]], axis=0)
        out_raw = lax.dynamic_slice_in_dim(out_sums, me * own_in, own_in, 1)
        raws = (reduce_part, group_part, expand_part, norm_raw, out_raw)
        scalars = trust_alone(raws, state)
    updates = list(update(scalars, raws, state))
    updates[5:10] = [value.T for value in updates[5:10]]
    return (block_out, input_grad, scalars[0, 0], scalars[2:5, 0], scalars[5:7, 0], *updates)


def solution(mesh):
    in_specs = (
        P("batch", "grp"),
        P("batch"),
        P("batch", "grp"),
        P(("grp", "batch"), None),
        P(None, ("grp", "batch")),
        P("batch", "grp"),
        P(None, "grp"),
        P(None, "grp"),
        P(("grp", "batch"), None),
        P(("grp", "batch"), None),
        P(None, ("grp", "batch")),
        P(None, ("grp", "batch")),
        P("batch", "grp"),
        P("batch", "grp"),
        P(None, "grp"),
        P(None, "grp"),
        P(None, "grp"),
        P(None, "grp"),
    )
    out_specs = (
        P("batch", "grp"),
        P("batch", "grp"),
        P(),
        P(),
        P(),
        P(("grp", "batch"), None),
        P(("grp", "batch"), None),
        P(("grp", "batch"), None),
        P(("grp", "batch"), None),
        P(("grp", "batch"), None),
        P(None, ("grp", "batch")),
        P(None, ("grp", "batch")),
        P(None, ("grp", "batch")),
        P(None, ("grp", "batch")),
        P(None, ("grp", "batch")),
        P("batch", "grp"),
        P("batch", "grp"),
        P("batch", "grp"),
        P("batch", "grp"),
        P("batch", "grp"),
        P(None, "grp"),
        P(None, "grp"),
        P(None, "grp"),
        P(None, "grp"),
        P(None, "grp"),
        P(None, "grp"),
        P(None, "grp"),
        P(None, "grp"),
    )
    return jax.shard_map(local, mesh=mesh, in_specs=in_specs, out_specs=out_specs, check_vma=False)
```

```python
import functools

import jax
import jax.numpy as jnp
from jax import lax
from jax.experimental import pallas as pl
from jax.experimental.pallas import tpu as pltpu
from jax.sharding import PartitionSpec as P

GW = 32
SIDE = 7
HW = SIDE * SIDE
BLK = 256

eps_norm = 1e-05
beta_one = 0.9
beta_two = 0.999
adam_eps = 1e-08
learn_rate = 0.25
step_count = 10.0
clip_norm = 1.0

MESH = pl.DeviceIdType.MESH
F32 = jnp.float32
BF16 = jnp.bfloat16
VMEM_LIMIT = 62 * 1024 * 1024


def params(**more):
    return pltpu.CompilerParams(vmem_limit_bytes=VMEM_LIMIT, **more)


def dot(a, b):
    return jnp.dot(a, b, preferred_element_type=F32)


def dot_left(a, b):
    return lax.dot_general(a, b, (((0,), (0,)), ((), ())), preferred_element_type=F32)


def dot_right(a, b):
    return lax.dot_general(a, b, (((1,), (1,)), ((), ())), preferred_element_type=F32)


def sigmoid(v):
    return 0.5 + 0.5 * jnp.tanh(0.5 * v)


def to_inner(rows, images):
    to = lax.broadcasted_iota(jnp.int32, (rows, rows), 0)
    source = (to % images) * HW + to // images
    at = lax.broadcasted_iota(jnp.int32, (rows, rows), 1)
    return jnp.where(at == source, 1.0, 0.0).astype(BF16)


def to_outer(rows, images):
    to = lax.broadcasted_iota(jnp.int32, (rows, rows), 0)
    source = (to % HW) * images + to // HW
    at = lax.broadcasted_iota(jnp.int32, (rows, rows), 1)
    return jnp.where(at == source, 1.0, 0.0).astype(BF16)


def wide(mask, columns):
    return jnp.concatenate([mask] * (columns // 128), axis=1)


def peers(axis):
    size = lax.axis_size(axis)
    mine = lax.axis_index(axis)
    return [{axis: lax.rem(mine + other, size)} for other in range(1, size)]


def greet(groups):
    barrier = pltpu.get_barrier_semaphore()
    for peer in groups:
        pl.semaphore_signal(barrier, inc=1, device_id=peer, device_id_type=MESH)


def greeted(groups):
    pl.semaphore_wait(pltpu.get_barrier_semaphore(), len(groups))


def everyone():
    return peers("grp") + peers("batch")


def sums_scratch(rows, columns):
    grp, batch = lax.axis_size("grp"), lax.axis_size("batch")
    return [
        pltpu.VMEM((grp - 1, rows, columns), F32),
        pltpu.VMEM((batch - 1, rows, columns), F32),
        pltpu.VMEM((rows, columns), F32),
        pltpu.SemaphoreType.DMA((grp - 1,)),
        pltpu.SemaphoreType.DMA((grp - 1,)),
        pltpu.SemaphoreType.DMA((batch - 1,)),
        pltpu.SemaphoreType.DMA((batch - 1,)),
    ]


def add_rows(parts):
    return functools.reduce(jnp.add, parts)


def merge_stats(parts):
    count = add_rows([part[2:3] for part in parts])
    total = add_rows([part[0:1] for part in parts])
    centre = total / count
    spread = add_rows([part[1:2] + part[2:3] * (part[0:1] / part[2:3] - centre) ** 2 for part in parts])
    return jnp.concatenate([total, spread, count], axis=0)


def over_devices(source, scratch, merge, beside=(None, None)):
    first, second, mid, *sems = scratch
    copies = []
    levels = (("grp", first, sems[0], sems[1], beside[0]), ("batch", second, sems[2], sems[3], beside[1]))
    for axis, slots, send, recv, meanwhile in levels:
        here = []
        for number, peer in enumerate(peers(axis)):
            copy = pltpu.make_async_remote_copy(
                source, slots.at[number], send.at[number], recv.at[number], device_id=peer, device_id_type=MESH
            )
            copy.start()
            here.append(copy)
        if meanwhile is not None:
            meanwhile()
        for copy in here:
            copy.wait_recv()
        copies += here
        merged = merge([source[...]] + [slots[number] for number in range(len(here))])
        if axis == "grp":
            mid[...] = merged
            source = mid
    for copy in copies:
        copy.wait_send()
    return merged


def norm_rows(merged):
    total, spread, count = merged[0:1], merged[1:2], merged[2:3]
    return jnp.concatenate([total / count, lax.rsqrt(spread / count + eps_norm), count], axis=0)


def clear_edges(col, images, reverse):
    for tap_row in range(3):
        for tap_col in range(3):
            tap = 3 * tap_row + tap_col
            dy, dx = (1 - tap_row, 1 - tap_col) if reverse else (tap_row - 1, tap_col - 1)
            for row in range(SIDE):
                for column in range(SIDE):
                    inside = 0 <= row + dy < SIDE and 0 <= column + dx < SIDE
                    if not inside:
                        at = (row * SIDE + column) * images
                        col[at : at + images, tap * BLK : (tap + 1) * BLK] = jnp.zeros((images, BLK), BF16)


def spread_row(col, value, row, images, reverse):
    for tap_row in range(3):
        for tap_col in range(3):
            tap = 3 * tap_row + tap_col
            dy, dx = (1 - tap_row, 1 - tap_col) if reverse else (tap_row - 1, tap_col - 1)
            to_row = row - dy
            if not 0 <= to_row < SIDE:
                continue
            first = max(0, dx)
            last = min(SIDE, SIDE + dx)
            at = (to_row * SIDE + first - dx) * images
            col[at : at + (last - first) * images, tap * BLK : (tap + 1) * BLK] = value[first * images : last * images]


class Links:
    def __init__(self, send, recv, local):
        self.send_sems, self.recv_sems, self.local_sems = send, recv, local
        self.sent = self.moved = 0
        self.open_sends, self.open_moves = [], []

    def send(self, source, target, peer, start=True):
        at = self.sent
        self.sent += 1
        copy = pltpu.make_async_remote_copy(
            source, target, self.send_sems.at[at], self.recv_sems.at[at], device_id=peer, device_id_type=MESH
        )
        if start:
            copy.start()
        self.open_sends.append(copy)
        return copy

    def move(self, source, target, keep=True):
        copy = pltpu.make_async_copy(source, target, self.local_sems.at[self.moved])
        self.moved += 1
        copy.start()
        if keep:
            self.open_moves.append(copy)
        return copy

    def close(self):
        for copy in self.open_sends:
            copy.wait_send()
        for copy in self.open_moves:
            copy.wait()


class Rounds:
    def __init__(self, rounds):
        self.rounds, self.at = rounds, 0

    def go(self, count=None):
        count = len(self.rounds) if count is None else count
        for copies in self.rounds[self.at : self.at + count]:
            for copy in copies:
                copy.start()
        self.at = min(self.at + count, len(self.rounds))

    def later(self, count=None):
        return lambda: self.go(count)

    def copies(self, first=0, last=None):
        return [copy for copies in self.rounds[first:last] for copy in copies]


def arrived(copies):
    for copy in copies:
        copy.wait_recv()


class Place:
    def __init__(self):
        grp, batch = lax.axis_size("grp"), lax.axis_size("batch")
        self.grp, self.lines = grp, batch // 2
        self.me, self.mine = lax.axis_index("grp"), lax.axis_index("batch")
        self.core, self.line = lax.rem(self.mine, 2), self.mine // 2
        self.sibling = {"batch": self.mine + 1 - 2 * self.core}
        self.across = [{"grp": self.partner(k)} for k in range(1, grp)]
        self.along = [{"batch": self.next_line(k) * 2 + self.core} for k in range(1, self.lines)]
        self.far = {"batch": (self.line + 2 - 4 * (self.line // 2)) * 2 + self.core}
        self.near = {"batch": (self.line + 1 - 2 * lax.rem(self.line, 2)) * 2 + self.core}

    def partner(self, k):
        low = lax.rem(lax.rem(self.me, 2) + (k % 2 if isinstance(k, int) else lax.rem(k, 2)), 2)
        return lax.rem(self.me // 2 + k // 2, 2) * 2 + low

    def next_line(self, k):
        return lax.rem(self.line + k, self.lines)


def partner_rounds(here, links, rows, part, pair, near=(0, None), far=(0, None)):
    rounds = []
    for ks, (first, last) in ((tuple(range(1, here.grp - 1)), near), ((here.grp - 1,), far)):
        for at in range(0, rows, part)[first:last]:
            copies = [links.send(*pair(k, pl.ds(at, part)), here.across[k - 1], start=False) for k in ks]
            rounds.append(copies)
    return rounds


def rows_of(index, rows, span):
    return pl.ds(pl.multiple_of(index * rows, rows) + span.start, span.size)


def aligned(at, size):
    return pl.ds(pl.multiple_of(at, size), size)


def block_weights(wg_ref, number, blocks):
    lanes = lax.broadcasted_iota(jnp.int32, (GW, 128), 1) // GW
    zero = jnp.zeros((GW, 128), BF16)
    for group in range(BLK // GW):
        for tap in range(9):
            piece = wg_ref[number, group // 2, group % 2, (tap // 4) * GW : (tap // 4 + 1) * GW].astype(F32)
            turn = ((group - tap) % 4) * GW
            if turn:
                piece = pltpu.roll(piece, turn, 1)
            piece = jnp.where(lanes == group % 4, piece, 0.0).astype(BF16)
            row = tap * BLK + group * GW
            left = (group // 4) * 128
            blocks[row : row + GW, left : left + 128] = piece
            blocks[row : row + GW, 128 - left : 256 - left] = zero


def block_stats(z_ref, left, columns, m_ref, st_ref, step):
    rows = z_ref.shape[0]
    for part in range(0, columns, BLK):
        span = pl.ds(pl.multiple_of(left + part, BLK), BLK)
        total = jnp.zeros((1, BLK), F32)
        count = jnp.zeros((1, 128), F32)
        for at in range(0, rows, step):
            mask = m_ref[at : at + step]
            total += jnp.sum(z_ref[at : at + step, span] * wide(mask, BLK), axis=0, keepdims=True)
            count += jnp.sum(mask, axis=0, keepdims=True)
        count = wide(count, BLK)
        centre = total / count
        spread = jnp.zeros((1, BLK), F32)
        for at in range(0, rows, step):
            off = (z_ref[at : at + step, span] - centre) * wide(m_ref[at : at + step], BLK)
            spread += jnp.sum(off * off, axis=0, keepdims=True)
        st_ref[0:1, span] = total
        st_ref[1:2, span] = spread
        st_ref[2:3, span] = count


def smooth(pre, mask):
    sigma = sigmoid(pre)
    masked = sigma * mask
    return pre * masked, masked * (1.0 + pre * (1.0 - sigma))


NEAR_ROUNDS = 3
FWD_OUTS = ("inner", "x1", "act1", "slope1", "x2", "act2", "slope2", "x3", "grads", "wr", "we", "wg", "far")


def forward_kernel(*refs, images, gather):
    (feat, cotg, m_ref, np_ref, op_ref, wr_in, we_in, wg_in) = refs[:8]
    big = dict(zip(FWD_OUTS, refs[8:21]))
    block_out, n1, n2, n3, norm_all, out_all, sums3 = refs[21:28]
    (inner, x1, act1, slope1, x2, act2, slope2, x3, grads, wr, we, wg) = refs[28:40]
    (land_f, land_c, cot, perm, back, z1, ze, col, blocks, st1, st2, st3, st4, send, recv, moves) = refs[40:56]
    ex1, ex2, ex3, ex4 = (refs[56 + 7 * k : 63 + 7 * k] for k in range(4))
    held = dict(zip(FWD_OUTS, (inner, x1, act1, slope1, x2, act2, slope2, x3, grads, wr, we, wg)))
    here = Place()
    grp = here.grp
    rows, own_in = land_f.shape[1:]
    width, channels = z1.shape[1], ze.shape[1]
    own_width = np_ref.shape[1]
    step = SIDE * images
    links = Links(send, recv, moves)

    greet(everyone())
    own_rows = aligned(here.me * rows, rows)
    own_f = links.move(feat.at[own_rows], land_f.at[0], keep=False)
    if gather:
        wr[here.me, here.line, here.core] = wr_in[...].astype(BF16)
        we[here.me, here.line, here.core] = we_in[...].astype(BF16)
        wg[here.me, here.line, here.core] = wg_in[...]
        loads = []
    else:
        loads = [links.move(wr_in, wr, keep=False), links.move(we_in, we, keep=False), links.move(wg_in, wg, keep=False)]
    norm_all[:, aligned(here.me * own_width, own_width)] = np_ref[...]
    out_all[:, aligned(here.me * own_in, own_in)] = op_ref[...]
    greeted(everyone())

    def spread_out(buffer, targets, rows=slice(None)):
        place = buffer.at[here.me, here.line, here.core, rows]
        return [links.send(place, place, peer) for peer in targets]

    if gather:
        quarter = wr.shape[3] // 4
        head, rest = pl.ds(0, quarter), pl.ds(quarter, 3 * quarter)
        half = we.shape[3] // 2
        lower, upper = pl.ds(0, half), pl.ds(half, half)
        wr_a = spread_out(wr, here.across, rest)
        wr_z = spread_out(wr, here.along, head)
    small = []
    for k in range(1, grp):
        peer = here.across[k - 1]
        span = aligned(here.me * own_width, own_width)
        small.append(links.send(np_ref, norm_all.at[:, span], peer))
        span = aligned(here.me * own_in, own_in)
        small.append(links.send(op_ref, out_all.at[:, span], peer))
    from_f = {}
    for k in range(1, grp):
        source = feat.at[aligned(here.partner(k) * rows, rows)]
        from_f[k] = links.send(source, land_f.at[k], here.across[k - 1])
    own_c = links.move(cotg.at[own_rows], land_c.at[0], keep=False)
    if gather:
        arrived(wr_a)
        place = wr.at[:, here.line, here.core, rest]
        wr_l = [links.send(place, place, peer) for peer in here.along]
        wr_b = [links.send(place, place, here.sibling)]
        arrived(wr_z)
        place = wr.at[here.me, :, here.core, head]
        wr_g = [links.send(place, place, peer) for peer in here.across]
        wg_a = spread_out(wg, here.along)
        we_a0 = spread_out(we, here.across, lower)
        we_a1 = spread_out(we, here.along, upper)
    perm[...] = to_inner(rows, images)
    back[...] = to_outer(rows, images)
    own_f.wait()
    for number in range(grp):
        if number:
            from_f[number].wait_recv()
        span = aligned(here.partner(number) * own_in, own_in)
        inner[:, span] = dot(perm[...], land_f[number]).astype(BF16)
    if gather:
        for k in range(1, here.lines):
            wr_l[k - 1].wait_recv()
            place = wr.at[:, here.next_line(here.lines - k), here.core, rest]
            wr_b.append(links.send(place, place, here.sibling))
        arrived(wr_g)
        place = wr.at[:, :, here.core, head]
        wr_b.append(links.send(place, place, here.sibling))
        arrived(wg_a)
        place = wg.at[here.me, :, here.core]
        wg_b = [links.send(place, place, peer) for peer in here.across]
        arrived(we_a0)
        arrived(we_a1)
        we_z = Rounds(
            [
                [
                    links.send(
                        we.at[a, here.line, here.core, lower], we.at[a, here.line, here.core, lower], peer, start=False
                    )
                    for peer in here.along
                ]
                for a in range(grp)
            ]
        )
        we_g = Rounds(
            [
                [
                    links.send(we.at[here.me, b, here.core, upper], we.at[here.me, b, here.core, upper], peer, start=False)
                    for peer in here.across
                ]
                for b in range(here.lines)
            ]
        )
        we_z.go(1)
        arrived(wr_b)
    for copy in loads:
        copy.wait()
    links.move(inner, big["inner"])

    steps = width // BLK

    @pl.loop(0, steps)
    def _(number):
        span = aligned(number * BLK, BLK)
        z1[:, span] = dot(inner[...], wr[:, :, :, :, span].reshape(channels, BLK))
        block_stats(z1, number * BLK, BLK, m_ref, st1, step)

    links.move(wr, big["wr"])
    arrived(small)
    from_c = Rounds(
        partner_rounds(
            here,
            links,
            rows,
            step,
            lambda k, span: (cotg.at[rows_of(here.partner(k), rows, span)], land_c.at[k, span]),
        )
    )
    wg_c = []

    def groups_on():
        if gather:
            arrived(wg_b)
            place = wg.at[:, :, here.core]
            wg_c.append(links.send(place, place, here.sibling))
            we_g.go(1)
            we_z.go(2)

    def expand_on():
        if gather:
            we_g.go(1)

    n1[...] = norm_rows(over_devices(st1, ex1, merge_stats, (expand_on, groups_on)))
    arrived(wg_c)
    if gather:
        we_g.go()

    clear_edges(col, images, False)

    @pl.loop(0, steps)
    def _(number):
        span = aligned(number * BLK, BLK)
        block_weights(wg, number, blocks)
        centre, scale = n1[0:1, span], n1[1:2, span]
        gain, bias = norm_all[0:1, span], norm_all[1:2, span]
        for row in range(SIDE):
            at = row * step
            mask = wide(m_ref[at : at + step], BLK)
            normed = (z1[at : at + step, span] - centre) * scale
            value, slope = smooth(normed * gain + bias, mask)
            act = value.astype(BF16)
            x1[at : at + step, span] = normed.astype(BF16)
            act1[at : at + step, span] = act
            slope1[at : at + step, span] = slope.astype(BF16)
            spread_row(col, act, row, images, False)
        z1[:, span] = dot(col[...], blocks[...])
        block_stats(z1, number * BLK, BLK, m_ref, st2, step)

    for name in ("x1", "act1", "slope1", "wg"):
        links.move(held[name], big[name])
    if gather:
        arrived(we_g.copies())
        arrived(we_z.copies(0, 3))
        place = we.at[:, :, here.core, upper]
        we_c = [links.send(place, place, here.sibling)]
        place = we.at[0 : grp - 1, :, here.core, lower]
        we_c.append(links.send(place, place, here.sibling))

    def expand_last():
        if gather:
            we_z.go()
        from_c.go(1)

    n2[...] = norm_rows(over_devices(st2, ex2, merge_stats, (from_c.later(1), expand_last)))
    from_c.go(2)

    @pl.loop(0, steps)
    def _(number):
        span = aligned(number * BLK, BLK)
        for at in range(0, rows, step):
            mask = wide(m_ref[at : at + step], BLK)
            normed = (z1[at : at + step, span] - n2[0:1, span]) * n2[1:2, span]
            value, slope = smooth(normed * norm_all[2:3, span] + norm_all[3:4, span], mask)
            x2[at : at + step, span] = normed.astype(BF16)
            act2[at : at + step, span] = value.astype(BF16)
            slope2[at : at + step, span] = slope.astype(BF16)

    for name in ("x2", "act2", "slope2"):
        links.move(held[name], big[name])
    from_c.go(3)
    if gather:
        arrived(we_z.copies(3))
        place = we.at[grp - 1, :, here.core, lower]
        we_c.append(links.send(place, place, here.sibling))
        arrived(we_c)
    links.move(we, big["we"])

    @pl.loop(0, grp)
    def _(number):
        for part in range(0, own_in, BLK):
            span = pl.ds(pl.multiple_of(number * own_in + part, BLK), BLK)
            ze[:, span] = dot(act2[...], we[number, :, :, :, part : part + BLK].reshape(width, BLK))
        block_stats(ze, number * own_in, own_in, m_ref, st3, step)

    n3[...] = norm_rows(over_devices(st3, ex3, merge_stats, (from_c.later(1), from_c.later(1))))
    from_c.go()
    own_c.wait()
    to_near = Rounds(
        partner_rounds(
            here,
            links,
            rows,
            step,
            lambda k, span: (land_f.at[k, span], block_out.at[rows_of(here.me, rows, span)]),
            near=(0, NEAR_ROUNDS),
            far=(0, 0),
        )
    )
    parts = SIDE
    arrived(from_c.copies(0, parts))

    def output_block(slot):
        number = here.partner(slot)
        cot[...] = dot(perm[...], land_c[slot])
        for part in range(0, own_in, BLK):
            span = pl.ds(pl.multiple_of(number * own_in + part, BLK), BLK)
            local = slice(part, part + BLK)
            bias_grad = jnp.zeros((1, BLK), F32)
            gain_grad = jnp.zeros((1, BLK), F32)
            for at in range(0, rows, step):
                mask = wide(m_ref[at : at + step], BLK)
                normed = (ze[at : at + step, span] - n3[0:1, span]) * n3[1:2, span]
                summed = normed * out_all[0:1, span] + out_all[1:2, span] + inner[at : at + step, span].astype(F32)
                value, slope = smooth(summed, mask)
                grad = cot[at : at + step, local] * slope
                x3[at : at + step, span] = normed.astype(BF16)
                col[at : at + step, local] = value.astype(BF16)
                grads[at : at + step, span] = grad.astype(BF16)
                bias_grad += jnp.sum(grad, axis=0, keepdims=True)
                gain_grad += jnp.sum(grad * normed, axis=0, keepdims=True)
            st4[0:1, span] = bias_grad
            st4[1:2, span] = gain_grad
        land_f[slot] = dot(back[...], col[:, 0:own_in]).astype(BF16)

    pl.loop(0, grp - 1)(output_block)
    to_near.go(1)
    arrived(from_c.copies(parts))
    output_block(grp - 1)
    links.move(land_f.at[0], block_out.at[own_rows])
    links.move(land_f.at[1:], big["far"])
    for name in ("x3", "grads"):
        links.move(held[name], big[name])
    sums3[...] = over_devices(st4, ex4, add_rows, (to_near.later(1), to_near.later()))
    arrived(to_near.copies())
    links.close()


def forward(features, out_cotangent, mask, norm_params, out_params, reduce_w, expand_w, group_w, gather):
    grp = lax.axis_size("grp")
    rows = features.shape[0] // grp
    own_in = features.shape[1]
    channels = own_in * grp
    width = norm_params.shape[1] * grp
    lines, cores = (lax.axis_size("batch") // 2, 2) if gather else (1, 1)
    r_shape = (grp, lines, cores, own_in // (lines * cores), width)
    e_shape = (grp, lines, cores, width // (lines * cores), own_in)
    g_shape = (width // BLK, BLK // GW // 2, 2, 3 * GW, 128)
    across = (rows, width)
    shapes = {
        "inner": (rows, channels),
        "x1": across,
        "act1": across,
        "slope1": across,
        "x2": across,
        "act2": across,
        "slope2": across,
        "x3": (rows, channels),
        "grads": (rows, channels),
        "far": (grp - 1, rows, own_in),
        "wr": r_shape,
        "we": e_shape,
        "wg": g_shape,
    }
    small = [(3, width), (3, width), (3, channels), (4, width), (2, channels), (2, channels)]
    vmem = pl.BlockSpec(memory_space=pltpu.VMEM)
    hbm = pl.BlockSpec(memory_space=pl.ANY)
    if gather:
        weights = (reduce_w, expand_w, group_w)
    else:
        weights = (reduce_w.reshape(r_shape), expand_w.reshape(e_shape), group_w.reshape(g_shape))
    results = pl.pallas_call(
        functools.partial(forward_kernel, images=rows // HW, gather=gather),
        out_shape=[jax.ShapeDtypeStruct(shapes[name], BF16) for name in FWD_OUTS]
        + [jax.ShapeDtypeStruct(features.shape, BF16)]
        + [jax.ShapeDtypeStruct(shape, F32) for shape in small],
        in_specs=[hbm, hbm, vmem, vmem, vmem] + [vmem if gather else hbm] * 3,
        out_specs=[hbm] * (len(FWD_OUTS) + 1) + [vmem] * len(small),
        scratch_shapes=[pltpu.VMEM(shapes[name], BF16) for name in FWD_OUTS[:-1]]
        + [
            pltpu.VMEM((grp, rows, own_in), BF16),
            pltpu.VMEM((grp, rows, own_in), BF16),
            pltpu.VMEM((rows, own_in), F32),
            pltpu.VMEM((rows, rows), BF16),
            pltpu.VMEM((rows, rows), BF16),
            pltpu.VMEM(across, F32),
            pltpu.VMEM((rows, channels), F32),
            pltpu.VMEM((rows, 9 * BLK), BF16),
            pltpu.VMEM((9 * BLK, BLK), BF16),
            pltpu.VMEM((3, width), F32),
            pltpu.VMEM((3, width), F32),
            pltpu.VMEM((3, channels), F32),
            pltpu.VMEM((2, channels), F32),
            pltpu.SemaphoreType.DMA((112,)),
            pltpu.SemaphoreType.DMA((112,)),
            pltpu.SemaphoreType.DMA((20,)),
        ]
        + sums_scratch(3, width)
        + sums_scratch(3, width)
        + sums_scratch(3, channels)
        + sums_scratch(2, channels),
        compiler_params=params(collective_id=1, has_side_effects=True),
    )(features, out_cotangent, mask, norm_params, out_params, *weights)
    return dict(zip(FWD_OUTS, results)), results[len(FWD_OUTS)], results[len(FWD_OUTS) + 1 :]


def packed_groups(weight):
    groups = weight.shape[1] // GW
    taps = jnp.pad(weight.reshape(9, GW, groups, GW), ((0, 3), (0, 0), (0, 0), (0, 0)))
    return taps.reshape(3, 4, GW, groups, GW).transpose(3, 0, 2, 1, 4).reshape(groups, 3 * GW, 4 * GW)


BWD_INS = ("grads", "x3", "we", "act2", "slope2", "x2", "act1", "slope1", "x1", "wg", "wr")


def backward_kernel(*refs, images, owners):
    _, far_in, inner_in = refs[:3]
    given = dict(zip(BWD_INS, refs[3:14]))
    m_ref, n1, n2, n3, norm_all, out_all, sums3 = refs[14:21]
    refs = refs[21:]
    state, refs = (refs[:15], refs[15:]) if owners else ((), refs)
    block_out, input_grad, reduce_out, expand_out, group_out, sums1, sums2 = refs[:7]
    raws, refs = ((reduce_out, group_out, expand_out, *refs[7:9]), refs[9:]) if owners else ((), refs[7:])
    scalars, refs = (refs[0], refs[1:]) if owners else (None, refs)
    (grads, x3, we, act2, slope2, x2, act1, slope1, x1, wg, wr) = refs[:11]
    held = dict(zip(BWD_INS, (grads, x3, we, act2, slope2, x2, act1, slope1, x1, wg, wr)))
    (ge, dp, col, blocks, turned, grad_in, back, st1, st2, raw_e, raw_r, raw_g, send, recv, moves) = refs[11:26]
    ex1, ex2 = refs[26:33], refs[33:40]
    here = Place()
    me, grp, core, line, lines = here.me, here.grp, here.core, here.line, here.lines
    rows, width = dp.shape
    channels = grads.shape[1]
    own_in = channels // grp
    step = SIDE * images
    steps = width // BLK
    links = Links(send, recv, moves)
    if owners:
        e_slots, r_slots = refs[40:45], refs[45:50]
        (g1, g2, g3, g4, gs1, gs2, gs3) = refs[50:57]
        trust_scratch = refs[57:]

    greet(everyone())
    loads = {name: links.move(given[name], held[name], keep=False) for name in BWD_INS[:4]}
    own_rows = aligned(me * rows, rows)
    back[...] = to_outer(rows, images)
    greeted(everyone())
    to_out = Rounds(
        partner_rounds(
            here,
            links,
            rows,
            step,
            lambda k, span: (far_in.at[k - 1, span], block_out.at[rows_of(me, rows, span)]),
            near=(NEAR_ROUNDS, None),
        )
    )
    to_out.go(7)

    def core_swap(raw, slots):
        return [
            links.send(raw.at[a, :, 1 - core], slots[0].at[a], here.sibling, start=False) for a in range(grp)
        ]

    def swap_now(copies, number):
        for a, copy in enumerate(copies):

            @pl.when(number == a)
            def _():
                copy.start()

    def add_core(raw, slots):
        @pl.loop(0, grp * lines)
        def _(at):
            a, b = at // lines, lax.rem(at, lines)
            slots[0][a, b] = (raw[a, b, core].astype(F32) + slots[0][a, b].astype(F32)).astype(BF16)

    def cuts(slots):
        cut, rest = slots[1].shape[2], slots[2].shape[2]
        return cut, pl.ds(0, cut), pl.ds(cut, rest)

    def spread_sums(slots):
        one, grp_slots, line_slots = slots[:3]
        _, lower, upper = cuts(slots)
        over = [
            links.send(one.at[here.partner(k), :, lower], grp_slots.at[k - 1], here.across[k - 1])
            for k in range(1, grp)
        ]
        along = [
            links.send(one.at[:, here.next_line(k), upper], line_slots.at[k - 1], here.along[k - 1])
            for k in range(1, lines)
        ]
        return over, along

    def add_over(slots):
        one, grp_slots = slots[:2]
        cut = cuts(slots)[0]

        @pl.loop(0, lines)
        def _(b):
            piece = one[me, b, 0:cut].astype(F32)
            for k in range(grp - 1):
                piece += grp_slots[k, b].astype(F32)
            grp_slots[0, b] = piece.astype(BF16)

        return [
            links.send(grp_slots.at[0, here.next_line(k)], slots[3].at[k - 1], here.along[k - 1])
            for k in range(1, lines)
        ]

    def add_along(slots):
        one, line_slots = slots[0], slots[2]
        cut = cuts(slots)[0]

        @pl.loop(0, grp)
        def _(a):
            piece = one[a, line, cut:].astype(F32)
            for k in range(lines - 1):
                piece += line_slots[k, a].astype(F32)
            line_slots[0, a] = piece.astype(BF16)

        return [
            links.send(line_slots.at[0, here.partner(k)], slots[4].at[k - 1], here.across[k - 1])
            for k in range(1, grp)
        ]

    def add_last(slots, out):
        cut = cuts(slots)[0]
        piece = slots[1][0, line].astype(F32)
        for k in range(lines - 1):
            piece += slots[3][k].astype(F32)
        out[0:cut] = piece
        piece = slots[2][0, me].astype(F32)
        for k in range(grp - 1):
            piece += slots[4][k].astype(F32)
        out[cut:] = piece

    for name in BWD_INS[:4]:
        loads[name].wait()
    loads.update({name: links.move(given[name], held[name], keep=False) for name in BWD_INS[4:]})
    if owners:
        e_core = core_swap(raw_e, e_slots)

    @pl.loop(0, grp)
    def _(number):
        for part in range(0, own_in, BLK):
            span = pl.ds(pl.multiple_of(number * own_in + part, BLK), BLK)
            inverse = 1.0 / n3[2:3, span]
            factor = out_all[0:1, span] * n3[1:2, span]
            for at in range(0, rows, step):
                mask = wide(m_ref[at : at + step], BLK)
                normed = x3[at : at + step, span].astype(F32)
                shift = (sums3[0:1, span] + normed * sums3[1:2, span]) * inverse
                value = mask * factor * (grads[at : at + step, span].astype(F32) - shift)
                ge[at : at + step, part : part + BLK] = value.astype(BF16)
        per = we.shape[3]
        taken = BLK // per if per < BLK else 1
        for left in range(0, width, BLK):
            if per < BLK:
                slots = [divmod(left // per + k, we.shape[2]) for k in range(taken)]
                weights = jnp.concatenate([we[number, b, c] for b, c in slots], axis=0)
            else:
                weights = we[number, 0, 0, left : left + BLK]
            part_sum = dot_right(ge[...], weights)
            block = dot_left(act2[:, left : left + BLK], ge[...]).astype(BF16)
            if per < BLK:
                for k, (b, c) in enumerate(slots):
                    raw_e[number, b, c] = block[k * per : (k + 1) * per]
            else:
                raw_e[number, 0, 0, left : left + BLK] = block

            @pl.when(number == 0)
            def _():
                dp[:, left : left + BLK] = part_sum

            @pl.when(number > 0)
            def _():
                dp[:, left : left + BLK] += part_sum

        if owners:
            swap_now(e_core, number)

    if not owners:
        links.move(raw_e, expand_out)
    for name in ("slope2", "x2"):
        loads[name].wait()

    def norm_sums(slope, normed, sums):
        @pl.loop(0, steps)
        def _(number):
            span = aligned(number * BLK, BLK)
            bias_grad = jnp.zeros((1, BLK), F32)
            gain_grad = jnp.zeros((1, BLK), F32)
            for at in range(0, rows, step):
                grad = dp[at : at + step, span] * slope[at : at + step, span].astype(F32)
                dp[at : at + step, span] = grad
                bias_grad += jnp.sum(grad, axis=0, keepdims=True)
                gain_grad += jnp.sum(grad * normed[at : at + step, span].astype(F32), axis=0, keepdims=True)
            sums[0:1, span] = bias_grad
            sums[1:2, span] = gain_grad

    norm_sums(slope2, x2, st2)
    sums2[...] = over_devices(st2, ex2, add_rows, (to_out.later(1), to_out.later(1)))
    if owners:
        arrived(e_core)
        add_core(raw_e, e_slots)
        e_over, e_along = spread_sums(e_slots)

    for name in ("act1", "slope1", "x1", "wg"):
        loads[name].wait()
    own = (
        lax.broadcasted_iota(jnp.int32, (BLK, BLK), 0) // GW == lax.broadcasted_iota(jnp.int32, (BLK, BLK), 1) // GW
    )

    @pl.loop(0, steps)
    def _(number):
        span = aligned(number * BLK, BLK)
        inverse = 1.0 / n2[2:3, span]
        factor = norm_all[2:3, span] * n2[1:2, span]
        clear_edges(col, images, False)
        for row in range(SIDE):
            at = row * step
            mask = wide(m_ref[at : at + step], BLK)
            normed = x2[at : at + step, span].astype(F32)
            shift = (sums2[0:1, span] + normed * sums2[1:2, span]) * inverse
            grad_in[at : at + step] = (mask * factor * (dp[at : at + step, span] - shift)).astype(BF16)
            spread_row(col, act1[at : at + step, span], row, images, False)
        for tap in range(9):
            product = dot_left(col[:, tap * BLK : (tap + 1) * BLK], grad_in[...])
            product = jnp.where(own, product, 0.0)
            piece = product[0:GW]
            for group in range(1, BLK // GW):
                piece += product[group * GW : (group + 1) * GW]
            raw_g[tap * GW : (tap + 1) * GW, span] = piece.astype(BF16)
        clear_edges(col, images, True)
        for row in range(SIDE):
            at = row * step
            spread_row(col, grad_in[at : at + step], row, images, True)
        block_weights(wg, number, blocks)
        for tap in range(9):
            turned[tap * BLK : (tap + 1) * BLK] = blocks[tap * BLK : (tap + 1) * BLK].astype(F32).T.astype(BF16)
        dp[:, span] = dot(col[...], turned[...])

    norm_sums(slope1, x1, st1)
    inner = col.at[:, 0:channels]
    load_inner = links.move(inner_in, inner, keep=False)
    g_grp = []

    def groups_on():
        if owners:
            g_grp.extend(
                links.send(raw_g.at[:, aligned(here.partner(k) * BLK, BLK)], g1.at[k - 1], here.across[k - 1])
                for k in range(1, grp)
            )

    if not owners:
        links.move(raw_g, group_out)
    sums1[...] = over_devices(st1, ex1, add_rows, (to_out.later(1), groups_on))
    if owners:
        arrived(e_over)
        e_last = add_over(e_slots)
        arrived(e_along)
        e_last += add_along(e_slots)
        r_core = core_swap(raw_r, r_slots)
    to_out.go()

    @pl.loop(0, steps)
    def _(number):
        span = aligned(number * BLK, BLK)
        inverse = 1.0 / n1[2:3, span]
        factor = norm_all[0:1, span] * n1[1:2, span]
        for at in range(0, rows, step):
            mask = wide(m_ref[at : at + step], BLK)
            normed = x1[at : at + step, span].astype(F32)
            shift = (sums1[0:1, span] + normed * sums1[1:2, span]) * inverse
            x1[at : at + step, span] = (mask * factor * (dp[at : at + step, span] - shift)).astype(BF16)

    grad_reduce = x1
    load_inner.wait()
    per_r = raw_r.shape[3]

    @pl.loop(0, grp)
    def _(number):
        for part in range(0, own_in, BLK):
            span = pl.ds(pl.multiple_of(number * own_in + part, BLK), BLK)
            block = dot_left(col[:, span], grad_reduce[...]).astype(BF16)
            if per_r < BLK:
                for k in range(BLK // per_r):
                    b, c = divmod(part // per_r + k, raw_r.shape[2])
                    raw_r[number, b, c] = block[k * per_r : (k + 1) * per_r]
            else:
                raw_r[number, 0, 0, part : part + BLK] = block
        if owners:
            swap_now(r_core, number)

    if owners:
        arrived(r_core)
        add_core(raw_r, r_slots)
        r_over, r_along = spread_sums(r_slots)
        arrived(g_grp)
        total = raw_g[:, aligned(me * BLK, BLK)].astype(F32)
        for k in range(grp - 1):
            total += g1[k].astype(F32)
        gs1[...] = total.astype(BF16)
        high = line // 2
        g_far = links.send(gs1.at[:, aligned((1 - high) * 128, 128)], g2, here.far)
    else:
        links.move(raw_r, reduce_out)
    loads["wr"].wait()

    @pl.loop(0, grp)
    def _(number):
        for part in range(0, own_in, BLK):
            span = pl.ds(pl.multiple_of(number * own_in + part, BLK), BLK)
            per = wr.shape[3]
            if per < BLK:
                slots = [divmod(part // per + k, wr.shape[2]) for k in range(BLK // per)]
                weights = jnp.concatenate([wr[number, b, c] for b, c in slots], axis=0)
            else:
                weights = wr[number, 0, 0, part : part + BLK]
            total = grads[:, span].astype(F32) + dot_right(grad_reduce[...], weights)
            ge[:, part : part + BLK] = total.astype(BF16)
        grads[:, aligned(number * own_in, own_in)] = dot(back[...], ge[...]).astype(BF16)

    to_in = Rounds(
        partner_rounds(
            here,
            links,
            rows,
            step,
            lambda k, span: (
                grads.at[span, aligned(here.partner(k) * own_in, own_in)],
                input_grad.at[rows_of(me, rows, span)],
            ),
        )
    )
    links.move(grads.at[:, aligned(me * own_in, own_in)], input_grad.at[own_rows])
    if owners:
        to_in.go(4)
        g_far.wait_recv()
        gs2[...] = (gs1[:, aligned(high * 128, 128)].astype(F32) + g2[...].astype(F32)).astype(BF16)
        g_near = links.send(gs2, g3, here.near)
        arrived(e_last)
        add_last(e_slots, expand_out)
        g_near.wait_recv()
        gs3[...] = (gs2[...].astype(F32) + g3[...].astype(F32)).astype(BF16)
        g_last = links.send(gs3, g4, here.sibling)
        own_width = width // grp
        span = aligned(me * own_width, own_width)
        raws[3][0:1], raws[3][1:2] = sums1[1:2, span], sums1[0:1, span]
        raws[3][2:3], raws[3][3:4] = sums2[1:2, span], sums2[0:1, span]
        span = aligned(me * own_in, own_in)
        raws[4][0:1], raws[4][1:2] = sums3[1:2, span], sums3[0:1, span]
        g_last.wait_recv()
        turned_sum = (gs3[...].astype(F32) + g4[...].astype(F32)).T
        quarter = lax.rem(here.mine, 4)
        piece = turned_sum[0:GW]
        for k in range(1, 4):
            piece = jnp.where(quarter == k, turned_sum[k * GW : (k + 1) * GW], piece)
        group_out[...] = piece
        arrived(r_over)
        r_last = add_over(r_slots)
        arrived(r_along)
        r_last += add_along(r_slots)
        to_in.go(1)
        arrived(r_last)
        add_last(r_slots, reduce_out)
        beside = (to_in.later(1), to_in.later(1), to_in.later(1), to_in.later())
        trust(
            raws,
            state[:5],
            state[5:10],
            state[10:],
            scalars,
            trust_scratch[0],
            trust_scratch[1:8],
            trust_scratch[8:],
            beside,
        )
    else:
        to_in.go()
    arrived(to_out.copies())
    arrived(to_in.copies())
    links.close()


def backward(kept, block_out, mask, n1, n2, n3, norm_all, out_all, sums3, state, owners):
    grp = lax.axis_size("grp")
    rows, width = kept["act1"].shape
    channels = kept["x3"].shape[1]
    own_in = channels // grp
    r_shape, e_shape = kept["wr"].shape, kept["we"].shape
    lines = r_shape[1]
    vmem = pl.BlockSpec(memory_space=pltpu.VMEM)
    hbm = pl.BlockSpec(memory_space=pl.ANY)
    if owners:
        parts = [
            jax.ShapeDtypeStruct(r_shape[3:], F32),
            jax.ShapeDtypeStruct(e_shape[3:], F32),
            jax.ShapeDtypeStruct((GW, 9 * GW), F32),
        ]
        last = [
            jax.ShapeDtypeStruct((4, width // grp), F32),
            jax.ShapeDtypeStruct((2, own_in), F32),
            jax.ShapeDtypeStruct((8, 128), F32),
        ]
    else:
        last = []
        parts = [jax.ShapeDtypeStruct(shape, BF16) for shape in (r_shape, e_shape, (9 * GW, width))]
    sums = [jax.ShapeDtypeStruct((2, width), F32)] * 2
    scratch = [pltpu.VMEM(kept[name].shape, BF16) for name in BWD_INS] + [
        pltpu.VMEM((rows, own_in), BF16),
        pltpu.VMEM((rows, width), F32),
        pltpu.VMEM((rows, 9 * BLK), BF16),
        pltpu.VMEM((9 * BLK, BLK), BF16),
        pltpu.VMEM((9 * BLK, BLK), BF16),
        pltpu.VMEM((rows, BLK), BF16),
        pltpu.VMEM((rows, rows), BF16),
        pltpu.VMEM((2, width), F32),
        pltpu.VMEM((2, width), F32),
        pltpu.VMEM(e_shape, BF16),
        pltpu.VMEM(r_shape, BF16),
        pltpu.VMEM((9 * GW, width), BF16),
        pltpu.SemaphoreType.DMA((96,)),
        pltpu.SemaphoreType.DMA((96,)),
        pltpu.SemaphoreType.DMA((20,)),
    ]
    scratch += sums_scratch(2, width) + sums_scratch(2, width)
    if owners:
        for shape in (e_shape, r_shape):
            cut = shape[3] * 5 // 128 * 16 if shape[3] > 64 else shape[3] // 2
            scratch += [
                pltpu.VMEM((grp, lines, *shape[3:]), BF16),
                pltpu.VMEM((grp - 1, lines, cut, shape[4]), BF16),
                pltpu.VMEM((lines - 1, grp, shape[3] - cut, shape[4]), BF16),
                pltpu.VMEM((lines - 1, cut, shape[4]), BF16),
                pltpu.VMEM((grp - 1, shape[3] - cut, shape[4]), BF16),
            ]
        narrow = pltpu.VMEM((9 * GW, 128), BF16)
        scratch += [pltpu.VMEM((grp - 1, 9 * GW, BLK), BF16), narrow, narrow, narrow]
        scratch += [pltpu.VMEM((9 * GW, BLK), BF16), narrow, narrow]
        scratch += [pltpu.VMEM((2, 8, 128), F32)] + sums_scratch(8, 128) + sums_scratch(8, 128)
    whole = jax.ShapeDtypeStruct((grp * rows, own_in), BF16)
    return pl.pallas_call(
        functools.partial(backward_kernel, images=rows // HW, owners=owners),
        out_shape=[whole, whole, *parts, *sums, *last],
        in_specs=[hbm] * 14 + [vmem] * (7 + len(state)),
        out_specs=[hbm, hbm] + [vmem if owners else hbm] * 3 + [vmem] * (2 + len(last)),
        scratch_shapes=scratch,
        input_output_aliases={0: 0},
        compiler_params=params(collective_id=2, has_side_effects=True),
    )(
        block_out,
        kept["far"],
        kept["inner"],
        *[kept[name] for name in BWD_INS],
        mask,
        n1,
        n2,
        n3,
        norm_all,
        out_all,
        sums3,
        *state,
    )


DECAYS = (0.01, 0.01, 0.01, 0.0, 0.0)


def whole_sum(value):
    return jnp.sum(jnp.sum(value, axis=0, keepdims=True), axis=1, keepdims=True)


def adam_direction(tensor, clipped, moment_one, moment_two, decay_rate):
    new_first = beta_one * moment_one + (1.0 - beta_one) * clipped
    new_second = beta_two * moment_two + (1.0 - beta_two) * clipped * clipped
    first_hat = new_first / (1.0 - beta_one**step_count)
    second_hat = new_second / (1.0 - beta_two**step_count)
    direction = first_hat / (jnp.sqrt(second_hat) + adam_eps) + decay_rate * tensor
    return (new_first, new_second, direction)


def trust(raws, tensors, firsts, seconds, out_ref, pay, one, two, beside=(None,) * 4):
    share = 1.0 / lax.axis_size("batch")
    shares = (1.0, 1.0, 1.0, share, share)
    square = jnp.zeros((1, 1), F32)
    pay[...] = jnp.zeros_like(pay)
    for number in range(5):
        square += shares[number] * whole_sum(raws[number][...] ** 2)
        weight = shares[number] * whole_sum(tensors[number][...] ** 2)
        pay[0, number + 1 : number + 2] = jnp.broadcast_to(weight, (1, 128))
    pay[0, 0:1] = jnp.broadcast_to(square, (1, 128))
    sums = over_devices(pay.at[0], one, add_rows, beside[:2])
    grad_norm = jnp.sqrt(sums[0:1])
    factor = jnp.minimum(1.0, clip_norm / grad_norm)
    for number in range(5):
        direction = adam_direction(
            tensors[number][...],
            factor[0:1, 0:1] * raws[number][...],
            firsts[number][...],
            seconds[number][...],
            DECAYS[number],
        )[2]
        step = shares[number] * whole_sum(direction * direction)
        pay[1, number + 1 : number + 2] = jnp.broadcast_to(step, (1, 128))
    steps = over_devices(pay.at[1], two, add_rows, beside[2:])
    out_ref[...] = jnp.zeros_like(out_ref)
    out_ref[0:1] = grad_norm
    out_ref[1:2] = factor
    out_ref[2:7] = jnp.sqrt(sums[1:6]) * lax.rsqrt(steps[1:6] + 1e-06)


def trust_kernel(*refs):
    raws, tensors, firsts, seconds = (refs[5 * k : 5 * k + 5] for k in range(4))
    greet(everyone())
    greeted(everyone())
    trust(raws, tensors, firsts, seconds, refs[20], refs[21], refs[22:29], refs[29:])


def update_kernel(*refs):
    scalars = refs[0]
    raws, tensors, firsts, seconds = (refs[5 * k + 1 : 5 * k + 6] for k in range(4))
    outs = refs[21:]
    at = 0
    for number in range(5):
        clipped = scalars[1:2, 0:1] * raws[number][...]
        tensor = tensors[number][...]
        new_first, new_second, direction = adam_direction(
            tensor, clipped, firsts[number][...], seconds[number][...], DECAYS[number]
        )
        updated = tensor - learn_rate * scalars[2 + number : 3 + number, 0:1] * direction
        values = [clipped, new_first, new_second, updated]
        if number < 3:
            values.append(updated.astype(BF16))
        for value in values:
            outs[at][...] = value
            at += 1


def trust_alone(raws, state):
    vmem = pl.BlockSpec(memory_space=pltpu.VMEM)
    return pl.pallas_call(
        trust_kernel,
        out_shape=jax.ShapeDtypeStruct((8, 128), F32),
        in_specs=[vmem] * 20,
        out_specs=vmem,
        scratch_shapes=[pltpu.VMEM((2, 8, 128), F32)] + sums_scratch(8, 128) + sums_scratch(8, 128),
        compiler_params=params(collective_id=3, has_side_effects=True),
    )(*raws, *state)


def update(scalars, raws, state):
    vmem = pl.BlockSpec(memory_space=pltpu.VMEM)
    shapes = []
    for number, tensor in enumerate(state[:5]):
        shapes += [jax.ShapeDtypeStruct(tensor.shape, F32)] * 4
        if number < 3:
            shapes.append(jax.ShapeDtypeStruct(tensor.shape, BF16))
    return pl.pallas_call(
        update_kernel,
        out_shape=shapes,
        in_specs=[vmem] * 21,
        out_specs=[vmem] * len(shapes),
        compiler_params=params(),
    )(scalars, *raws, *state)


def local(
    features,
    pixel_mask,
    out_cotangent,
    reduce_master,
    group_master,
    expand_master,
    norm_params,
    out_params,
    reduce_first,
    reduce_second,
    group_first,
    group_second,
    expand_first,
    expand_second,
    norm_first,
    norm_second,
    out_first,
    out_second,
):
    grp, batch = lax.axis_size("grp"), lax.axis_size("batch")
    both = ("grp", "batch")
    me = lax.axis_index("grp")
    rows = features.shape[0] // grp
    images = rows // HW
    own_in = features.shape[1]
    own_width = norm_params.shape[1]
    inside = batch == 8 and own_width == 8 * GW
    validity = lax.dynamic_slice_in_dim(pixel_mask, me * rows, rows, 0).astype(F32)
    mask = jnp.broadcast_to(validity.reshape(images, HW).T.reshape(rows, 1), (rows, 128))
    state = (
        *(reduce_master, group_master.T, expand_master, norm_params, out_params),
        *(reduce_first, group_first.T, expand_first, norm_first, out_first),
        *(reduce_second, group_second.T, expand_second, norm_second, out_second),
    )
    group_w = group_master.astype(BF16)
    if inside:
        reduce_w, expand_w = reduce_master, expand_master
        group_w = packed_groups(group_w)[0]
    else:
        reduce_w = lax.all_gather(reduce_master.astype(BF16), both, axis=0, tiled=True)
        expand_w = lax.all_gather(expand_master.astype(BF16), both, axis=0, tiled=True)
        group_w = packed_groups(lax.all_gather(group_w, both, axis=1, tiled=True))
    kept, block_out, (n1, n2, n3, norm_all, out_all, sums_three) = forward(
        features, out_cotangent, mask, norm_params, out_params, reduce_w, expand_w, group_w, inside
    )
    block_out, input_grad, reduce_part, expand_part, group_part, sums_one, sums_two, *last = backward(
        kept, block_out, mask, n1, n2, n3, norm_all, out_all, sums_three, state if inside else (), inside
    )
    if inside:
        norm_raw, out_raw, scalars = last
        raws = (reduce_part, group_part, expand_part, norm_raw, out_raw)
    else:
        flat = group_part.reshape(9 * GW, grp * batch, -1).transpose(1, 2, 0)
        reduce_part, expand_part, group_part = (
            lax.psum_scatter(value, both, scatter_dimension=0).astype(F32)
            for value in (
                reduce_part.reshape(grp * batch, own_in // batch, -1),
                expand_part.reshape(grp * batch, -1, own_in),
                flat,
            )
        )
        norm_sums = jnp.concatenate([sums_one[1:2], sums_one[0:1], sums_two[1:2], sums_two[0:1]], axis=0)
        norm_raw = lax.dynamic_slice_in_dim(norm_sums, me * own_width, own_width, 1)
        out_sums = jnp.concatenate([sums_three[1:2], sums_three[0:1]], axis=0)
        out_raw = lax.dynamic_slice_in_dim(out_sums, me * own_in, own_in, 1)
        raws = (reduce_part, group_part, expand_part, norm_raw, out_raw)
        scalars = trust_alone(raws, state)
    updates = list(update(scalars, raws, state))
    updates[5:10] = [value.T for value in updates[5:10]]
    return (block_out, input_grad, scalars[0, 0], scalars[2:5, 0], scalars[5:7, 0], *updates)


def solution(mesh):
    in_specs = (
        P("batch", "grp"),
        P("batch"),
        P("batch", "grp"),
        P(("grp", "batch"), None),
        P(None, ("grp", "batch")),
        P("batch", "grp"),
        P(None, "grp"),
        P(None, "grp"),
        P(("grp", "batch"), None),
        P(("grp", "batch"), None),
        P(None, ("grp", "batch")),
        P(None, ("grp", "batch")),
        P("batch", "grp"),
        P("batch", "grp"),
        P(None, "grp"),
        P(None, "grp"),
        P(None, "grp"),
        P(None, "grp"),
    )
    out_specs = (
        P("batch", "grp"),
        P("batch", "grp"),
        P(),
        P(),
        P(),
        P(("grp", "batch"), None),
        P(("grp", "batch"), None),
        P(("grp", "batch"), None),
        P(("grp", "batch"), None),
        P(("grp", "batch"), None),
        P(None, ("grp", "batch")),
        P(None, ("grp", "batch")),
        P(None, ("grp", "batch")),
        P(None, ("grp", "batch")),
        P(None, ("grp", "batch")),
        P("batch", "grp"),
        P("batch", "grp"),
        P("batch", "grp"),
        P("batch", "grp"),
        P("batch", "grp"),
        P(None, "grp"),
        P(None, "grp"),
        P(None, "grp"),
        P(None, "grp"),
        P(None, "grp"),
        P(None, "grp"),
        P(None, "grp"),
        P(None, "grp"),
    )
    return jax.shard_map(local, mesh=mesh, in_specs=in_specs, out_specs=out_specs, check_vma=False)
```

```python
import functools

import jax
import jax.numpy as jnp
from jax import lax
from jax.experimental import pallas as pl
from jax.experimental.pallas import tpu as pltpu
from jax.sharding import PartitionSpec as P

GW = 32
SIDE = 7
HW = SIDE * SIDE
BLK = 256

eps_norm = 1e-05
beta_one = 0.9
beta_two = 0.999
adam_eps = 1e-08
learn_rate = 0.25
step_count = 10.0
clip_norm = 1.0

MESH = pl.DeviceIdType.MESH
F32 = jnp.float32
BF16 = jnp.bfloat16
VMEM_LIMIT = 62 * 1024 * 1024


def params(**more):
    return pltpu.CompilerParams(vmem_limit_bytes=VMEM_LIMIT, **more)


def dot(a, b):
    return jnp.dot(a, b, preferred_element_type=F32)


def dot_left(a, b):
    return lax.dot_general(a, b, (((0,), (0,)), ((), ())), preferred_element_type=F32)


def dot_right(a, b):
    return lax.dot_general(a, b, (((1,), (1,)), ((), ())), preferred_element_type=F32)


def sigmoid(v):
    return 0.5 + 0.5 * jnp.tanh(0.5 * v)


def to_inner(rows, images):
    to = lax.broadcasted_iota(jnp.int32, (rows, rows), 0)
    source = (to % images) * HW + to // images
    at = lax.broadcasted_iota(jnp.int32, (rows, rows), 1)
    return jnp.where(at == source, 1.0, 0.0).astype(BF16)


def to_outer(rows, images):
    to = lax.broadcasted_iota(jnp.int32, (rows, rows), 0)
    source = (to % HW) * images + to // HW
    at = lax.broadcasted_iota(jnp.int32, (rows, rows), 1)
    return jnp.where(at == source, 1.0, 0.0).astype(BF16)


def wide(mask, columns):
    return jnp.concatenate([mask] * (columns // 128), axis=1)


def peers(axis):
    size = lax.axis_size(axis)
    mine = lax.axis_index(axis)
    return [{axis: lax.rem(mine + other, size)} for other in range(1, size)]


def greet(groups):
    barrier = pltpu.get_barrier_semaphore()
    for peer in groups:
        pl.semaphore_signal(barrier, inc=1, device_id=peer, device_id_type=MESH)


def greeted(groups):
    pl.semaphore_wait(pltpu.get_barrier_semaphore(), len(groups))


def everyone():
    return peers("grp") + peers("batch")


def sums_scratch(rows, columns):
    grp, batch = lax.axis_size("grp"), lax.axis_size("batch")
    return [
        pltpu.VMEM((grp - 1, rows, columns), F32),
        pltpu.VMEM((batch - 1, rows, columns), F32),
        pltpu.VMEM((rows, columns), F32),
        pltpu.SemaphoreType.DMA((grp - 1,)),
        pltpu.SemaphoreType.DMA((grp - 1,)),
        pltpu.SemaphoreType.DMA((batch - 1,)),
        pltpu.SemaphoreType.DMA((batch - 1,)),
    ]


def add_rows(parts):
    return functools.reduce(jnp.add, parts)


def merge_stats(parts):
    count = add_rows([part[2:3] for part in parts])
    total = add_rows([part[0:1] for part in parts])
    centre = total / count
    spread = add_rows([part[1:2] + part[2:3] * (part[0:1] / part[2:3] - centre) ** 2 for part in parts])
    return jnp.concatenate([total, spread, count], axis=0)


def over_devices(source, scratch, merge, beside=(None, None)):
    first, second, mid, *sems = scratch
    copies = []
    levels = (("grp", first, sems[0], sems[1], beside[0]), ("batch", second, sems[2], sems[3], beside[1]))
    for axis, slots, send, recv, meanwhile in levels:
        here = []
        for number, peer in enumerate(peers(axis)):
            copy = pltpu.make_async_remote_copy(
                source, slots.at[number], send.at[number], recv.at[number], device_id=peer, device_id_type=MESH
            )
            copy.start()
            here.append(copy)
        if meanwhile is not None:
            meanwhile()
        for copy in here:
            copy.wait_recv()
        copies += here
        merged = merge([source[...]] + [slots[number] for number in range(len(here))])
        if axis == "grp":
            mid[...] = merged
            source = mid
    for copy in copies:
        copy.wait_send()
    return merged


def norm_rows(merged):
    total, spread, count = merged[0:1], merged[1:2], merged[2:3]
    return jnp.concatenate([total / count, lax.rsqrt(spread / count + eps_norm), count], axis=0)


def clear_edges(col, images, reverse):
    for tap_row in range(3):
        for tap_col in range(3):
            tap = 3 * tap_row + tap_col
            dy, dx = (1 - tap_row, 1 - tap_col) if reverse else (tap_row - 1, tap_col - 1)
            for row in range(SIDE):
                for column in range(SIDE):
                    inside = 0 <= row + dy < SIDE and 0 <= column + dx < SIDE
                    if not inside:
                        at = (row * SIDE + column) * images
                        col[at : at + images, tap * BLK : (tap + 1) * BLK] = jnp.zeros((images, BLK), BF16)


def spread_row(col, value, row, images, reverse):
    for tap_row in range(3):
        for tap_col in range(3):
            tap = 3 * tap_row + tap_col
            dy, dx = (1 - tap_row, 1 - tap_col) if reverse else (tap_row - 1, tap_col - 1)
            to_row = row - dy
            if not 0 <= to_row < SIDE:
                continue
            first = max(0, dx)
            last = min(SIDE, SIDE + dx)
            at = (to_row * SIDE + first - dx) * images
            col[at : at + (last - first) * images, tap * BLK : (tap + 1) * BLK] = value[first * images : last * images]


class Links:
    def __init__(self, send, recv, local):
        self.send_sems, self.recv_sems, self.local_sems = send, recv, local
        self.sent = self.moved = 0
        self.open_sends, self.open_moves = [], []

    def send(self, source, target, peer, start=True):
        at = self.sent
        self.sent += 1
        copy = pltpu.make_async_remote_copy(
            source, target, self.send_sems.at[at], self.recv_sems.at[at], device_id=peer, device_id_type=MESH
        )
        if start:
            copy.start()
        self.open_sends.append(copy)
        return copy

    def move(self, source, target, keep=True):
        copy = pltpu.make_async_copy(source, target, self.local_sems.at[self.moved])
        self.moved += 1
        copy.start()
        if keep:
            self.open_moves.append(copy)
        return copy

    def close(self):
        for copy in self.open_sends:
            copy.wait_send()
        for copy in self.open_moves:
            copy.wait()


class Rounds:
    def __init__(self, rounds):
        self.rounds, self.at = rounds, 0

    def go(self, count=None):
        count = len(self.rounds) if count is None else count
        for copies in self.rounds[self.at : self.at + count]:
            for copy in copies:
                copy.start()
        self.at = min(self.at + count, len(self.rounds))

    def later(self, count=None):
        return lambda: self.go(count)

    def copies(self, first=0, last=None):
        return [copy for copies in self.rounds[first:last] for copy in copies]


def arrived(copies):
    for copy in copies:
        copy.wait_recv()


class Place:
    def __init__(self):
        grp, batch = lax.axis_size("grp"), lax.axis_size("batch")
        self.grp, self.lines = grp, batch // 2
        self.me, self.mine = lax.axis_index("grp"), lax.axis_index("batch")
        self.core, self.line = lax.rem(self.mine, 2), self.mine // 2
        self.sibling = {"batch": self.mine + 1 - 2 * self.core}
        self.across = [{"grp": self.partner(k)} for k in range(1, grp)]
        self.along = [{"batch": self.next_line(k) * 2 + self.core} for k in range(1, self.lines)]
        self.far = {"batch": (self.line + 2 - 4 * (self.line // 2)) * 2 + self.core}
        self.near = {"batch": (self.line + 1 - 2 * lax.rem(self.line, 2)) * 2 + self.core}

    def partner(self, k):
        low = lax.rem(lax.rem(self.me, 2) + (k % 2 if isinstance(k, int) else lax.rem(k, 2)), 2)
        return lax.rem(self.me // 2 + k // 2, 2) * 2 + low

    def next_line(self, k):
        return lax.rem(self.line + k, self.lines)


def partner_rounds(here, links, rows, part, pair, near=(0, None), far=(0, None)):
    rounds = []
    for ks, (first, last) in ((tuple(range(1, here.grp - 1)), near), ((here.grp - 1,), far)):
        for at in range(0, rows, part)[first:last]:
            copies = [links.send(*pair(k, pl.ds(at, part)), here.across[k - 1], start=False) for k in ks]
            rounds.append(copies)
    return rounds


def rows_of(index, rows, span):
    return pl.ds(pl.multiple_of(index * rows, rows) + span.start, span.size)


def aligned(at, size):
    return pl.ds(pl.multiple_of(at, size), size)


def block_weights(wg_ref, number, blocks):
    lanes = lax.broadcasted_iota(jnp.int32, (GW, 128), 1) // GW
    zero = jnp.zeros((GW, 128), BF16)
    for group in range(BLK // GW):
        for tap in range(9):
            piece = wg_ref[number, group // 2, group % 2, (tap // 4) * GW : (tap // 4 + 1) * GW].astype(F32)
            turn = ((group - tap) % 4) * GW
            if turn:
                piece = pltpu.roll(piece, turn, 1)
            piece = jnp.where(lanes == group % 4, piece, 0.0).astype(BF16)
            row = tap * BLK + group * GW
            left = (group // 4) * 128
            blocks[row : row + GW, left : left + 128] = piece
            blocks[row : row + GW, 128 - left : 256 - left] = zero


def block_stats(z_ref, left, columns, m_ref, st_ref, step):
    rows = z_ref.shape[0]
    for part in range(0, columns, BLK):
        span = pl.ds(pl.multiple_of(left + part, BLK), BLK)
        total = jnp.zeros((1, BLK), F32)
        count = jnp.zeros((1, 128), F32)
        for at in range(0, rows, step):
            mask = m_ref[at : at + step]
            total += jnp.sum(z_ref[at : at + step, span] * wide(mask, BLK), axis=0, keepdims=True)
            count += jnp.sum(mask, axis=0, keepdims=True)
        count = wide(count, BLK)
        centre = total / count
        spread = jnp.zeros((1, BLK), F32)
        for at in range(0, rows, step):
            off = (z_ref[at : at + step, span] - centre) * wide(m_ref[at : at + step], BLK)
            spread += jnp.sum(off * off, axis=0, keepdims=True)
        st_ref[0:1, span] = total
        st_ref[1:2, span] = spread
        st_ref[2:3, span] = count


def smooth(pre, mask):
    sigma = sigmoid(pre)
    masked = sigma * mask
    return pre * masked, masked * (1.0 + pre * (1.0 - sigma))


NEAR_ROUNDS = 3
FWD_OUTS = ("inner", "x1", "act1", "slope1", "x2", "act2", "slope2", "x3", "grads", "wr", "we", "wg", "far")


def forward_kernel(*refs, images, gather):
    (feat, cotg, m_ref, np_ref, op_ref, wr_in, we_in, wg_in) = refs[:8]
    big = dict(zip(FWD_OUTS, refs[8:21]))
    block_out, n1, n2, n3, norm_all, out_all, sums3 = refs[21:28]
    (inner, x1, act1, slope1, x2, act2, slope2, x3, grads, wr, we, wg) = refs[28:40]
    (land_f, land_c, cot, perm, back, z1, ze, col, blocks, st1, st2, st3, st4, send, recv, moves) = refs[40:56]
    ex1, ex2, ex3, ex4 = (refs[56 + 7 * k : 63 + 7 * k] for k in range(4))
    held = dict(zip(FWD_OUTS, (inner, x1, act1, slope1, x2, act2, slope2, x3, grads, wr, we, wg)))
    here = Place()
    grp = here.grp
    rows, own_in = land_f.shape[1:]
    width, channels = z1.shape[1], ze.shape[1]
    own_width = np_ref.shape[1]
    step = SIDE * images
    links = Links(send, recv, moves)

    greet(everyone())
    own_rows = aligned(here.me * rows, rows)
    own_f = links.move(feat.at[own_rows], land_f.at[0], keep=False)
    if gather:
        shard_r, shard_e = refs[84:86]
        shards = [
            links.move(wr_in, shard_r, keep=False),
            links.move(we_in, shard_e, keep=False),
            links.move(wg_in, wg.at[here.me, here.line, here.core], keep=False),
        ]
        for copy in shards:
            copy.wait()
        wr[here.me, here.line, here.core] = shard_r[...].astype(BF16)
        we[here.me, here.line, here.core] = shard_e[...].astype(BF16)
        loads = []
    else:
        loads = [links.move(wr_in, wr, keep=False), links.move(we_in, we, keep=False), links.move(wg_in, wg, keep=False)]
    norm_all[:, aligned(here.me * own_width, own_width)] = np_ref[...]
    out_all[:, aligned(here.me * own_in, own_in)] = op_ref[...]
    greeted(everyone())

    def spread_out(buffer, targets, rows=slice(None)):
        place = buffer.at[here.me, here.line, here.core, rows]
        return [links.send(place, place, peer) for peer in targets]

    if gather:
        quarter = wr.shape[3] // 4
        head, rest = pl.ds(0, quarter), pl.ds(quarter, 3 * quarter)
        half = we.shape[3] // 2
        lower, upper = pl.ds(0, half), pl.ds(half, half)
        wr_a = spread_out(wr, here.across, rest)
        wr_z = spread_out(wr, here.along, head)
    small = []
    for k in range(1, grp):
        peer = here.across[k - 1]
        span = aligned(here.me * own_width, own_width)
        small.append(links.send(np_ref, norm_all.at[:, span], peer))
        span = aligned(here.me * own_in, own_in)
        small.append(links.send(op_ref, out_all.at[:, span], peer))
    from_f = {}
    for k in range(1, grp):
        source = feat.at[aligned(here.partner(k) * rows, rows)]
        from_f[k] = links.send(source, land_f.at[k], here.across[k - 1])
    own_c = links.move(cotg.at[own_rows], land_c.at[0], keep=False)
    if gather:
        arrived(wr_a)
        place = wr.at[:, here.line, here.core, rest]
        wr_l = [links.send(place, place, peer) for peer in here.along]
        wr_b = [links.send(place, place, here.sibling)]
        arrived(wr_z)
        place = wr.at[here.me, :, here.core, head]
        wr_g = [links.send(place, place, peer) for peer in here.across]
        wg_a = spread_out(wg, here.along)
        we_a0 = spread_out(we, here.across, lower)
        we_a1 = spread_out(we, here.along, upper)
    perm[...] = to_inner(rows, images)
    back[...] = to_outer(rows, images)
    own_f.wait()
    for number in range(grp):
        if number:
            from_f[number].wait_recv()
        span = aligned(here.partner(number) * own_in, own_in)
        inner[:, span] = dot(perm[...], land_f[number]).astype(BF16)
    if gather:
        for k in range(1, here.lines):
            wr_l[k - 1].wait_recv()
            place = wr.at[:, here.next_line(here.lines - k), here.core, rest]
            wr_b.append(links.send(place, place, here.sibling))
        arrived(wr_g)
        place = wr.at[:, :, here.core, head]
        wr_b.append(links.send(place, place, here.sibling))
        arrived(wg_a)
        place = wg.at[here.me, :, here.core]
        wg_b = [links.send(place, place, peer) for peer in here.across]
        arrived(we_a0)
        arrived(we_a1)
        we_z = Rounds(
            [
                [
                    links.send(
                        we.at[a, here.line, here.core, lower], we.at[a, here.line, here.core, lower], peer, start=False
                    )
                    for peer in here.along
                ]
                for a in range(grp)
            ]
        )
        we_g = Rounds(
            [
                [
                    links.send(we.at[here.me, b, here.core, upper], we.at[here.me, b, here.core, upper], peer, start=False)
                    for peer in here.across
                ]
                for b in range(here.lines)
            ]
        )
        we_z.go(1)
        we_g.go(1)
        arrived(wr_b)
    for copy in loads:
        copy.wait()
    links.move(inner, big["inner"])

    steps = width // BLK

    @pl.loop(0, steps)
    def _(number):
        span = aligned(number * BLK, BLK)
        z1[:, span] = dot(inner[...], wr[:, :, :, :, span].reshape(channels, BLK))
        block_stats(z1, number * BLK, BLK, m_ref, st1, step)

    links.move(wr, big["wr"])
    arrived(small)
    from_c = Rounds(
        partner_rounds(
            here,
            links,
            rows,
            step,
            lambda k, span: (cotg.at[rows_of(here.partner(k), rows, span)], land_c.at[k, span]),
        )
    )
    wg_c = []

    def groups_on():
        if gather:
            arrived(wg_b)
            place = wg.at[:, :, here.core]
            wg_c.append(links.send(place, place, here.sibling))
            we_g.go(1)
            we_z.go(2)

    def expand_on():
        if gather:
            we_g.go(1)

    n1[...] = norm_rows(over_devices(st1, ex1, merge_stats, (expand_on, groups_on)))
    arrived(wg_c)
    if gather:
        we_g.go()
    from_c.go(1)

    clear_edges(col, images, False)

    @pl.loop(0, steps)
    def _(number):
        span = aligned(number * BLK, BLK)
        block_weights(wg, number, blocks)
        centre, scale = n1[0:1, span], n1[1:2, span]
        gain, bias = norm_all[0:1, span], norm_all[1:2, span]
        for row in range(SIDE):
            at = row * step
            mask = wide(m_ref[at : at + step], BLK)
            normed = (z1[at : at + step, span] - centre) * scale
            value, slope = smooth(normed * gain + bias, mask)
            act = value.astype(BF16)
            x1[at : at + step, span] = normed.astype(BF16)
            act1[at : at + step, span] = act
            slope1[at : at + step, span] = slope.astype(BF16)
            spread_row(col, act, row, images, False)
        z1[:, span] = dot(col[...], blocks[...])
        block_stats(z1, number * BLK, BLK, m_ref, st2, step)

    for name in ("x1", "act1", "slope1", "wg"):
        links.move(held[name], big[name])
    if gather:
        arrived(we_g.copies())
        arrived(we_z.copies(0, 3))
        place = we.at[:, :, here.core, upper]
        we_c = [links.send(place, place, here.sibling)]
        place = we.at[0 : grp - 1, :, here.core, lower]
        we_c.append(links.send(place, place, here.sibling))

    def expand_last():
        if gather:
            we_z.go()
        from_c.go(2)

    n2[...] = norm_rows(over_devices(st2, ex2, merge_stats, (from_c.later(2), expand_last)))
    from_c.go(2)

    @pl.loop(0, steps)
    def _(number):
        span = aligned(number * BLK, BLK)
        for at in range(0, rows, step):
            mask = wide(m_ref[at : at + step], BLK)
            normed = (z1[at : at + step, span] - n2[0:1, span]) * n2[1:2, span]
            value, slope = smooth(normed * norm_all[2:3, span] + norm_all[3:4, span], mask)
            x2[at : at + step, span] = normed.astype(BF16)
            act2[at : at + step, span] = value.astype(BF16)
            slope2[at : at + step, span] = slope.astype(BF16)

    for name in ("x2", "act2", "slope2"):
        links.move(held[name], big[name])
    from_c.go(3)
    if gather:
        arrived(we_z.copies(3))
        place = we.at[grp - 1, :, here.core, lower]
        we_c.append(links.send(place, place, here.sibling))
        arrived(we_c)
    links.move(we, big["we"])

    @pl.loop(0, grp)
    def _(number):
        for part in range(0, own_in, BLK):
            span = pl.ds(pl.multiple_of(number * own_in + part, BLK), BLK)
            ze[:, span] = dot(act2[...], we[number, :, :, :, part : part + BLK].reshape(width, BLK))
        block_stats(ze, number * own_in, own_in, m_ref, st3, step)

    n3[...] = norm_rows(over_devices(st3, ex3, merge_stats, (from_c.later(1), from_c.later(1))))
    from_c.go()
    own_c.wait()
    to_near = Rounds(
        partner_rounds(
            here,
            links,
            rows,
            step,
            lambda k, span: (land_f.at[k, span], block_out.at[rows_of(here.me, rows, span)]),
            near=(0, NEAR_ROUNDS),
            far=(0, 0),
        )
    )
    parts = SIDE
    arrived(from_c.copies(0, parts))

    def output_block(slot):
        number = here.partner(slot)
        cot[...] = dot(perm[...], land_c[slot])
        for part in range(0, own_in, BLK):
            span = pl.ds(pl.multiple_of(number * own_in + part, BLK), BLK)
            local = slice(part, part + BLK)
            bias_grad = jnp.zeros((1, BLK), F32)
            gain_grad = jnp.zeros((1, BLK), F32)
            for at in range(0, rows, step):
                mask = wide(m_ref[at : at + step], BLK)
                normed = (ze[at : at + step, span] - n3[0:1, span]) * n3[1:2, span]
                summed = normed * out_all[0:1, span] + out_all[1:2, span] + inner[at : at + step, span].astype(F32)
                value, slope = smooth(summed, mask)
                grad = cot[at : at + step, local] * slope
                x3[at : at + step, span] = normed.astype(BF16)
                col[at : at + step, local] = value.astype(BF16)
                grads[at : at + step, span] = grad.astype(BF16)
                bias_grad += jnp.sum(grad, axis=0, keepdims=True)
                gain_grad += jnp.sum(grad * normed, axis=0, keepdims=True)
            st4[0:1, span] = bias_grad
            st4[1:2, span] = gain_grad
        land_f[slot] = dot(back[...], col[:, 0:own_in]).astype(BF16)

    pl.loop(0, grp - 1)(output_block)
    to_near.go(1)
    arrived(from_c.copies(parts))
    output_block(grp - 1)
    links.move(land_f.at[0], block_out.at[own_rows])
    links.move(land_f.at[1:], big["far"])
    for name in ("x3", "grads"):
        links.move(held[name], big[name])
    sums3[...] = over_devices(st4, ex4, add_rows, (to_near.later(1), to_near.later()))
    arrived(to_near.copies())
    links.close()


def forward(features, out_cotangent, mask, norm_params, out_params, reduce_w, expand_w, group_w, gather):
    grp = lax.axis_size("grp")
    rows = features.shape[0] // grp
    own_in = features.shape[1]
    channels = own_in * grp
    width = norm_params.shape[1] * grp
    lines, cores = (lax.axis_size("batch") // 2, 2) if gather else (1, 1)
    r_shape = (grp, lines, cores, own_in // (lines * cores), width)
    e_shape = (grp, lines, cores, width // (lines * cores), own_in)
    g_shape = (width // BLK, BLK // GW // 2, 2, 3 * GW, 128)
    across = (rows, width)
    shapes = {
        "inner": (rows, channels),
        "x1": across,
        "act1": across,
        "slope1": across,
        "x2": across,
        "act2": across,
        "slope2": across,
        "x3": (rows, channels),
        "grads": (rows, channels),
        "far": (grp - 1, rows, own_in),
        "wr": r_shape,
        "we": e_shape,
        "wg": g_shape,
    }
    small = [(3, width), (3, width), (3, channels), (4, width), (2, channels), (2, channels)]
    vmem = pl.BlockSpec(memory_space=pltpu.VMEM)
    hbm = pl.BlockSpec(memory_space=pl.ANY)
    if gather:
        weights = (reduce_w, expand_w, group_w)
    else:
        weights = (reduce_w.reshape(r_shape), expand_w.reshape(e_shape), group_w.reshape(g_shape))
    results = pl.pallas_call(
        functools.partial(forward_kernel, images=rows // HW, gather=gather),
        out_shape=[jax.ShapeDtypeStruct(shapes[name], BF16) for name in FWD_OUTS]
        + [jax.ShapeDtypeStruct(features.shape, BF16)]
        + [jax.ShapeDtypeStruct(shape, F32) for shape in small],
        in_specs=[hbm, hbm, vmem, vmem, vmem] + [hbm] * 3,
        out_specs=[hbm] * (len(FWD_OUTS) + 1) + [vmem] * len(small),
        scratch_shapes=[pltpu.VMEM(shapes[name], BF16) for name in FWD_OUTS[:-1]]
        + [
            pltpu.VMEM((grp, rows, own_in), BF16),
            pltpu.VMEM((grp, rows, own_in), BF16),
            pltpu.VMEM((rows, own_in), F32),
            pltpu.VMEM((rows, rows), BF16),
            pltpu.VMEM((rows, rows), BF16),
            pltpu.VMEM(across, F32),
            pltpu.VMEM((rows, channels), F32),
            pltpu.VMEM((rows, 9 * BLK), BF16),
            pltpu.VMEM((9 * BLK, BLK), BF16),
            pltpu.VMEM((3, width), F32),
            pltpu.VMEM((3, width), F32),
            pltpu.VMEM((3, channels), F32),
            pltpu.VMEM((2, channels), F32),
            pltpu.SemaphoreType.DMA((112,)),
            pltpu.SemaphoreType.DMA((112,)),
            pltpu.SemaphoreType.DMA((24,)),
        ]
        + sums_scratch(3, width)
        + sums_scratch(3, width)
        + sums_scratch(3, channels)
        + sums_scratch(2, channels)
        + ([pltpu.VMEM(reduce_w.shape, F32), pltpu.VMEM(expand_w.shape, F32)] if gather else []),
        compiler_params=params(collective_id=1, has_side_effects=True),
    )(features, out_cotangent, mask, norm_params, out_params, *weights)
    return dict(zip(FWD_OUTS, results)), results[len(FWD_OUTS)], results[len(FWD_OUTS) + 1 :]


def packed_groups(weight):
    groups = weight.shape[1] // GW
    taps = jnp.pad(weight.reshape(9, GW, groups, GW), ((0, 3), (0, 0), (0, 0), (0, 0)))
    return taps.reshape(3, 4, GW, groups, GW).transpose(3, 0, 2, 1, 4).reshape(groups, 3 * GW, 4 * GW)


BWD_INS = ("grads", "x3", "we", "act2", "slope2", "x2", "act1", "slope1", "x1", "wg", "wr")


def backward_kernel(*refs, images, owners):
    _, far_in, inner_in = refs[:3]
    given = dict(zip(BWD_INS, refs[3:14]))
    m_ref, n1, n2, n3, norm_all, out_all, sums3 = refs[14:21]
    refs = refs[21:]
    state, refs = (refs[:15], refs[15:]) if owners else ((), refs)
    block_out, input_grad, reduce_out, expand_out, group_out, sums1, sums2 = refs[:7]
    raws, refs = ((reduce_out, group_out, expand_out, *refs[7:9]), refs[9:]) if owners else ((), refs[7:])
    scalars, refs = (refs[0], refs[1:]) if owners else (None, refs)
    (grads, x3, we, act2, slope2, x2, act1, slope1, x1, wg, wr) = refs[:11]
    held = dict(zip(BWD_INS, (grads, x3, we, act2, slope2, x2, act1, slope1, x1, wg, wr)))
    (ge, dp, col, blocks, turned, grad_in, back, st1, st2, raw_e, raw_r, raw_g, send, recv, moves) = refs[11:26]
    ex1, ex2 = refs[26:33], refs[33:40]
    here = Place()
    me, grp, core, line, lines = here.me, here.grp, here.core, here.line, here.lines
    rows, width = dp.shape
    channels = grads.shape[1]
    own_in = channels // grp
    step = SIDE * images
    steps = width // BLK
    links = Links(send, recv, moves)
    if owners:
        e_slots, r_slots = refs[40:45], refs[45:50]
        (g1, g2, g3, g4, gs1, gs2, gs3) = refs[50:57]
        trust_scratch = refs[57:72]
        state_in, state = state, refs[72:]

    greet(everyone())
    loads = {name: links.move(given[name], held[name], keep=False) for name in BWD_INS[:4]}
    own_rows = aligned(me * rows, rows)
    back[...] = to_outer(rows, images)
    greeted(everyone())
    to_out = Rounds(
        partner_rounds(
            here,
            links,
            rows,
            step,
            lambda k, span: (far_in.at[k - 1, span], block_out.at[rows_of(me, rows, span)]),
            near=(NEAR_ROUNDS, None),
        )
    )
    to_out.go(7)

    def core_swap(raw, slots):
        return [
            links.send(raw.at[a, :, 1 - core], slots[0].at[a], here.sibling, start=False) for a in range(grp)
        ]

    def swap_now(copies, number):
        for a, copy in enumerate(copies):

            @pl.when(number == a)
            def _():
                copy.start()

    def add_core(raw, slots):
        @pl.loop(0, grp * lines)
        def _(at):
            a, b = at // lines, lax.rem(at, lines)
            slots[0][a, b] = (raw[a, b, core].astype(F32) + slots[0][a, b].astype(F32)).astype(BF16)

    def cuts(slots):
        cut, rest = slots[1].shape[2], slots[2].shape[2]
        return cut, pl.ds(0, cut), pl.ds(cut, rest)

    def spread_sums(slots):
        one, grp_slots, line_slots = slots[:3]
        _, lower, upper = cuts(slots)
        over = [
            links.send(one.at[here.partner(k), :, lower], grp_slots.at[k - 1], here.across[k - 1])
            for k in range(1, grp)
        ]
        along = [
            links.send(one.at[:, here.next_line(k), upper], line_slots.at[k - 1], here.along[k - 1])
            for k in range(1, lines)
        ]
        return over, along

    def add_over(slots):
        one, grp_slots = slots[:2]
        cut = cuts(slots)[0]

        @pl.loop(0, lines)
        def _(b):
            piece = one[me, b, 0:cut].astype(F32)
            for k in range(grp - 1):
                piece += grp_slots[k, b].astype(F32)
            grp_slots[0, b] = piece.astype(BF16)

        return [
            links.send(grp_slots.at[0, here.next_line(k)], slots[3].at[k - 1], here.along[k - 1])
            for k in range(1, lines)
        ]

    def add_along(slots):
        one, line_slots = slots[0], slots[2]
        cut = cuts(slots)[0]

        @pl.loop(0, grp)
        def _(a):
            piece = one[a, line, cut:].astype(F32)
            for k in range(lines - 1):
                piece += line_slots[k, a].astype(F32)
            line_slots[0, a] = piece.astype(BF16)

        return [
            links.send(line_slots.at[0, here.partner(k)], slots[4].at[k - 1], here.across[k - 1])
            for k in range(1, grp)
        ]

    def add_last(slots, out):
        cut = cuts(slots)[0]
        piece = slots[1][0, line].astype(F32)
        for k in range(lines - 1):
            piece += slots[3][k].astype(F32)
        out[0:cut] = piece
        piece = slots[2][0, me].astype(F32)
        for k in range(grp - 1):
            piece += slots[4][k].astype(F32)
        out[cut:] = piece

    for name in BWD_INS[:4]:
        loads[name].wait()
    loads.update({name: links.move(given[name], held[name], keep=False) for name in BWD_INS[4:]})
    if owners:
        state_loads = [links.move(source, target, keep=False) for source, target in zip(state_in, state)]
        e_core = core_swap(raw_e, e_slots)

    @pl.loop(0, grp)
    def _(number):
        for part in range(0, own_in, BLK):
            span = pl.ds(pl.multiple_of(number * own_in + part, BLK), BLK)
            inverse = 1.0 / n3[2:3, span]
            factor = out_all[0:1, span] * n3[1:2, span]
            for at in range(0, rows, step):
                mask = wide(m_ref[at : at + step], BLK)
                normed = x3[at : at + step, span].astype(F32)
                shift = (sums3[0:1, span] + normed * sums3[1:2, span]) * inverse
                value = mask * factor * (grads[at : at + step, span].astype(F32) - shift)
                ge[at : at + step, part : part + BLK] = value.astype(BF16)
        per = we.shape[3]
        taken = BLK // per if per < BLK else 1
        for left in range(0, width, BLK):
            if per < BLK:
                slots = [divmod(left // per + k, we.shape[2]) for k in range(taken)]
                weights = jnp.concatenate([we[number, b, c] for b, c in slots], axis=0)
            else:
                weights = we[number, 0, 0, left : left + BLK]
            part_sum = dot_right(ge[...], weights)
            block = dot_left(act2[:, left : left + BLK], ge[...]).astype(BF16)
            if per < BLK:
                for k, (b, c) in enumerate(slots):
                    raw_e[number, b, c] = block[k * per : (k + 1) * per]
            else:
                raw_e[number, 0, 0, left : left + BLK] = block

            @pl.when(number == 0)
            def _():
                dp[:, left : left + BLK] = part_sum

            @pl.when(number > 0)
            def _():
                dp[:, left : left + BLK] += part_sum

        if owners:
            swap_now(e_core, number)

    if not owners:
        links.move(raw_e, expand_out)
    for name in ("slope2", "x2"):
        loads[name].wait()

    def norm_sums(slope, normed, sums):
        @pl.loop(0, steps)
        def _(number):
            span = aligned(number * BLK, BLK)
            bias_grad = jnp.zeros((1, BLK), F32)
            gain_grad = jnp.zeros((1, BLK), F32)
            for at in range(0, rows, step):
                grad = dp[at : at + step, span] * slope[at : at + step, span].astype(F32)
                dp[at : at + step, span] = grad
                bias_grad += jnp.sum(grad, axis=0, keepdims=True)
                gain_grad += jnp.sum(grad * normed[at : at + step, span].astype(F32), axis=0, keepdims=True)
            sums[0:1, span] = bias_grad
            sums[1:2, span] = gain_grad

    norm_sums(slope2, x2, st2)
    sums2[...] = over_devices(st2, ex2, add_rows, (to_out.later(1), to_out.later(1)))
    if owners:
        arrived(e_core)
        add_core(raw_e, e_slots)
        e_over, e_along = spread_sums(e_slots)

    for name in ("act1", "slope1", "x1", "wg"):
        loads[name].wait()
    own = (
        lax.broadcasted_iota(jnp.int32, (BLK, BLK), 0) // GW == lax.broadcasted_iota(jnp.int32, (BLK, BLK), 1) // GW
    )

    @pl.loop(0, steps)
    def _(number):
        span = aligned(number * BLK, BLK)
        inverse = 1.0 / n2[2:3, span]
        factor = norm_all[2:3, span] * n2[1:2, span]
        clear_edges(col, images, False)
        for row in range(SIDE):
            at = row * step
            mask = wide(m_ref[at : at + step], BLK)
            normed = x2[at : at + step, span].astype(F32)
            shift = (sums2[0:1, span] + normed * sums2[1:2, span]) * inverse
            grad_in[at : at + step] = (mask * factor * (dp[at : at + step, span] - shift)).astype(BF16)
            spread_row(col, act1[at : at + step, span], row, images, False)
        for tap in range(9):
            product = dot_left(col[:, tap * BLK : (tap + 1) * BLK], grad_in[...])
            product = jnp.where(own, product, 0.0)
            piece = product[0:GW]
            for group in range(1, BLK // GW):
                piece += product[group * GW : (group + 1) * GW]
            raw_g[tap * GW : (tap + 1) * GW, span] = piece.astype(BF16)
        clear_edges(col, images, True)
        for row in range(SIDE):
            at = row * step
            spread_row(col, grad_in[at : at + step], row, images, True)
        block_weights(wg, number, blocks)
        for tap in range(9):
            turned[tap * BLK : (tap + 1) * BLK] = blocks[tap * BLK : (tap + 1) * BLK].astype(F32).T.astype(BF16)
        dp[:, span] = dot(col[...], turned[...])

    norm_sums(slope1, x1, st1)
    inner = col.at[:, 0:channels]
    load_inner = links.move(inner_in, inner, keep=False)
    g_grp = []

    def groups_on():
        if owners:
            g_grp.extend(
                links.send(raw_g.at[:, aligned(here.partner(k) * BLK, BLK)], g1.at[k - 1], here.across[k - 1])
                for k in range(1, grp)
            )

    if not owners:
        links.move(raw_g, group_out)
    sums1[...] = over_devices(st1, ex1, add_rows, (to_out.later(1), groups_on))
    if owners:
        arrived(e_over)
        e_last = add_over(e_slots)
        arrived(e_along)
        e_last += add_along(e_slots)
        r_core = core_swap(raw_r, r_slots)
    to_out.go()

    @pl.loop(0, steps)
    def _(number):
        span = aligned(number * BLK, BLK)
        inverse = 1.0 / n1[2:3, span]
        factor = norm_all[0:1, span] * n1[1:2, span]
        for at in range(0, rows, step):
            mask = wide(m_ref[at : at + step], BLK)
            normed = x1[at : at + step, span].astype(F32)
            shift = (sums1[0:1, span] + normed * sums1[1:2, span]) * inverse
            x1[at : at + step, span] = (mask * factor * (dp[at : at + step, span] - shift)).astype(BF16)

    grad_reduce = x1
    load_inner.wait()
    per_r = raw_r.shape[3]

    @pl.loop(0, grp)
    def _(number):
        for part in range(0, own_in, BLK):
            span = pl.ds(pl.multiple_of(number * own_in + part, BLK), BLK)
            block = dot_left(col[:, span], grad_reduce[...]).astype(BF16)
            if per_r < BLK:
                for k in range(BLK // per_r):
                    b, c = divmod(part // per_r + k, raw_r.shape[2])
                    raw_r[number, b, c] = block[k * per_r : (k + 1) * per_r]
            else:
                raw_r[number, 0, 0, part : part + BLK] = block
        if owners:
            swap_now(r_core, number)

    if owners:
        arrived(r_core)
        add_core(raw_r, r_slots)
        r_over, r_along = spread_sums(r_slots)
        arrived(g_grp)
        total = raw_g[:, aligned(me * BLK, BLK)].astype(F32)
        for k in range(grp - 1):
            total += g1[k].astype(F32)
        gs1[...] = total.astype(BF16)
        high = line // 2
        g_far = links.send(gs1.at[:, aligned((1 - high) * 128, 128)], g2, here.far)
    else:
        links.move(raw_r, reduce_out)
    loads["wr"].wait()

    @pl.loop(0, grp)
    def _(number):
        for part in range(0, own_in, BLK):
            span = pl.ds(pl.multiple_of(number * own_in + part, BLK), BLK)
            per = wr.shape[3]
            if per < BLK:
                slots = [divmod(part // per + k, wr.shape[2]) for k in range(BLK // per)]
                weights = jnp.concatenate([wr[number, b, c] for b, c in slots], axis=0)
            else:
                weights = wr[number, 0, 0, part : part + BLK]
            total = grads[:, span].astype(F32) + dot_right(grad_reduce[...], weights)
            ge[:, part : part + BLK] = total.astype(BF16)
        grads[:, aligned(number * own_in, own_in)] = dot(back[...], ge[...]).astype(BF16)

    to_in = Rounds(
        partner_rounds(
            here,
            links,
            rows,
            step,
            lambda k, span: (
                grads.at[span, aligned(here.partner(k) * own_in, own_in)],
                input_grad.at[rows_of(me, rows, span)],
            ),
        )
    )
    links.move(grads.at[:, aligned(me * own_in, own_in)], input_grad.at[own_rows])
    if owners:
        to_in.go(7)
        g_far.wait_recv()
        gs2[...] = (gs1[:, aligned(high * 128, 128)].astype(F32) + g2[...].astype(F32)).astype(BF16)
        g_near = links.send(gs2, g3, here.near)
        arrived(e_last)
        add_last(e_slots, expand_out)
        g_near.wait_recv()
        gs3[...] = (gs2[...].astype(F32) + g3[...].astype(F32)).astype(BF16)
        g_last = links.send(gs3, g4, here.sibling)
        own_width = width // grp
        span = aligned(me * own_width, own_width)
        raws[3][0:1], raws[3][1:2] = sums1[1:2, span], sums1[0:1, span]
        raws[3][2:3], raws[3][3:4] = sums2[1:2, span], sums2[0:1, span]
        span = aligned(me * own_in, own_in)
        raws[4][0:1], raws[4][1:2] = sums3[1:2, span], sums3[0:1, span]
        g_last.wait_recv()
        turned_sum = (gs3[...].astype(F32) + g4[...].astype(F32)).T
        quarter = lax.rem(here.mine, 4)
        piece = turned_sum[0:GW]
        for k in range(1, 4):
            piece = jnp.where(quarter == k, turned_sum[k * GW : (k + 1) * GW], piece)
        group_out[...] = piece
        arrived(r_over)
        r_last = add_over(r_slots)
        arrived(r_along)
        r_last += add_along(r_slots)
        to_in.go(2)
        arrived(r_last)
        add_last(r_slots, reduce_out)
        for copy in state_loads:
            copy.wait()
        beside = (to_in.later(1), to_in.later(2), to_in.later(1), to_in.later())
        trust(
            raws,
            state[:5],
            state[5:10],
            state[10:],
            scalars,
            trust_scratch[0],
            trust_scratch[1:8],
            trust_scratch[8:],
            beside,
        )
    else:
        to_in.go()
    arrived(to_out.copies())
    arrived(to_in.copies())
    links.close()


def backward(kept, block_out, mask, n1, n2, n3, norm_all, out_all, sums3, state, owners):
    grp = lax.axis_size("grp")
    rows, width = kept["act1"].shape
    channels = kept["x3"].shape[1]
    own_in = channels // grp
    r_shape, e_shape = kept["wr"].shape, kept["we"].shape
    lines = r_shape[1]
    vmem = pl.BlockSpec(memory_space=pltpu.VMEM)
    hbm = pl.BlockSpec(memory_space=pl.ANY)
    if owners:
        parts = [
            jax.ShapeDtypeStruct(r_shape[3:], F32),
            jax.ShapeDtypeStruct(e_shape[3:], F32),
            jax.ShapeDtypeStruct((GW, 9 * GW), F32),
        ]
        last = [
            jax.ShapeDtypeStruct((4, width // grp), F32),
            jax.ShapeDtypeStruct((2, own_in), F32),
            jax.ShapeDtypeStruct((8, 128), F32),
        ]
    else:
        last = []
        parts = [jax.ShapeDtypeStruct(shape, BF16) for shape in (r_shape, e_shape, (9 * GW, width))]
    sums = [jax.ShapeDtypeStruct((2, width), F32)] * 2
    scratch = [pltpu.VMEM(kept[name].shape, BF16) for name in BWD_INS] + [
        pltpu.VMEM((rows, own_in), BF16),
        pltpu.VMEM((rows, width), F32),
        pltpu.VMEM((rows, 9 * BLK), BF16),
        pltpu.VMEM((9 * BLK, BLK), BF16),
        pltpu.VMEM((9 * BLK, BLK), BF16),
        pltpu.VMEM((rows, BLK), BF16),
        pltpu.VMEM((rows, rows), BF16),
        pltpu.VMEM((2, width), F32),
        pltpu.VMEM((2, width), F32),
        pltpu.VMEM(e_shape, BF16),
        pltpu.VMEM(r_shape, BF16),
        pltpu.VMEM((9 * GW, width), BF16),
        pltpu.SemaphoreType.DMA((96,)),
        pltpu.SemaphoreType.DMA((96,)),
        pltpu.SemaphoreType.DMA((40,)),
    ]
    scratch += sums_scratch(2, width) + sums_scratch(2, width)
    if owners:
        for shape in (e_shape, r_shape):
            cut = shape[3] * 5 // 128 * 16 if shape[3] > 64 else shape[3] // 2
            scratch += [
                pltpu.VMEM((grp, lines, *shape[3:]), BF16),
                pltpu.VMEM((grp - 1, lines, cut, shape[4]), BF16),
                pltpu.VMEM((lines - 1, grp, shape[3] - cut, shape[4]), BF16),
                pltpu.VMEM((lines - 1, cut, shape[4]), BF16),
                pltpu.VMEM((grp - 1, shape[3] - cut, shape[4]), BF16),
            ]
        narrow = pltpu.VMEM((9 * GW, 128), BF16)
        scratch += [pltpu.VMEM((grp - 1, 9 * GW, BLK), BF16), narrow, narrow, narrow]
        scratch += [pltpu.VMEM((9 * GW, BLK), BF16), narrow, narrow]
        scratch += [pltpu.VMEM((2, 8, 128), F32)] + sums_scratch(8, 128) + sums_scratch(8, 128)
        scratch += [pltpu.VMEM(value.shape, F32) for value in state]
    whole = jax.ShapeDtypeStruct((grp * rows, own_in), BF16)
    return pl.pallas_call(
        functools.partial(backward_kernel, images=rows // HW, owners=owners),
        out_shape=[whole, whole, *parts, *sums, *last],
        in_specs=[hbm] * 14 + [vmem] * 7 + [hbm] * len(state),
        out_specs=[hbm, hbm] + [vmem if owners else hbm] * 3 + [vmem] * (2 + len(last)),
        scratch_shapes=scratch,
        input_output_aliases={0: 0},
        compiler_params=params(collective_id=2, has_side_effects=True),
    )(
        block_out,
        kept["far"],
        kept["inner"],
        *[kept[name] for name in BWD_INS],
        mask,
        n1,
        n2,
        n3,
        norm_all,
        out_all,
        sums3,
        *state,
    )


DECAYS = (0.01, 0.01, 0.01, 0.0, 0.0)


def whole_sum(value):
    return jnp.sum(jnp.sum(value, axis=0, keepdims=True), axis=1, keepdims=True)


def adam_direction(tensor, clipped, moment_one, moment_two, decay_rate):
    new_first = beta_one * moment_one + (1.0 - beta_one) * clipped
    new_second = beta_two * moment_two + (1.0 - beta_two) * clipped * clipped
    first_hat = new_first / (1.0 - beta_one**step_count)
    second_hat = new_second / (1.0 - beta_two**step_count)
    direction = first_hat / (jnp.sqrt(second_hat) + adam_eps) + decay_rate * tensor
    return (new_first, new_second, direction)


def trust(raws, tensors, firsts, seconds, out_ref, pay, one, two, beside=(None,) * 4):
    share = 1.0 / lax.axis_size("batch")
    shares = (1.0, 1.0, 1.0, share, share)
    square = jnp.zeros((1, 1), F32)
    pay[...] = jnp.zeros_like(pay)
    for number in range(5):
        square += shares[number] * whole_sum(raws[number][...] ** 2)
        weight = shares[number] * whole_sum(tensors[number][...] ** 2)
        pay[0, number + 1 : number + 2] = jnp.broadcast_to(weight, (1, 128))
    pay[0, 0:1] = jnp.broadcast_to(square, (1, 128))
    sums = over_devices(pay.at[0], one, add_rows, beside[:2])
    grad_norm = jnp.sqrt(sums[0:1])
    factor = jnp.minimum(1.0, clip_norm / grad_norm)
    for number in range(5):
        direction = adam_direction(
            tensors[number][...],
            factor[0:1, 0:1] * raws[number][...],
            firsts[number][...],
            seconds[number][...],
            DECAYS[number],
        )[2]
        step = shares[number] * whole_sum(direction * direction)
        pay[1, number + 1 : number + 2] = jnp.broadcast_to(step, (1, 128))
    steps = over_devices(pay.at[1], two, add_rows, beside[2:])
    out_ref[...] = jnp.zeros_like(out_ref)
    out_ref[0:1] = grad_norm
    out_ref[1:2] = factor
    out_ref[2:7] = jnp.sqrt(sums[1:6]) * lax.rsqrt(steps[1:6] + 1e-06)


def trust_kernel(*refs):
    raws, tensors, firsts, seconds = (refs[5 * k : 5 * k + 5] for k in range(4))
    greet(everyone())
    greeted(everyone())
    trust(raws, tensors, firsts, seconds, refs[20], refs[21], refs[22:29], refs[29:])


def update_kernel(*refs):
    scalars, results = refs[0], refs[1:3]
    raws, tensors, firsts, seconds = (refs[5 * k + 3 : 5 * k + 8] for k in range(4))
    norm_out, weight_out, rows_out, *refs = refs[23:]
    targets, outs, rooms, sems = refs[:2], refs[2:-3], refs[-3:-1], refs[-1]
    copies, onward = [], []
    for number, (source, room, target) in enumerate(zip(results, rooms, targets)):
        part = source.shape[0] // 4
        for at in range(4):
            span = pl.ds(at * part, part)
            copies.append(pltpu.make_async_copy(source.at[span], room.at[span], sems.at[0, number, at]))
            onward.append(pltpu.make_async_copy(room.at[span], target.at[span], sems.at[1, number, at]))
            copies[-1].start()
    norm_out[0] = scalars[0, 0]
    at = 0
    for number in range(5):
        trust_ratio = scalars[2 + number, 0]
        if number < 3:
            weight_out[number] = trust_ratio
        else:
            rows_out[number - 3] = trust_ratio
        clipped = scalars[1, 0] * raws[number][...]
        tensor = tensors[number][...]
        new_first, new_second, direction = adam_direction(
            tensor, clipped, firsts[number][...], seconds[number][...], DECAYS[number]
        )
        updated = tensor - learn_rate * trust_ratio * direction
        values = [clipped, new_first, new_second, updated]
        if number < 3:
            values.append(updated.astype(BF16))
        for value in values:
            outs[at][...] = value
            at += 1
        if number < 4:
            for copy, after in list(zip(copies, onward))[2 * number : 2 * number + 2]:
                copy.wait()
                after.start()
    for copy in onward:
        copy.wait()


def trust_alone(raws, state):
    vmem = pl.BlockSpec(memory_space=pltpu.VMEM)
    return pl.pallas_call(
        trust_kernel,
        out_shape=jax.ShapeDtypeStruct((8, 128), F32),
        in_specs=[vmem] * 20,
        out_specs=vmem,
        scratch_shapes=[pltpu.VMEM((2, 8, 128), F32)] + sums_scratch(8, 128) + sums_scratch(8, 128),
        compiler_params=params(collective_id=3, has_side_effects=True),
    )(*raws, *state)


def update(scalars, results, raws, state):
    vmem = pl.BlockSpec(memory_space=pltpu.VMEM)
    smem = pl.BlockSpec(memory_space=pltpu.SMEM)
    hbm = pl.BlockSpec(memory_space=pl.ANY)
    shapes = []
    for number, tensor in enumerate(state[:5]):
        shapes += [jax.ShapeDtypeStruct(tensor.shape, F32)] * 4
        if number < 3:
            shapes.append(jax.ShapeDtypeStruct(tensor.shape, BF16))
    outs = pl.pallas_call(
        update_kernel,
        out_shape=[jax.ShapeDtypeStruct((size,), F32) for size in (1, 3, 2)]
        + [jax.ShapeDtypeStruct(result.shape, result.dtype) for result in results]
        + shapes,
        in_specs=[smem, hbm, hbm] + [vmem] * 20,
        out_specs=[smem] * 3 + [hbm] * 2 + [vmem] * len(shapes),
        scratch_shapes=[pltpu.VMEM(result.shape, result.dtype) for result in results]
        + [pltpu.SemaphoreType.DMA((2, 2, 4))],
        compiler_params=params(),
    )(scalars, *results, *raws, *state)
    return outs[:3], outs[3:5], list(outs[5:])


def local(
    features,
    pixel_mask,
    out_cotangent,
    reduce_master,
    group_master,
    expand_master,
    norm_params,
    out_params,
    reduce_first,
    reduce_second,
    group_first,
    group_second,
    expand_first,
    expand_second,
    norm_first,
    norm_second,
    out_first,
    out_second,
):
    grp, batch = lax.axis_size("grp"), lax.axis_size("batch")
    both = ("grp", "batch")
    me = lax.axis_index("grp")
    rows = features.shape[0] // grp
    images = rows // HW
    own_in = features.shape[1]
    own_width = norm_params.shape[1]
    inside = batch == 8 and own_width == 8 * GW
    validity = lax.dynamic_slice_in_dim(pixel_mask, me * rows, rows, 0).astype(F32)
    mask = jnp.broadcast_to(validity.reshape(images, HW).T.reshape(rows, 1), (rows, 128))
    state = (
        *(reduce_master, group_master.T, expand_master, norm_params, out_params),
        *(reduce_first, group_first.T, expand_first, norm_first, out_first),
        *(reduce_second, group_second.T, expand_second, norm_second, out_second),
    )
    group_w = group_master.astype(BF16)
    if inside:
        reduce_w, expand_w = reduce_master, expand_master
        group_w = packed_groups(group_w)[0]
    else:
        reduce_w = lax.all_gather(reduce_master.astype(BF16), both, axis=0, tiled=True)
        expand_w = lax.all_gather(expand_master.astype(BF16), both, axis=0, tiled=True)
        group_w = packed_groups(lax.all_gather(group_w, both, axis=1, tiled=True))
    kept, block_out, (n1, n2, n3, norm_all, out_all, sums_three) = forward(
        features, out_cotangent, mask, norm_params, out_params, reduce_w, expand_w, group_w, inside
    )
    block_out, input_grad, reduce_part, expand_part, group_part, sums_one, sums_two, *last = backward(
        kept, block_out, mask, n1, n2, n3, norm_all, out_all, sums_three, state if inside else (), inside
    )
    if inside:
        norm_raw, out_raw, scalars = last
        raws = (reduce_part, group_part, expand_part, norm_raw, out_raw)
    else:
        flat = group_part.reshape(9 * GW, grp * batch, -1).transpose(1, 2, 0)
        reduce_part, expand_part, group_part = (
            lax.psum_scatter(value, both, scatter_dimension=0).astype(F32)
            for value in (
                reduce_part.reshape(grp * batch, own_in // batch, -1),
                expand_part.reshape(grp * batch, -1, own_in),
                flat,
            )
        )
        norm_sums = jnp.concatenate([sums_one[1:2], sums_one[0:1], sums_two[1:2], sums_two[0:1]], axis=0)
        norm_raw = lax.dynamic_slice_in_dim(norm_sums, me * own_width, own_width, 1)
        out_sums = jnp.concatenate([sums_three[1:2], sums_three[0:1]], axis=0)
        out_raw = lax.dynamic_slice_in_dim(out_sums, me * own_in, own_in, 1)
        raws = (reduce_part, group_part, expand_part, norm_raw, out_raw)
        scalars = trust_alone(raws, state)
    (grad_norm, weight_trust, norm_trust), results, updates = update(scalars, (block_out, input_grad), raws, state)
    updates[5:10] = [value.T for value in updates[5:10]]
    return (*results, grad_norm.reshape(()), weight_trust, norm_trust, *updates)


def solution(mesh):
    in_specs = (
        P("batch", "grp"),
        P("batch"),
        P("batch", "grp"),
        P(("grp", "batch"), None),
        P(None, ("grp", "batch")),
        P("batch", "grp"),
        P(None, "grp"),
        P(None, "grp"),
        P(("grp", "batch"), None),
        P(("grp", "batch"), None),
        P(None, ("grp", "batch")),
        P(None, ("grp", "batch")),
        P("batch", "grp"),
        P("batch", "grp"),
        P(None, "grp"),
        P(None, "grp"),
        P(None, "grp"),
        P(None, "grp"),
    )
    out_specs = (
        P("batch", "grp"),
        P("batch", "grp"),
        P(),
        P(),
        P(),
        P(("grp", "batch"), None),
        P(("grp", "batch"), None),
        P(("grp", "batch"), None),
        P(("grp", "batch"), None),
        P(("grp", "batch"), None),
        P(None, ("grp", "batch")),
        P(None, ("grp", "batch")),
        P(None, ("grp", "batch")),
        P(None, ("grp", "batch")),
        P(None, ("grp", "batch")),
        P("batch", "grp"),
        P("batch", "grp"),
        P("batch", "grp"),
        P("batch", "grp"),
        P("batch", "grp"),
        P(None, "grp"),
        P(None, "grp"),
        P(None, "grp"),
        P(None, "grp"),
        P(None, "grp"),
        P(None, "grp"),
        P(None, "grp"),
        P(None, "grp"),
    )
    return jax.shard_map(local, mesh=mesh, in_specs=in_specs, out_specs=out_specs, check_vma=False)
```

```python
import functools

import jax
import jax.numpy as jnp
from jax import lax
from jax.experimental import pallas as pl
from jax.experimental.pallas import tpu as pltpu
from jax.sharding import PartitionSpec as P

GW = 32
SIDE = 7
HW = SIDE * SIDE
BLK = 256

eps_norm = 1e-05
beta_one = 0.9
beta_two = 0.999
adam_eps = 1e-08
learn_rate = 0.25
step_count = 10.0
clip_norm = 1.0

MESH = pl.DeviceIdType.MESH
F32 = jnp.float32
BF16 = jnp.bfloat16
VMEM_LIMIT = 62 * 1024 * 1024


def params(**more):
    return pltpu.CompilerParams(vmem_limit_bytes=VMEM_LIMIT, **more)


def dot(a, b):
    return jnp.dot(a, b, preferred_element_type=F32)


def dot_left(a, b):
    return lax.dot_general(a, b, (((0,), (0,)), ((), ())), preferred_element_type=F32)


def dot_right(a, b):
    return lax.dot_general(a, b, (((1,), (1,)), ((), ())), preferred_element_type=F32)


def sigmoid(v):
    return 0.5 + 0.5 * jnp.tanh(0.5 * v)


def to_inner(rows, images):
    to = lax.broadcasted_iota(jnp.int32, (rows, rows), 0)
    source = (to % images) * HW + to // images
    at = lax.broadcasted_iota(jnp.int32, (rows, rows), 1)
    return jnp.where(at == source, 1.0, 0.0).astype(BF16)


def to_outer(rows, images):
    to = lax.broadcasted_iota(jnp.int32, (rows, rows), 0)
    source = (to % HW) * images + to // HW
    at = lax.broadcasted_iota(jnp.int32, (rows, rows), 1)
    return jnp.where(at == source, 1.0, 0.0).astype(BF16)


def wide(mask, columns):
    return jnp.concatenate([mask] * (columns // 128), axis=1)


def peers(axis):
    size = lax.axis_size(axis)
    mine = lax.axis_index(axis)
    return [{axis: lax.rem(mine + other, size)} for other in range(1, size)]


def greet(groups):
    barrier = pltpu.get_barrier_semaphore()
    for peer in groups:
        pl.semaphore_signal(barrier, inc=1, device_id=peer, device_id_type=MESH)


def greeted(groups):
    pl.semaphore_wait(pltpu.get_barrier_semaphore(), len(groups))


def everyone():
    return peers("grp") + peers("batch")


def sums_scratch(rows, columns):
    grp, batch = lax.axis_size("grp"), lax.axis_size("batch")
    return [
        pltpu.VMEM((grp - 1, rows, columns), F32),
        pltpu.VMEM((batch - 1, rows, columns), F32),
        pltpu.VMEM((rows, columns), F32),
        pltpu.SemaphoreType.DMA((grp - 1,)),
        pltpu.SemaphoreType.DMA((grp - 1,)),
        pltpu.SemaphoreType.DMA((batch - 1,)),
        pltpu.SemaphoreType.DMA((batch - 1,)),
    ]


def add_rows(parts):
    return functools.reduce(jnp.add, parts)


def merge_stats(parts):
    count = add_rows([part[2:3] for part in parts])
    total = add_rows([part[0:1] for part in parts])
    centre = total / count
    spread = add_rows([part[1:2] + part[2:3] * (part[0:1] / part[2:3] - centre) ** 2 for part in parts])
    return jnp.concatenate([total, spread, count], axis=0)


def over_devices(source, scratch, merge, beside=(None, None)):
    first, second, mid, *sems = scratch
    copies = []
    levels = (("grp", first, sems[0], sems[1], beside[0]), ("batch", second, sems[2], sems[3], beside[1]))
    for axis, slots, send, recv, meanwhile in levels:
        here = []
        for number, peer in enumerate(peers(axis)):
            copy = pltpu.make_async_remote_copy(
                source, slots.at[number], send.at[number], recv.at[number], device_id=peer, device_id_type=MESH
            )
            copy.start()
            here.append(copy)
        if meanwhile is not None:
            meanwhile()
        for copy in here:
            copy.wait_recv()
        copies += here
        merged = merge([source[...]] + [slots[number] for number in range(len(here))])
        if axis == "grp":
            mid[...] = merged
            source = mid
    for copy in copies:
        copy.wait_send()
    return merged


def norm_rows(merged):
    total, spread, count = merged[0:1], merged[1:2], merged[2:3]
    return jnp.concatenate([total / count, lax.rsqrt(spread / count + eps_norm), count], axis=0)


def clear_edges(col, images, reverse):
    for tap_row in range(3):
        for tap_col in range(3):
            tap = 3 * tap_row + tap_col
            dy, dx = (1 - tap_row, 1 - tap_col) if reverse else (tap_row - 1, tap_col - 1)
            for row in range(SIDE):
                for column in range(SIDE):
                    inside = 0 <= row + dy < SIDE and 0 <= column + dx < SIDE
                    if not inside:
                        at = (row * SIDE + column) * images
                        col[at : at + images, tap * BLK : (tap + 1) * BLK] = jnp.zeros((images, BLK), BF16)


def spread_row(col, value, row, images, reverse):
    for tap_row in range(3):
        for tap_col in range(3):
            tap = 3 * tap_row + tap_col
            dy, dx = (1 - tap_row, 1 - tap_col) if reverse else (tap_row - 1, tap_col - 1)
            to_row = row - dy
            if not 0 <= to_row < SIDE:
                continue
            first = max(0, dx)
            last = min(SIDE, SIDE + dx)
            at = (to_row * SIDE + first - dx) * images
            col[at : at + (last - first) * images, tap * BLK : (tap + 1) * BLK] = value[first * images : last * images]


class Links:
    def __init__(self, send, recv, local):
        self.send_sems, self.recv_sems, self.local_sems = send, recv, local
        self.sent = self.moved = 0
        self.open_sends, self.open_moves = [], []

    def send(self, source, target, peer, start=True):
        at = self.sent
        self.sent += 1
        copy = pltpu.make_async_remote_copy(
            source, target, self.send_sems.at[at], self.recv_sems.at[at], device_id=peer, device_id_type=MESH
        )
        if start:
            copy.start()
        self.open_sends.append(copy)
        return copy

    def move(self, source, target, keep=True):
        copy = pltpu.make_async_copy(source, target, self.local_sems.at[self.moved])
        self.moved += 1
        copy.start()
        if keep:
            self.open_moves.append(copy)
        return copy

    def close(self):
        for copy in self.open_sends:
            copy.wait_send()
        for copy in self.open_moves:
            copy.wait()


class Rounds:
    def __init__(self, rounds):
        self.rounds, self.at = rounds, 0

    def go(self, count=None):
        count = len(self.rounds) if count is None else count
        for copies in self.rounds[self.at : self.at + count]:
            for copy in copies:
                copy.start()
        self.at = min(self.at + count, len(self.rounds))

    def later(self, count=None):
        return lambda: self.go(count)

    def copies(self, first=0, last=None):
        return [copy for copies in self.rounds[first:last] for copy in copies]


def arrived(copies):
    for copy in copies:
        copy.wait_recv()


class Place:
    def __init__(self):
        grp, batch = lax.axis_size("grp"), lax.axis_size("batch")
        self.grp, self.lines = grp, batch // 2
        self.me, self.mine = lax.axis_index("grp"), lax.axis_index("batch")
        self.core, self.line = lax.rem(self.mine, 2), self.mine // 2
        self.sibling = {"batch": self.mine + 1 - 2 * self.core}
        self.across = [{"grp": self.partner(k)} for k in range(1, grp)]
        self.along = [{"batch": self.next_line(k) * 2 + self.core} for k in range(1, self.lines)]
        self.far = {"batch": (self.line + 2 - 4 * (self.line // 2)) * 2 + self.core}
        self.near = {"batch": (self.line + 1 - 2 * lax.rem(self.line, 2)) * 2 + self.core}

    def partner(self, k):
        low = lax.rem(lax.rem(self.me, 2) + (k % 2 if isinstance(k, int) else lax.rem(k, 2)), 2)
        return lax.rem(self.me // 2 + k // 2, 2) * 2 + low

    def next_line(self, k):
        return lax.rem(self.line + k, self.lines)


def partner_rounds(here, links, rows, part, pair, near=(0, None), far=(0, None)):
    rounds = []
    for ks, (first, last) in ((tuple(range(1, here.grp - 1)), near), ((here.grp - 1,), far)):
        for at in range(0, rows, part)[first:last]:
            copies = [links.send(*pair(k, pl.ds(at, part)), here.across[k - 1], start=False) for k in ks]
            rounds.append(copies)
    return rounds


def rows_of(index, rows, span):
    return pl.ds(pl.multiple_of(index * rows, rows) + span.start, span.size)


def aligned(at, size):
    return pl.ds(pl.multiple_of(at, size), size)


def block_weights(wg_ref, number, blocks):
    lanes = lax.broadcasted_iota(jnp.int32, (GW, 128), 1) // GW
    zero = jnp.zeros((GW, 128), BF16)
    for group in range(BLK // GW):
        for tap in range(9):
            piece = wg_ref[number, group // 2, group % 2, (tap // 4) * GW : (tap // 4 + 1) * GW].astype(F32)
            turn = ((group - tap) % 4) * GW
            if turn:
                piece = pltpu.roll(piece, turn, 1)
            piece = jnp.where(lanes == group % 4, piece, 0.0).astype(BF16)
            row = tap * BLK + group * GW
            left = (group // 4) * 128
            blocks[row : row + GW, left : left + 128] = piece
            blocks[row : row + GW, 128 - left : 256 - left] = zero


def pack_groups(transposed):
    lanes = lax.broadcasted_iota(jnp.int32, (GW, 128), 1) - lax.broadcasted_iota(jnp.int32, (GW, 128), 0)
    at = [dot_left(transposed, jnp.where(lanes == tap * GW, 1.0, 0.0).astype(BF16)) for tap in range(4)]
    rows = []
    for first in range(0, 9, 4):
        taps = range(first, min(first + 4, 9))
        rows.append(add_rows([at[tap % 4][tap * GW : (tap + 1) * GW] for tap in taps]))
    return jnp.concatenate(rows, axis=0).astype(BF16)


def spread_mask(valid, images):
    rows = images * HW
    image = lax.broadcasted_iota(jnp.int32, (rows, images), 0) % images
    chosen = jnp.where(image == lax.broadcasted_iota(jnp.int32, (rows, images), 1), 1.0, 0.0)
    frames = dot(chosen.astype(BF16), valid.astype(BF16))
    pixel = lax.broadcasted_iota(jnp.int32, (rows, HW), 0) // images
    own = jnp.where(pixel == lax.broadcasted_iota(jnp.int32, (rows, HW), 1), frames, 0.0)
    return jnp.broadcast_to(jnp.sum(own, axis=1, keepdims=True), (rows, 128))


def block_stats(z_ref, left, columns, m_ref, st_ref, step):
    rows = z_ref.shape[0]
    for part in range(0, columns, BLK):
        span = pl.ds(pl.multiple_of(left + part, BLK), BLK)
        total = jnp.zeros((1, BLK), F32)
        count = jnp.zeros((1, 128), F32)
        for at in range(0, rows, step):
            mask = m_ref[at : at + step]
            total += jnp.sum(z_ref[at : at + step, span] * wide(mask, BLK), axis=0, keepdims=True)
            count += jnp.sum(mask, axis=0, keepdims=True)
        count = wide(count, BLK)
        centre = total / count
        spread = jnp.zeros((1, BLK), F32)
        for at in range(0, rows, step):
            off = (z_ref[at : at + step, span] - centre) * wide(m_ref[at : at + step], BLK)
            spread += jnp.sum(off * off, axis=0, keepdims=True)
        st_ref[0:1, span] = total
        st_ref[1:2, span] = spread
        st_ref[2:3, span] = count


def smooth(pre, mask):
    sigma = sigmoid(pre)
    masked = sigma * mask
    return pre * masked, masked * (1.0 + pre * (1.0 - sigma))


NEAR_ROUNDS = 3
FWD_OUTS = ("inner", "x1", "act1", "slope1", "x2", "act2", "slope2", "x3", "grads", "wr", "we", "wg", "far")


def forward_kernel(*refs, images, gather):
    (feat, cotg, valid_ref, np_ref, op_ref, wr_in, we_in, wg_in) = refs[:8]
    big = dict(zip(FWD_OUTS, refs[8:21]))
    block_out, m_ref, n1, n2, n3, norm_all, out_all, sums3 = refs[21:29]
    refs = refs[:28] + refs[29:]
    (inner, x1, act1, slope1, x2, act2, slope2, x3, grads, wr, we, wg) = refs[28:40]
    (land_f, land_c, cot, perm, back, z1, ze, col, blocks, st1, st2, st3, st4, send, recv, moves) = refs[40:56]
    ex1, ex2, ex3, ex4 = (refs[56 + 7 * k : 63 + 7 * k] for k in range(4))
    held = dict(zip(FWD_OUTS, (inner, x1, act1, slope1, x2, act2, slope2, x3, grads, wr, we, wg)))
    here = Place()
    grp = here.grp
    rows, own_in = land_f.shape[1:]
    width, channels = z1.shape[1], ze.shape[1]
    own_width = np_ref.shape[1]
    step = SIDE * images
    links = Links(send, recv, moves)

    greet(everyone())
    own_rows = aligned(here.me * rows, rows)
    own_f = links.move(feat.at[own_rows], land_f.at[0], keep=False)
    if gather:
        shard_r, shard_e = refs[84:86]
        shards = [
            links.move(wr_in, shard_r, keep=False),
            links.move(we_in, shard_e, keep=False),
        ]
        wg[here.me, here.line, here.core] = pack_groups(wg_in[...].astype(BF16))
        for copy in shards:
            copy.wait()
        wr[here.me, here.line, here.core] = shard_r[...].astype(BF16)
        we[here.me, here.line, here.core] = shard_e[...].astype(BF16)
        loads = []
    else:
        loads = [links.move(wr_in, wr, keep=False), links.move(we_in, we, keep=False), links.move(wg_in, wg, keep=False)]
    norm_all[:, aligned(here.me * own_width, own_width)] = np_ref[...]
    out_all[:, aligned(here.me * own_in, own_in)] = op_ref[...]
    greeted(everyone())

    def spread_out(buffer, targets, rows=slice(None)):
        place = buffer.at[here.me, here.line, here.core, rows]
        return [links.send(place, place, peer) for peer in targets]

    if gather:
        quarter = wr.shape[3] // 4
        head, rest = pl.ds(0, quarter), pl.ds(quarter, 3 * quarter)
        half = we.shape[3] // 2
        lower, upper = pl.ds(0, half), pl.ds(half, half)
        wr_a = spread_out(wr, here.across, rest)
        wr_z = spread_out(wr, here.along, head)
    small = []
    for k in range(1, grp):
        peer = here.across[k - 1]
        span = aligned(here.me * own_width, own_width)
        small.append(links.send(np_ref, norm_all.at[:, span], peer))
        span = aligned(here.me * own_in, own_in)
        small.append(links.send(op_ref, out_all.at[:, span], peer))
    from_f = {}
    for k in range(1, grp):
        source = feat.at[aligned(here.partner(k) * rows, rows)]
        from_f[k] = links.send(source, land_f.at[k], here.across[k - 1])
    own_c = links.move(cotg.at[own_rows], land_c.at[0], keep=False)
    if gather:
        arrived(wr_a)
        place = wr.at[:, here.line, here.core, rest]
        wr_l = [links.send(place, place, peer) for peer in here.along]
        wr_b = [links.send(place, place, here.sibling)]
        arrived(wr_z)
        place = wr.at[here.me, :, here.core, head]
        wr_g = [links.send(place, place, peer) for peer in here.across]
        wg_a = spread_out(wg, here.along)
        we_a0 = spread_out(we, here.across, lower)
        we_a1 = spread_out(we, here.along, upper)
    perm[...] = to_inner(rows, images)
    back[...] = to_outer(rows, images)
    m_ref[...] = spread_mask(valid_ref[...], images)
    own_f.wait()
    for number in range(grp):
        if number:
            from_f[number].wait_recv()
        span = aligned(here.partner(number) * own_in, own_in)
        inner[:, span] = dot(perm[...], land_f[number]).astype(BF16)
    if gather:
        for k in range(1, here.lines):
            wr_l[k - 1].wait_recv()
            place = wr.at[:, here.next_line(here.lines - k), here.core, rest]
            wr_b.append(links.send(place, place, here.sibling))
        arrived(wr_g)
        place = wr.at[:, :, here.core, head]
        wr_b.append(links.send(place, place, here.sibling))
        arrived(wg_a)
        place = wg.at[here.me, :, here.core]
        wg_b = [links.send(place, place, peer) for peer in here.across]
        arrived(we_a0)
        arrived(we_a1)
        we_z = Rounds(
            [
                [
                    links.send(
                        we.at[a, here.line, here.core, lower], we.at[a, here.line, here.core, lower], peer, start=False
                    )
                    for peer in here.along
                ]
                for a in range(grp)
            ]
        )
        we_g = Rounds(
            [
                [
                    links.send(we.at[here.me, b, here.core, upper], we.at[here.me, b, here.core, upper], peer, start=False)
                    for peer in here.across
                ]
                for b in range(here.lines)
            ]
        )
        we_z.go(1)
        we_g.go(1)
        arrived(wr_b)
    for copy in loads:
        copy.wait()
    links.move(inner, big["inner"])

    steps = width // BLK

    @pl.loop(0, steps)
    def _(number):
        span = aligned(number * BLK, BLK)
        z1[:, span] = dot(inner[...], wr[:, :, :, :, span].reshape(channels, BLK))
        block_stats(z1, number * BLK, BLK, m_ref, st1, step)

    links.move(wr, big["wr"])
    arrived(small)
    from_c = Rounds(
        partner_rounds(
            here,
            links,
            rows,
            step,
            lambda k, span: (cotg.at[rows_of(here.partner(k), rows, span)], land_c.at[k, span]),
        )
    )
    wg_c = []

    def groups_on():
        if gather:
            arrived(wg_b)
            place = wg.at[:, :, here.core]
            wg_c.append(links.send(place, place, here.sibling))
            we_g.go(1)
            we_z.go(2)

    def expand_on():
        if gather:
            we_g.go(1)

    n1[...] = norm_rows(over_devices(st1, ex1, merge_stats, (expand_on, groups_on)))
    arrived(wg_c)
    if gather:
        we_g.go()
    from_c.go(1)

    clear_edges(col, images, False)

    @pl.loop(0, steps)
    def _(number):
        span = aligned(number * BLK, BLK)
        block_weights(wg, number, blocks)
        centre, scale = n1[0:1, span], n1[1:2, span]
        gain, bias = norm_all[0:1, span], norm_all[1:2, span]
        for row in range(SIDE):
            at = row * step
            mask = wide(m_ref[at : at + step], BLK)
            normed = (z1[at : at + step, span] - centre) * scale
            value, slope = smooth(normed * gain + bias, mask)
            act = value.astype(BF16)
            x1[at : at + step, span] = normed.astype(BF16)
            act1[at : at + step, span] = act
            slope1[at : at + step, span] = slope.astype(BF16)
            spread_row(col, act, row, images, False)
        z1[:, span] = dot(col[...], blocks[...])
        block_stats(z1, number * BLK, BLK, m_ref, st2, step)

    for name in ("x1", "act1", "slope1", "wg"):
        links.move(held[name], big[name])
    if gather:
        arrived(we_g.copies())
        arrived(we_z.copies(0, 3))
        place = we.at[:, :, here.core, upper]
        we_c = [links.send(place, place, here.sibling)]
        place = we.at[0 : grp - 1, :, here.core, lower]
        we_c.append(links.send(place, place, here.sibling))

    def expand_last():
        if gather:
            we_z.go()
        from_c.go(2)

    n2[...] = norm_rows(over_devices(st2, ex2, merge_stats, (from_c.later(2), expand_last)))
    from_c.go(2)

    @pl.loop(0, steps)
    def _(number):
        span = aligned(number * BLK, BLK)
        for at in range(0, rows, step):
            mask = wide(m_ref[at : at + step], BLK)
            normed = (z1[at : at + step, span] - n2[0:1, span]) * n2[1:2, span]
            value, slope = smooth(normed * norm_all[2:3, span] + norm_all[3:4, span], mask)
            x2[at : at + step, span] = normed.astype(BF16)
            act2[at : at + step, span] = value.astype(BF16)
            slope2[at : at + step, span] = slope.astype(BF16)

    for name in ("x2", "act2", "slope2"):
        links.move(held[name], big[name])
    from_c.go(3)
    if gather:
        arrived(we_z.copies(3))
        place = we.at[grp - 1, :, here.core, lower]
        we_c.append(links.send(place, place, here.sibling))
        arrived(we_c)
    links.move(we, big["we"])

    @pl.loop(0, grp)
    def _(number):
        for part in range(0, own_in, BLK):
            span = pl.ds(pl.multiple_of(number * own_in + part, BLK), BLK)
            ze[:, span] = dot(act2[...], we[number, :, :, :, part : part + BLK].reshape(width, BLK))
        block_stats(ze, number * own_in, own_in, m_ref, st3, step)

    n3[...] = norm_rows(over_devices(st3, ex3, merge_stats, (from_c.later(1), from_c.later(1))))
    from_c.go()
    own_c.wait()
    to_near = Rounds(
        partner_rounds(
            here,
            links,
            rows,
            step,
            lambda k, span: (land_f.at[k, span], block_out.at[rows_of(here.me, rows, span)]),
            near=(0, NEAR_ROUNDS),
            far=(0, 0),
        )
    )
    parts = SIDE
    arrived(from_c.copies(0, parts))

    def output_block(slot):
        number = here.partner(slot)
        cot[...] = dot(perm[...], land_c[slot])
        for part in range(0, own_in, BLK):
            span = pl.ds(pl.multiple_of(number * own_in + part, BLK), BLK)
            local = slice(part, part + BLK)
            bias_grad = jnp.zeros((1, BLK), F32)
            gain_grad = jnp.zeros((1, BLK), F32)
            for at in range(0, rows, step):
                mask = wide(m_ref[at : at + step], BLK)
                normed = (ze[at : at + step, span] - n3[0:1, span]) * n3[1:2, span]
                summed = normed * out_all[0:1, span] + out_all[1:2, span] + inner[at : at + step, span].astype(F32)
                value, slope = smooth(summed, mask)
                grad = cot[at : at + step, local] * slope
                x3[at : at + step, span] = normed.astype(BF16)
                col[at : at + step, local] = value.astype(BF16)
                grads[at : at + step, span] = grad.astype(BF16)
                bias_grad += jnp.sum(grad, axis=0, keepdims=True)
                gain_grad += jnp.sum(grad * normed, axis=0, keepdims=True)
            st4[0:1, span] = bias_grad
            st4[1:2, span] = gain_grad
        land_f[slot] = dot(back[...], col[:, 0:own_in]).astype(BF16)

    pl.loop(0, grp - 1)(output_block)
    to_near.go(1)
    arrived(from_c.copies(parts))
    output_block(grp - 1)
    links.move(land_f.at[0], block_out.at[own_rows])
    links.move(land_f.at[1:], big["far"])
    for name in ("x3", "grads"):
        links.move(held[name], big[name])
    sums3[...] = over_devices(st4, ex4, add_rows, (to_near.later(1), to_near.later()))
    arrived(to_near.copies())
    links.close()


def forward(features, out_cotangent, valid, norm_params, out_params, reduce_w, expand_w, group_w, gather):
    grp = lax.axis_size("grp")
    rows = features.shape[0] // grp
    own_in = features.shape[1]
    channels = own_in * grp
    width = norm_params.shape[1] * grp
    lines, cores = (lax.axis_size("batch") // 2, 2) if gather else (1, 1)
    r_shape = (grp, lines, cores, own_in // (lines * cores), width)
    e_shape = (grp, lines, cores, width // (lines * cores), own_in)
    g_shape = (width // BLK, BLK // GW // 2, 2, 3 * GW, 128)
    across = (rows, width)
    shapes = {
        "inner": (rows, channels),
        "x1": across,
        "act1": across,
        "slope1": across,
        "x2": across,
        "act2": across,
        "slope2": across,
        "x3": (rows, channels),
        "grads": (rows, channels),
        "far": (grp - 1, rows, own_in),
        "wr": r_shape,
        "we": e_shape,
        "wg": g_shape,
    }
    small = [(rows, 128), (3, width), (3, width), (3, channels), (4, width), (2, channels), (2, channels)]
    vmem = pl.BlockSpec(memory_space=pltpu.VMEM)
    hbm = pl.BlockSpec(memory_space=pl.ANY)
    if gather:
        weights = (reduce_w, expand_w, group_w)
    else:
        weights = (reduce_w.reshape(r_shape), expand_w.reshape(e_shape), group_w.reshape(g_shape))
    results = pl.pallas_call(
        functools.partial(forward_kernel, images=rows // HW, gather=gather),
        out_shape=[jax.ShapeDtypeStruct(shapes[name], BF16) for name in FWD_OUTS]
        + [jax.ShapeDtypeStruct(features.shape, BF16)]
        + [jax.ShapeDtypeStruct(shape, F32) for shape in small],
        in_specs=[hbm, hbm, vmem, vmem, vmem, hbm, hbm, vmem if gather else hbm],
        out_specs=[hbm] * (len(FWD_OUTS) + 1) + [vmem] * len(small),
        scratch_shapes=[pltpu.VMEM(shapes[name], BF16) for name in FWD_OUTS[:-1]]
        + [
            pltpu.VMEM((grp, rows, own_in), BF16),
            pltpu.VMEM((grp, rows, own_in), BF16),
            pltpu.VMEM((rows, own_in), F32),
            pltpu.VMEM((rows, rows), BF16),
            pltpu.VMEM((rows, rows), BF16),
            pltpu.VMEM(across, F32),
            pltpu.VMEM((rows, channels), F32),
            pltpu.VMEM((rows, 9 * BLK), BF16),
            pltpu.VMEM((9 * BLK, BLK), BF16),
            pltpu.VMEM((3, width), F32),
            pltpu.VMEM((3, width), F32),
            pltpu.VMEM((3, channels), F32),
            pltpu.VMEM((2, channels), F32),
            pltpu.SemaphoreType.DMA((112,)),
            pltpu.SemaphoreType.DMA((112,)),
            pltpu.SemaphoreType.DMA((24,)),
        ]
        + sums_scratch(3, width)
        + sums_scratch(3, width)
        + sums_scratch(3, channels)
        + sums_scratch(2, channels)
        + ([pltpu.VMEM(reduce_w.shape, F32), pltpu.VMEM(expand_w.shape, F32)] if gather else []),
        compiler_params=params(collective_id=1, has_side_effects=True),
    )(features, out_cotangent, valid, norm_params, out_params, *weights)
    return dict(zip(FWD_OUTS, results)), results[len(FWD_OUTS)], results[len(FWD_OUTS) + 1 :]


def packed_groups(weight):
    groups = weight.shape[1] // GW
    taps = jnp.pad(weight.reshape(9, GW, groups, GW), ((0, 3), (0, 0), (0, 0), (0, 0)))
    return taps.reshape(3, 4, GW, groups, GW).transpose(3, 0, 2, 1, 4).reshape(groups, 3 * GW, 4 * GW)


BWD_INS = ("grads", "x3", "we", "act2", "slope2", "x2", "act1", "slope1", "x1", "wg", "wr")


def backward_kernel(*refs, images, owners):
    _, far_in, inner_in = refs[:3]
    given = dict(zip(BWD_INS, refs[3:14]))
    m_ref, n1, n2, n3, norm_all, out_all, sums3 = refs[14:21]
    refs = refs[21:]
    state, refs = (refs[:15], refs[15:]) if owners else ((), refs)
    block_out, input_grad, reduce_out, expand_out, group_out, sums1, sums2 = refs[:7]
    raws, refs = ((reduce_out, group_out, expand_out, *refs[7:9]), refs[9:]) if owners else ((), refs[7:])
    scalars, refs = (refs[0], refs[1:]) if owners else (None, refs)
    (grads, x3, we, act2, slope2, x2, act1, slope1, x1, wg, wr) = refs[:11]
    held = dict(zip(BWD_INS, (grads, x3, we, act2, slope2, x2, act1, slope1, x1, wg, wr)))
    (ge, dp, col, blocks, turned, grad_in, back, st1, st2, raw_e, raw_r, raw_g, send, recv, moves) = refs[11:26]
    ex1, ex2 = refs[26:33], refs[33:40]
    here = Place()
    me, grp, core, line, lines = here.me, here.grp, here.core, here.line, here.lines
    rows, width = dp.shape
    channels = grads.shape[1]
    own_in = channels // grp
    step = SIDE * images
    steps = width // BLK
    links = Links(send, recv, moves)
    if owners:
        e_slots, r_slots = refs[40:45], refs[45:50]
        (g1, g2, g3, g4, gs1, gs2, gs3) = refs[50:57]
        trust_scratch = refs[57:72]
        state_in, state = state, refs[72:]

    greet(everyone())
    loads = {name: links.move(given[name], held[name], keep=False) for name in BWD_INS[:4]}
    own_rows = aligned(me * rows, rows)
    back[...] = to_outer(rows, images)
    greeted(everyone())
    to_out = Rounds(
        partner_rounds(
            here,
            links,
            rows,
            step,
            lambda k, span: (far_in.at[k - 1, span], block_out.at[rows_of(me, rows, span)]),
            near=(NEAR_ROUNDS, None),
        )
    )
    to_out.go(7)

    def core_swap(raw, slots):
        return [
            links.send(raw.at[a, :, 1 - core], slots[0].at[a], here.sibling, start=False) for a in range(grp)
        ]

    def swap_now(copies, number):
        for a, copy in enumerate(copies):

            @pl.when(number == a)
            def _():
                copy.start()

    def add_core(raw, slots):
        @pl.loop(0, grp * lines)
        def _(at):
            a, b = at // lines, lax.rem(at, lines)
            slots[0][a, b] = (raw[a, b, core].astype(F32) + slots[0][a, b].astype(F32)).astype(BF16)

    def cuts(slots):
        cut, rest = slots[1].shape[2], slots[2].shape[2]
        return cut, pl.ds(0, cut), pl.ds(cut, rest)

    def spread_sums(slots):
        one, grp_slots, line_slots = slots[:3]
        _, lower, upper = cuts(slots)
        over = [
            links.send(one.at[here.partner(k), :, lower], grp_slots.at[k - 1], here.across[k - 1])
            for k in range(1, grp)
        ]
        along = [
            links.send(one.at[:, here.next_line(k), upper], line_slots.at[k - 1], here.along[k - 1])
            for k in range(1, lines)
        ]
        return over, along

    def add_over(slots):
        one, grp_slots = slots[:2]
        cut = cuts(slots)[0]

        @pl.loop(0, lines)
        def _(b):
            piece = one[me, b, 0:cut].astype(F32)
            for k in range(grp - 1):
                piece += grp_slots[k, b].astype(F32)
            grp_slots[0, b] = piece.astype(BF16)

        return [
            links.send(grp_slots.at[0, here.next_line(k)], slots[3].at[k - 1], here.along[k - 1])
            for k in range(1, lines)
        ]

    def add_along(slots):
        one, line_slots = slots[0], slots[2]
        cut = cuts(slots)[0]

        @pl.loop(0, grp)
        def _(a):
            piece = one[a, line, cut:].astype(F32)
            for k in range(lines - 1):
                piece += line_slots[k, a].astype(F32)
            line_slots[0, a] = piece.astype(BF16)

        return [
            links.send(line_slots.at[0, here.partner(k)], slots[4].at[k - 1], here.across[k - 1])
            for k in range(1, grp)
        ]

    def add_last(slots, out):
        cut = cuts(slots)[0]
        piece = slots[1][0, line].astype(F32)
        for k in range(lines - 1):
            piece += slots[3][k].astype(F32)
        out[0:cut] = piece
        piece = slots[2][0, me].astype(F32)
        for k in range(grp - 1):
            piece += slots[4][k].astype(F32)
        out[cut:] = piece

    for name in BWD_INS[:4]:
        loads[name].wait()
    loads.update({name: links.move(given[name], held[name], keep=False) for name in BWD_INS[4:]})
    if owners:
        state_loads = [links.move(source, target, keep=False) for source, target in zip(state_in, state)]
        e_core = core_swap(raw_e, e_slots)

    @pl.loop(0, grp)
    def _(number):
        for part in range(0, own_in, BLK):
            span = pl.ds(pl.multiple_of(number * own_in + part, BLK), BLK)
            inverse = 1.0 / n3[2:3, span]
            factor = out_all[0:1, span] * n3[1:2, span]
            for at in range(0, rows, step):
                mask = wide(m_ref[at : at + step], BLK)
                normed = x3[at : at + step, span].astype(F32)
                shift = (sums3[0:1, span] + normed * sums3[1:2, span]) * inverse
                value = mask * factor * (grads[at : at + step, span].astype(F32) - shift)
                ge[at : at + step, part : part + BLK] = value.astype(BF16)
        per = we.shape[3]
        taken = BLK // per if per < BLK else 1
        for left in range(0, width, BLK):
            if per < BLK:
                slots = [divmod(left // per + k, we.shape[2]) for k in range(taken)]
                weights = jnp.concatenate([we[number, b, c] for b, c in slots], axis=0)
            else:
                weights = we[number, 0, 0, left : left + BLK]
            part_sum = dot_right(ge[...], weights)
            block = dot_left(act2[:, left : left + BLK], ge[...]).astype(BF16)
            if per < BLK:
                for k, (b, c) in enumerate(slots):
                    raw_e[number, b, c] = block[k * per : (k + 1) * per]
            else:
                raw_e[number, 0, 0, left : left + BLK] = block

            @pl.when(number == 0)
            def _():
                dp[:, left : left + BLK] = part_sum

            @pl.when(number > 0)
            def _():
                dp[:, left : left + BLK] += part_sum

        if owners:
            swap_now(e_core, number)

    if not owners:
        links.move(raw_e, expand_out)
    for name in ("slope2", "x2"):
        loads[name].wait()

    def norm_sums(slope, normed, sums):
        @pl.loop(0, steps)
        def _(number):
            span = aligned(number * BLK, BLK)
            bias_grad = jnp.zeros((1, BLK), F32)
            gain_grad = jnp.zeros((1, BLK), F32)
            for at in range(0, rows, step):
                grad = dp[at : at + step, span] * slope[at : at + step, span].astype(F32)
                dp[at : at + step, span] = grad
                bias_grad += jnp.sum(grad, axis=0, keepdims=True)
                gain_grad += jnp.sum(grad * normed[at : at + step, span].astype(F32), axis=0, keepdims=True)
            sums[0:1, span] = bias_grad
            sums[1:2, span] = gain_grad

    norm_sums(slope2, x2, st2)
    sums2[...] = over_devices(st2, ex2, add_rows, (to_out.later(1), to_out.later(1)))
    if owners:
        arrived(e_core)
        add_core(raw_e, e_slots)
        e_over, e_along = spread_sums(e_slots)

    for name in ("act1", "slope1", "x1", "wg"):
        loads[name].wait()
    own = (
        lax.broadcasted_iota(jnp.int32, (BLK, BLK), 0) // GW == lax.broadcasted_iota(jnp.int32, (BLK, BLK), 1) // GW
    )

    @pl.loop(0, steps)
    def _(number):
        span = aligned(number * BLK, BLK)
        inverse = 1.0 / n2[2:3, span]
        factor = norm_all[2:3, span] * n2[1:2, span]
        clear_edges(col, images, False)
        for row in range(SIDE):
            at = row * step
            mask = wide(m_ref[at : at + step], BLK)
            normed = x2[at : at + step, span].astype(F32)
            shift = (sums2[0:1, span] + normed * sums2[1:2, span]) * inverse
            grad_in[at : at + step] = (mask * factor * (dp[at : at + step, span] - shift)).astype(BF16)
            spread_row(col, act1[at : at + step, span], row, images, False)
        for tap in range(9):
            product = dot_left(col[:, tap * BLK : (tap + 1) * BLK], grad_in[...])
            product = jnp.where(own, product, 0.0)
            piece = product[0:GW]
            for group in range(1, BLK // GW):
                piece += product[group * GW : (group + 1) * GW]
            raw_g[tap * GW : (tap + 1) * GW, span] = piece.astype(BF16)
        clear_edges(col, images, True)
        for row in range(SIDE):
            at = row * step
            spread_row(col, grad_in[at : at + step], row, images, True)
        block_weights(wg, number, blocks)
        for tap in range(9):
            turned[tap * BLK : (tap + 1) * BLK] = blocks[tap * BLK : (tap + 1) * BLK].astype(F32).T.astype(BF16)
        dp[:, span] = dot(col[...], turned[...])

    norm_sums(slope1, x1, st1)
    inner = col.at[:, 0:channels]
    load_inner = links.move(inner_in, inner, keep=False)
    g_grp = []

    def groups_on():
        if owners:
            g_grp.extend(
                links.send(raw_g.at[:, aligned(here.partner(k) * BLK, BLK)], g1.at[k - 1], here.across[k - 1])
                for k in range(1, grp)
            )

    if not owners:
        links.move(raw_g, group_out)
    sums1[...] = over_devices(st1, ex1, add_rows, (to_out.later(1), groups_on))
    if owners:
        arrived(e_over)
        e_last = add_over(e_slots)
        arrived(e_along)
        e_last += add_along(e_slots)
        r_core = core_swap(raw_r, r_slots)
    to_out.go()

    @pl.loop(0, steps)
    def _(number):
        span = aligned(number * BLK, BLK)
        inverse = 1.0 / n1[2:3, span]
        factor = norm_all[0:1, span] * n1[1:2, span]
        for at in range(0, rows, step):
            mask = wide(m_ref[at : at + step], BLK)
            normed = x1[at : at + step, span].astype(F32)
            shift = (sums1[0:1, span] + normed * sums1[1:2, span]) * inverse
            x1[at : at + step, span] = (mask * factor * (dp[at : at + step, span] - shift)).astype(BF16)

    grad_reduce = x1
    load_inner.wait()
    per_r = raw_r.shape[3]

    @pl.loop(0, grp)
    def _(number):
        for part in range(0, own_in, BLK):
            span = pl.ds(pl.multiple_of(number * own_in + part, BLK), BLK)
            block = dot_left(col[:, span], grad_reduce[...]).astype(BF16)
            if per_r < BLK:
                for k in range(BLK // per_r):
                    b, c = divmod(part // per_r + k, raw_r.shape[2])
                    raw_r[number, b, c] = block[k * per_r : (k + 1) * per_r]
            else:
                raw_r[number, 0, 0, part : part + BLK] = block
        if owners:
            swap_now(r_core, number)

    if owners:
        arrived(r_core)
        add_core(raw_r, r_slots)
        r_over, r_along = spread_sums(r_slots)
        arrived(g_grp)
        total = raw_g[:, aligned(me * BLK, BLK)].astype(F32)
        for k in range(grp - 1):
            total += g1[k].astype(F32)
        gs1[...] = total.astype(BF16)
        high = line // 2
        g_far = links.send(gs1.at[:, aligned((1 - high) * 128, 128)], g2, here.far)
    else:
        links.move(raw_r, reduce_out)
    loads["wr"].wait()

    @pl.loop(0, grp)
    def _(number):
        for part in range(0, own_in, BLK):
            span = pl.ds(pl.multiple_of(number * own_in + part, BLK), BLK)
            per = wr.shape[3]
            if per < BLK:
                slots = [divmod(part // per + k, wr.shape[2]) for k in range(BLK // per)]
                weights = jnp.concatenate([wr[number, b, c] for b, c in slots], axis=0)
            else:
                weights = wr[number, 0, 0, part : part + BLK]
            total = grads[:, span].astype(F32) + dot_right(grad_reduce[...], weights)
            ge[:, part : part + BLK] = total.astype(BF16)
        grads[:, aligned(number * own_in, own_in)] = dot(back[...], ge[...]).astype(BF16)

    to_in = Rounds(
        partner_rounds(
            here,
            links,
            rows,
            step,
            lambda k, span: (
                grads.at[span, aligned(here.partner(k) * own_in, own_in)],
                input_grad.at[rows_of(me, rows, span)],
            ),
        )
    )
    links.move(grads.at[:, aligned(me * own_in, own_in)], input_grad.at[own_rows])
    if owners:
        to_in.go(7)
        g_far.wait_recv()
        gs2[...] = (gs1[:, aligned(high * 128, 128)].astype(F32) + g2[...].astype(F32)).astype(BF16)
        g_near = links.send(gs2, g3, here.near)
        arrived(e_last)
        add_last(e_slots, expand_out)
        g_near.wait_recv()
        gs3[...] = (gs2[...].astype(F32) + g3[...].astype(F32)).astype(BF16)
        g_last = links.send(gs3, g4, here.sibling)
        own_width = width // grp
        span = aligned(me * own_width, own_width)
        raws[3][0:1], raws[3][1:2] = sums1[1:2, span], sums1[0:1, span]
        raws[3][2:3], raws[3][3:4] = sums2[1:2, span], sums2[0:1, span]
        span = aligned(me * own_in, own_in)
        raws[4][0:1], raws[4][1:2] = sums3[1:2, span], sums3[0:1, span]
        g_last.wait_recv()
        turned_sum = (gs3[...].astype(F32) + g4[...].astype(F32)).T
        quarter = lax.rem(here.mine, 4)
        piece = turned_sum[0:GW]
        for k in range(1, 4):
            piece = jnp.where(quarter == k, turned_sum[k * GW : (k + 1) * GW], piece)
        group_out[...] = piece
        arrived(r_over)
        r_last = add_over(r_slots)
        arrived(r_along)
        r_last += add_along(r_slots)
        to_in.go(2)
        arrived(r_last)
        add_last(r_slots, reduce_out)
        for copy in state_loads:
            copy.wait()
        beside = (to_in.later(1), to_in.later(2), to_in.later(1), to_in.later())
        trust(
            raws,
            state[:5],
            state[5:10],
            state[10:],
            scalars,
            trust_scratch[0],
            trust_scratch[1:8],
            trust_scratch[8:],
            beside,
        )
    else:
        to_in.go()
    arrived(to_out.copies())
    arrived(to_in.copies())
    links.close()


def backward(kept, block_out, mask, n1, n2, n3, norm_all, out_all, sums3, state, owners):
    grp = lax.axis_size("grp")
    rows, width = kept["act1"].shape
    channels = kept["x3"].shape[1]
    own_in = channels // grp
    r_shape, e_shape = kept["wr"].shape, kept["we"].shape
    lines = r_shape[1]
    vmem = pl.BlockSpec(memory_space=pltpu.VMEM)
    hbm = pl.BlockSpec(memory_space=pl.ANY)
    if owners:
        parts = [
            jax.ShapeDtypeStruct(r_shape[3:], F32),
            jax.ShapeDtypeStruct(e_shape[3:], F32),
            jax.ShapeDtypeStruct((GW, 9 * GW), F32),
        ]
        last = [
            jax.ShapeDtypeStruct((4, width // grp), F32),
            jax.ShapeDtypeStruct((2, own_in), F32),
            jax.ShapeDtypeStruct((8, 128), F32),
        ]
    else:
        last = []
        parts = [jax.ShapeDtypeStruct(shape, BF16) for shape in (r_shape, e_shape, (9 * GW, width))]
    sums = [jax.ShapeDtypeStruct((2, width), F32)] * 2
    scratch = [pltpu.VMEM(kept[name].shape, BF16) for name in BWD_INS] + [
        pltpu.VMEM((rows, own_in), BF16),
        pltpu.VMEM((rows, width), F32),
        pltpu.VMEM((rows, 9 * BLK), BF16),
        pltpu.VMEM((9 * BLK, BLK), BF16),
        pltpu.VMEM((9 * BLK, BLK), BF16),
        pltpu.VMEM((rows, BLK), BF16),
        pltpu.VMEM((rows, rows), BF16),
        pltpu.VMEM((2, width), F32),
        pltpu.VMEM((2, width), F32),
        pltpu.VMEM(e_shape, BF16),
        pltpu.VMEM(r_shape, BF16),
        pltpu.VMEM((9 * GW, width), BF16),
        pltpu.SemaphoreType.DMA((96,)),
        pltpu.SemaphoreType.DMA((96,)),
        pltpu.SemaphoreType.DMA((40,)),
    ]
    scratch += sums_scratch(2, width) + sums_scratch(2, width)
    if owners:
        for shape in (e_shape, r_shape):
            cut = shape[3] * 5 // 128 * 16 if shape[3] > 64 else shape[3] // 2
            scratch += [
                pltpu.VMEM((grp, lines, *shape[3:]), BF16),
                pltpu.VMEM((grp - 1, lines, cut, shape[4]), BF16),
                pltpu.VMEM((lines - 1, grp, shape[3] - cut, shape[4]), BF16),
                pltpu.VMEM((lines - 1, cut, shape[4]), BF16),
                pltpu.VMEM((grp - 1, shape[3] - cut, shape[4]), BF16),
            ]
        narrow = pltpu.VMEM((9 * GW, 128), BF16)
        scratch += [pltpu.VMEM((grp - 1, 9 * GW, BLK), BF16), narrow, narrow, narrow]
        scratch += [pltpu.VMEM((9 * GW, BLK), BF16), narrow, narrow]
        scratch += [pltpu.VMEM((2, 8, 128), F32)] + sums_scratch(8, 128) + sums_scratch(8, 128)
        scratch += [pltpu.VMEM(value.shape, F32) for value in state]
    whole = jax.ShapeDtypeStruct((grp * rows, own_in), BF16)
    return pl.pallas_call(
        functools.partial(backward_kernel, images=rows // HW, owners=owners),
        out_shape=[whole, whole, *parts, *sums, *last],
        in_specs=[hbm] * 14 + [vmem] * 7 + [hbm] * len(state),
        out_specs=[hbm, hbm] + [vmem if owners else hbm] * 3 + [vmem] * (2 + len(last)),
        scratch_shapes=scratch,
        input_output_aliases={0: 0},
        compiler_params=params(collective_id=2, has_side_effects=True),
    )(
        block_out,
        kept["far"],
        kept["inner"],
        *[kept[name] for name in BWD_INS],
        mask,
        n1,
        n2,
        n3,
        norm_all,
        out_all,
        sums3,
        *state,
    )


DECAYS = (0.01, 0.01, 0.01, 0.0, 0.0)


def whole_sum(value):
    return jnp.sum(jnp.sum(value, axis=0, keepdims=True), axis=1, keepdims=True)


def adam_direction(tensor, clipped, moment_one, moment_two, decay_rate):
    new_first = beta_one * moment_one + (1.0 - beta_one) * clipped
    new_second = beta_two * moment_two + (1.0 - beta_two) * clipped * clipped
    first_hat = new_first / (1.0 - beta_one**step_count)
    second_hat = new_second / (1.0 - beta_two**step_count)
    direction = first_hat / (jnp.sqrt(second_hat) + adam_eps) + decay_rate * tensor
    return (new_first, new_second, direction)


def trust(raws, tensors, firsts, seconds, out_ref, pay, one, two, beside=(None,) * 4):
    share = 1.0 / lax.axis_size("batch")
    shares = (1.0, 1.0, 1.0, share, share)
    square = jnp.zeros((1, 1), F32)
    pay[...] = jnp.zeros_like(pay)
    for number in range(5):
        square += shares[number] * whole_sum(raws[number][...] ** 2)
        weight = shares[number] * whole_sum(tensors[number][...] ** 2)
        pay[0, number + 1 : number + 2] = jnp.broadcast_to(weight, (1, 128))
    pay[0, 0:1] = jnp.broadcast_to(square, (1, 128))
    sums = over_devices(pay.at[0], one, add_rows, beside[:2])
    grad_norm = jnp.sqrt(sums[0:1])
    factor = jnp.minimum(1.0, clip_norm / grad_norm)
    for number in range(5):
        direction = adam_direction(
            tensors[number][...],
            factor[0:1, 0:1] * raws[number][...],
            firsts[number][...],
            seconds[number][...],
            DECAYS[number],
        )[2]
        step = shares[number] * whole_sum(direction * direction)
        pay[1, number + 1 : number + 2] = jnp.broadcast_to(step, (1, 128))
    steps = over_devices(pay.at[1], two, add_rows, beside[2:])
    out_ref[...] = jnp.zeros_like(out_ref)
    out_ref[0:1] = grad_norm
    out_ref[1:2] = factor
    out_ref[2:7] = jnp.sqrt(sums[1:6]) * lax.rsqrt(steps[1:6] + 1e-06)


def trust_kernel(*refs):
    raws, tensors, firsts, seconds = (refs[5 * k : 5 * k + 5] for k in range(4))
    greet(everyone())
    greeted(everyone())
    trust(raws, tensors, firsts, seconds, refs[20], refs[21], refs[22:29], refs[29:])


def update_kernel(*refs):
    scalars, results = refs[0], refs[1:3]
    raws, tensors, firsts, seconds = (refs[5 * k + 3 : 5 * k + 8] for k in range(4))
    norm_out, weight_out, rows_out, *refs = refs[23:]
    targets, refs = refs[:2], refs[2:]
    rooms, sems, out_sems = refs[-4:-2], refs[-2], refs[-1]
    outs, held = refs[: len(refs) // 2 - 2], refs[len(refs) // 2 - 2 : -4]
    copies, onward = [], []
    for number, (source, room, target) in enumerate(zip(results, rooms, targets)):
        part = source.shape[0] // 4
        for at in range(4):
            span = pl.ds(at * part, part)
            copies.append(pltpu.make_async_copy(source.at[span], room.at[span], sems.at[0, number, at]))
            onward.append(pltpu.make_async_copy(room.at[span], target.at[span], sems.at[1, number, at]))
            copies[-1].start()
    norm_out[0] = scalars[0, 0]
    at = 0
    for number in range(5):
        trust_ratio = scalars[2 + number, 0]
        if number < 3:
            weight_out[number] = trust_ratio
        else:
            rows_out[number - 3] = trust_ratio
        clipped = scalars[1, 0] * raws[number][...]
        tensor = tensors[number][...]
        new_first, new_second, direction = adam_direction(
            tensor, clipped, firsts[number][...], seconds[number][...], DECAYS[number]
        )
        updated = tensor - learn_rate * trust_ratio * direction
        values = [clipped, new_first, new_second, updated]
        if number < 3:
            values.append(updated.astype(BF16))
        for value in values:
            held[at][...] = value
            onward.append(pltpu.make_async_copy(held[at], outs[at], out_sems.at[at]))
            onward[-1].start()
            at += 1
        if number < 4:
            for copy, after in list(zip(copies, onward))[2 * number : 2 * number + 2]:
                copy.wait()
                after.start()
    for copy in onward:
        copy.wait()


def trust_alone(raws, state):
    vmem = pl.BlockSpec(memory_space=pltpu.VMEM)
    return pl.pallas_call(
        trust_kernel,
        out_shape=jax.ShapeDtypeStruct((8, 128), F32),
        in_specs=[vmem] * 20,
        out_specs=vmem,
        scratch_shapes=[pltpu.VMEM((2, 8, 128), F32)] + sums_scratch(8, 128) + sums_scratch(8, 128),
        compiler_params=params(collective_id=3, has_side_effects=True),
    )(*raws, *state)


def update(scalars, results, raws, state):
    vmem = pl.BlockSpec(memory_space=pltpu.VMEM)
    smem = pl.BlockSpec(memory_space=pltpu.SMEM)
    hbm = pl.BlockSpec(memory_space=pl.ANY)
    shapes = []
    for number, tensor in enumerate(state[:5]):
        shapes += [jax.ShapeDtypeStruct(tensor.shape, F32)] * 4
        if number < 3:
            shapes.append(jax.ShapeDtypeStruct(tensor.shape, BF16))
    outs = pl.pallas_call(
        update_kernel,
        out_shape=[jax.ShapeDtypeStruct((size,), F32) for size in (1, 3, 2)]
        + [jax.ShapeDtypeStruct(result.shape, result.dtype) for result in results]
        + shapes,
        in_specs=[smem, hbm, hbm] + [vmem] * 20,
        out_specs=[smem] * 3 + [hbm] * (2 + len(shapes)),
        scratch_shapes=[pltpu.VMEM(shape.shape, shape.dtype) for shape in shapes]
        + [pltpu.VMEM(result.shape, result.dtype) for result in results]
        + [pltpu.SemaphoreType.DMA((2, 2, 4)), pltpu.SemaphoreType.DMA((len(shapes),))],
        compiler_params=params(),
    )(scalars, *results, *raws, *state)
    return outs[:3], outs[3:5], list(outs[5:])


def local(
    features,
    pixel_mask,
    out_cotangent,
    reduce_master,
    group_master,
    expand_master,
    norm_params,
    out_params,
    reduce_first,
    reduce_second,
    group_first,
    group_second,
    expand_first,
    expand_second,
    norm_first,
    norm_second,
    out_first,
    out_second,
):
    grp, batch = lax.axis_size("grp"), lax.axis_size("batch")
    both = ("grp", "batch")
    me = lax.axis_index("grp")
    rows = features.shape[0] // grp
    images = rows // HW
    own_in = features.shape[1]
    own_width = norm_params.shape[1]
    inside = batch == 8 and own_width == 8 * GW
    valid = lax.dynamic_slice_in_dim(pixel_mask, me * rows, rows, 0).astype(F32).reshape(images, HW)
    state = (
        *(reduce_master, group_master.T, expand_master, norm_params, out_params),
        *(reduce_first, group_first.T, expand_first, norm_first, out_first),
        *(reduce_second, group_second.T, expand_second, norm_second, out_second),
    )
    if inside:
        reduce_w, expand_w, group_w = reduce_master, expand_master, group_master.T
    else:
        reduce_w = lax.all_gather(reduce_master.astype(BF16), both, axis=0, tiled=True)
        expand_w = lax.all_gather(expand_master.astype(BF16), both, axis=0, tiled=True)
        group_w = packed_groups(lax.all_gather(group_master.astype(BF16), both, axis=1, tiled=True))
    kept, block_out, (mask, n1, n2, n3, norm_all, out_all, sums_three) = forward(
        features, out_cotangent, valid, norm_params, out_params, reduce_w, expand_w, group_w, inside
    )
    block_out, input_grad, reduce_part, expand_part, group_part, sums_one, sums_two, *last = backward(
        kept, block_out, mask, n1, n2, n3, norm_all, out_all, sums_three, state if inside else (), inside
    )
    if inside:
        norm_raw, out_raw, scalars = last
        raws = (reduce_part, group_part, expand_part, norm_raw, out_raw)
    else:
        flat = group_part.reshape(9 * GW, grp * batch, -1).transpose(1, 2, 0)
        reduce_part, expand_part, group_part = (
            lax.psum_scatter(value, both, scatter_dimension=0).astype(F32)
            for value in (
                reduce_part.reshape(grp * batch, own_in // batch, -1),
                expand_part.reshape(grp * batch, -1, own_in),
                flat,
            )
        )
        norm_sums = jnp.concatenate([sums_one[1:2], sums_one[0:1], sums_two[1:2], sums_two[0:1]], axis=0)
        norm_raw = lax.dynamic_slice_in_dim(norm_sums, me * own_width, own_width, 1)
        out_sums = jnp.concatenate([sums_three[1:2], sums_three[0:1]], axis=0)
        out_raw = lax.dynamic_slice_in_dim(out_sums, me * own_in, own_in, 1)
        raws = (reduce_part, group_part, expand_part, norm_raw, out_raw)
        scalars = trust_alone(raws, state)
    (grad_norm, weight_trust, norm_trust), results, updates = update(scalars, (block_out, input_grad), raws, state)
    updates[5:10] = [value.T for value in updates[5:10]]
    return (*results, grad_norm.reshape(()), weight_trust, norm_trust, *updates)


def solution(mesh):
    in_specs = (
        P("batch", "grp"),
        P("batch"),
        P("batch", "grp"),
        P(("grp", "batch"), None),
        P(None, ("grp", "batch")),
        P("batch", "grp"),
        P(None, "grp"),
        P(None, "grp"),
        P(("grp", "batch"), None),
        P(("grp", "batch"), None),
        P(None, ("grp", "batch")),
        P(None, ("grp", "batch")),
        P("batch", "grp"),
        P("batch", "grp"),
        P(None, "grp"),
        P(None, "grp"),
        P(None, "grp"),
        P(None, "grp"),
    )
    out_specs = (
        P("batch", "grp"),
        P("batch", "grp"),
        P(),
        P(),
        P(),
        P(("grp", "batch"), None),
        P(("grp", "batch"), None),
        P(("grp", "batch"), None),
        P(("grp", "batch"), None),
        P(("grp", "batch"), None),
        P(None, ("grp", "batch")),
        P(None, ("grp", "batch")),
        P(None, ("grp", "batch")),
        P(None, ("grp", "batch")),
        P(None, ("grp", "batch")),
        P("batch", "grp"),
        P("batch", "grp"),
        P("batch", "grp"),
        P("batch", "grp"),
        P("batch", "grp"),
        P(None, "grp"),
        P(None, "grp"),
        P(None, "grp"),
        P(None, "grp"),
        P(None, "grp"),
        P(None, "grp"),
        P(None, "grp"),
        P(None, "grp"),
    )
    return jax.shard_map(local, mesh=mesh, in_specs=in_specs, out_specs=out_specs, check_vma=False)
```

```python
import functools

import jax
import jax.numpy as jnp
from jax import lax
from jax.experimental import pallas as pl
from jax.experimental.pallas import tpu as pltpu
from jax.sharding import PartitionSpec as P

GW = 32
SIDE = 7
HW = SIDE * SIDE
BLK = 256

eps_norm = 1e-05
beta_one = 0.9
beta_two = 0.999
adam_eps = 1e-08
learn_rate = 0.25
step_count = 10.0
clip_norm = 1.0

MESH = pl.DeviceIdType.MESH
F32 = jnp.float32
BF16 = jnp.bfloat16
VMEM_LIMIT = 62 * 1024 * 1024


def params(**more):
    return pltpu.CompilerParams(vmem_limit_bytes=VMEM_LIMIT, **more)


def dot(a, b):
    return jnp.dot(a, b, preferred_element_type=F32)


def dot_left(a, b):
    return lax.dot_general(a, b, (((0,), (0,)), ((), ())), preferred_element_type=F32)


def dot_right(a, b):
    return lax.dot_general(a, b, (((1,), (1,)), ((), ())), preferred_element_type=F32)


def sigmoid(v):
    return 0.5 + 0.5 * jnp.tanh(0.5 * v)


def to_inner(rows, images):
    to = lax.broadcasted_iota(jnp.int32, (rows, rows), 0)
    source = (to % images) * HW + to // images
    at = lax.broadcasted_iota(jnp.int32, (rows, rows), 1)
    return jnp.where(at == source, 1.0, 0.0).astype(BF16)


def to_outer(rows, images):
    to = lax.broadcasted_iota(jnp.int32, (rows, rows), 0)
    source = (to % HW) * images + to // HW
    at = lax.broadcasted_iota(jnp.int32, (rows, rows), 1)
    return jnp.where(at == source, 1.0, 0.0).astype(BF16)


def wide(mask, columns):
    return jnp.concatenate([mask] * (columns // 128), axis=1)


def peers(axis):
    size = lax.axis_size(axis)
    mine = lax.axis_index(axis)
    return [{axis: lax.rem(mine + other, size)} for other in range(1, size)]


def greet(groups):
    barrier = pltpu.get_barrier_semaphore()
    for peer in groups:
        pl.semaphore_signal(barrier, inc=1, device_id=peer, device_id_type=MESH)


def greeted(groups):
    pl.semaphore_wait(pltpu.get_barrier_semaphore(), len(groups))


def everyone():
    return peers("grp") + peers("batch")


def sums_scratch(rows, columns):
    grp, batch = lax.axis_size("grp"), lax.axis_size("batch")
    return [
        pltpu.VMEM((grp - 1, rows, columns), F32),
        pltpu.VMEM((batch - 1, rows, columns), F32),
        pltpu.VMEM((rows, columns), F32),
        pltpu.SemaphoreType.DMA((grp - 1,)),
        pltpu.SemaphoreType.DMA((grp - 1,)),
        pltpu.SemaphoreType.DMA((batch - 1,)),
        pltpu.SemaphoreType.DMA((batch - 1,)),
    ]


def add_rows(parts):
    return functools.reduce(jnp.add, parts)


def merge_stats(parts):
    count = add_rows([part[2:3] for part in parts])
    total = add_rows([part[0:1] for part in parts])
    centre = total / count
    spread = add_rows([part[1:2] + part[2:3] * (part[0:1] / part[2:3] - centre) ** 2 for part in parts])
    return jnp.concatenate([total, spread, count], axis=0)


def over_devices(source, scratch, merge, beside=(None, None)):
    first, second, mid, *sems = scratch
    copies = []
    levels = (("grp", first, sems[0], sems[1], beside[0]), ("batch", second, sems[2], sems[3], beside[1]))
    for axis, slots, send, recv, meanwhile in levels:
        here = []
        for number, peer in enumerate(peers(axis)):
            copy = pltpu.make_async_remote_copy(
                source, slots.at[number], send.at[number], recv.at[number], device_id=peer, device_id_type=MESH
            )
            copy.start()
            here.append(copy)
        if meanwhile is not None:
            meanwhile()
        for copy in here:
            copy.wait_recv()
        copies += here
        merged = merge([source[...]] + [slots[number] for number in range(len(here))])
        if axis == "grp":
            mid[...] = merged
            source = mid
    for copy in copies:
        copy.wait_send()
    return merged


def norm_rows(merged):
    total, spread, count = merged[0:1], merged[1:2], merged[2:3]
    return jnp.concatenate([total / count, lax.rsqrt(spread / count + eps_norm), count], axis=0)


def clear_edges(col, images, reverse):
    for tap_row in range(3):
        for tap_col in range(3):
            tap = 3 * tap_row + tap_col
            dy, dx = (1 - tap_row, 1 - tap_col) if reverse else (tap_row - 1, tap_col - 1)
            for row in range(SIDE):
                for column in range(SIDE):
                    inside = 0 <= row + dy < SIDE and 0 <= column + dx < SIDE
                    if not inside:
                        at = (row * SIDE + column) * images
                        col[at : at + images, tap * BLK : (tap + 1) * BLK] = jnp.zeros((images, BLK), BF16)


def spread_row(col, value, row, images, reverse):
    for tap_row in range(3):
        for tap_col in range(3):
            tap = 3 * tap_row + tap_col
            dy, dx = (1 - tap_row, 1 - tap_col) if reverse else (tap_row - 1, tap_col - 1)
            to_row = row - dy
            if not 0 <= to_row < SIDE:
                continue
            first = max(0, dx)
            last = min(SIDE, SIDE + dx)
            at = (to_row * SIDE + first - dx) * images
            col[at : at + (last - first) * images, tap * BLK : (tap + 1) * BLK] = value[first * images : last * images]


class Links:
    def __init__(self, send, recv, local):
        self.send_sems, self.recv_sems, self.local_sems = send, recv, local
        self.sent = self.moved = 0
        self.open_sends, self.open_moves, self.at_times = [], [], []

    def send(self, source, target, peer, start=True):
        at = self.sent
        self.sent += 1
        copy = pltpu.make_async_remote_copy(
            source, target, self.send_sems.at[at], self.recv_sems.at[at], device_id=peer, device_id_type=MESH
        )
        if start:
            copy.start()
        self.open_sends.append(copy)
        return copy

    def send_when(self, condition, source, target, peer):
        copy = self.send(source, target, peer, start=False)
        self.open_sends.pop()
        self.at_times.append((condition, copy))
        pl.when(condition)(copy.start)
        return copy

    def move(self, source, target, keep=True):
        copy = pltpu.make_async_copy(source, target, self.local_sems.at[self.moved])
        self.moved += 1
        copy.start()
        if keep:
            self.open_moves.append(copy)
        return copy

    def close(self):
        for copy in self.open_sends:
            copy.wait_send()
        for condition, copy in self.at_times:
            pl.when(condition)(copy.wait_send)
        for copy in self.open_moves:
            copy.wait()


class Rounds:
    def __init__(self, rounds):
        self.rounds, self.at = rounds, 0

    def go(self, count=None):
        count = len(self.rounds) if count is None else count
        for copies in self.rounds[self.at : self.at + count]:
            for copy in copies:
                copy.start()
        self.at = min(self.at + count, len(self.rounds))

    def later(self, count=None):
        return lambda: self.go(count)

    def copies(self, first=0, last=None):
        return [copy for copies in self.rounds[first:last] for copy in copies]


def arrived(copies):
    for copy in copies:
        copy.wait_recv()


class Place:
    def __init__(self):
        grp, batch = lax.axis_size("grp"), lax.axis_size("batch")
        self.grp, self.lines = grp, batch // 2
        self.me, self.mine = lax.axis_index("grp"), lax.axis_index("batch")
        self.core, self.line = lax.rem(self.mine, 2), self.mine // 2
        self.sibling = {"batch": self.mine + 1 - 2 * self.core}
        self.across = [{"grp": self.partner(k)} for k in range(1, grp)]
        self.along = [{"batch": self.next_line(k) * 2 + self.core} for k in range(1, self.lines)]
        self.far = {"batch": (self.line + 2 - 4 * (self.line // 2)) * 2 + self.core}
        self.near = {"batch": (self.line + 1 - 2 * lax.rem(self.line, 2)) * 2 + self.core}

    def partner(self, k):
        low = lax.rem(lax.rem(self.me, 2) + (k % 2 if isinstance(k, int) else lax.rem(k, 2)), 2)
        return lax.rem(self.me // 2 + k // 2, 2) * 2 + low

    def next_line(self, k):
        return lax.rem(self.line + k, self.lines)


def partner_rounds(here, links, rows, part, pair, near=(0, None), far=(0, None)):
    rounds = []
    for ks, (first, last) in ((tuple(range(1, here.grp - 1)), near), ((here.grp - 1,), far)):
        for at in range(0, rows, part)[first:last]:
            copies = [links.send(*pair(k, pl.ds(at, part)), here.across[k - 1], start=False) for k in ks]
            rounds.append(copies)
    return rounds


def rows_of(index, rows, span):
    return pl.ds(pl.multiple_of(index * rows, rows) + span.start, span.size)


def aligned(at, size):
    return pl.ds(pl.multiple_of(at, size), size)


def block_weights(wg_ref, number, blocks):
    lanes = lax.broadcasted_iota(jnp.int32, (GW, 128), 1) // GW
    zero = jnp.zeros((GW, 128), BF16)
    for group in range(BLK // GW):
        for tap in range(9):
            piece = wg_ref[number, group // 2, group % 2, (tap // 4) * GW : (tap // 4 + 1) * GW].astype(F32)
            turn = ((group - tap) % 4) * GW
            if turn:
                piece = pltpu.roll(piece, turn, 1)
            piece = jnp.where(lanes == group % 4, piece, 0.0).astype(BF16)
            row = tap * BLK + group * GW
            left = (group // 4) * 128
            blocks[row : row + GW, left : left + 128] = piece
            blocks[row : row + GW, 128 - left : 256 - left] = zero


def pack_groups(transposed):
    lanes = lax.broadcasted_iota(jnp.int32, (GW, 128), 1) - lax.broadcasted_iota(jnp.int32, (GW, 128), 0)
    at = [dot_left(transposed, jnp.where(lanes == tap * GW, 1.0, 0.0).astype(BF16)) for tap in range(4)]
    rows = []
    for first in range(0, 9, 4):
        taps = range(first, min(first + 4, 9))
        rows.append(add_rows([at[tap % 4][tap * GW : (tap + 1) * GW] for tap in taps]))
    return jnp.concatenate(rows, axis=0).astype(BF16)


def spread_mask(valid, images):
    rows = images * HW
    image = lax.broadcasted_iota(jnp.int32, (rows, images), 0) % images
    chosen = jnp.where(image == lax.broadcasted_iota(jnp.int32, (rows, images), 1), 1.0, 0.0)
    frames = dot(chosen.astype(BF16), valid.astype(BF16))
    pixel = lax.broadcasted_iota(jnp.int32, (rows, HW), 0) // images
    own = jnp.where(pixel == lax.broadcasted_iota(jnp.int32, (rows, HW), 1), frames, 0.0)
    return jnp.broadcast_to(jnp.sum(own, axis=1, keepdims=True), (rows, 128))


def block_stats(z_ref, left, columns, m_ref, st_ref, step):
    rows = z_ref.shape[0]
    for part in range(0, columns, BLK):
        span = pl.ds(pl.multiple_of(left + part, BLK), BLK)
        total = jnp.zeros((1, BLK), F32)
        count = jnp.zeros((1, 128), F32)
        for at in range(0, rows, step):
            mask = m_ref[at : at + step]
            total += jnp.sum(z_ref[at : at + step, span] * wide(mask, BLK), axis=0, keepdims=True)
            count += jnp.sum(mask, axis=0, keepdims=True)
        count = wide(count, BLK)
        centre = total / count
        spread = jnp.zeros((1, BLK), F32)
        for at in range(0, rows, step):
            off = (z_ref[at : at + step, span] - centre) * wide(m_ref[at : at + step], BLK)
            spread += jnp.sum(off * off, axis=0, keepdims=True)
        st_ref[0:1, span] = total
        st_ref[1:2, span] = spread
        st_ref[2:3, span] = count


def smooth(pre, mask):
    sigma = sigmoid(pre)
    masked = sigma * mask
    return pre * masked, masked * (1.0 + pre * (1.0 - sigma))


NEAR_ROUNDS = 3
FWD_OUTS = ("inner", "x1", "act1", "slope1", "x2", "act2", "slope2", "x3", "grads", "wr", "we", "wg", "far")


def forward_kernel(*refs, images, gather):
    (feat, cotg, valid_ref, np_ref, op_ref, wr_in, we_in, wg_in) = refs[:8]
    big = dict(zip(FWD_OUTS, refs[8:21]))
    block_out, m_ref, n1, n2, n3, norm_all, out_all, sums3 = refs[21:29]
    refs = refs[:28] + refs[29:]
    (inner, x1, act1, slope1, x2, act2, slope2, x3, grads, wr, we, wg) = refs[28:40]
    (land_f, land_c, cot, perm, back, z1, ze, col, blocks, st1, st2, st3, st4, send, recv, moves) = refs[40:56]
    ex1, ex2, ex3, ex4 = (refs[56 + 7 * k : 63 + 7 * k] for k in range(4))
    held = dict(zip(FWD_OUTS, (inner, x1, act1, slope1, x2, act2, slope2, x3, grads, wr, we, wg)))
    here = Place()
    grp = here.grp
    rows, own_in = land_f.shape[1:]
    width, channels = z1.shape[1], ze.shape[1]
    own_width = np_ref.shape[1]
    step = SIDE * images
    links = Links(send, recv, moves)

    greet(everyone())
    own_rows = aligned(here.me * rows, rows)
    own_f = links.move(feat.at[own_rows], land_f.at[0], keep=False)
    if gather:
        shard_r, shard_e = refs[84:86]
        shards = [
            links.move(wr_in, shard_r, keep=False),
            links.move(we_in, shard_e, keep=False),
        ]
        wg[here.me, here.line, here.core] = pack_groups(wg_in[...].astype(BF16))
        for copy in shards:
            copy.wait()
        wr[here.me, here.line, here.core] = shard_r[...].astype(BF16)
        we[here.me, here.line, here.core] = shard_e[...].astype(BF16)
        loads = []
    else:
        loads = [links.move(wr_in, wr, keep=False), links.move(we_in, we, keep=False), links.move(wg_in, wg, keep=False)]
    norm_all[:, aligned(here.me * own_width, own_width)] = np_ref[...]
    out_all[:, aligned(here.me * own_in, own_in)] = op_ref[...]
    greeted(everyone())

    def spread_out(buffer, targets, rows=slice(None)):
        place = buffer.at[here.me, here.line, here.core, rows]
        return [links.send(place, place, peer) for peer in targets]

    if gather:
        quarter = wr.shape[3] // 4
        head, rest = pl.ds(0, quarter), pl.ds(quarter, 3 * quarter)
        half = we.shape[3] // 2
        lower, upper = pl.ds(0, half), pl.ds(half, half)
        wr_a = spread_out(wr, here.across, rest)
        wr_z = spread_out(wr, here.along, head)
    small = []
    for k in range(1, grp):
        peer = here.across[k - 1]
        span = aligned(here.me * own_width, own_width)
        small.append(links.send(np_ref, norm_all.at[:, span], peer))
        span = aligned(here.me * own_in, own_in)
        small.append(links.send(op_ref, out_all.at[:, span], peer))
    from_f = {}
    for k in range(1, grp):
        source = feat.at[aligned(here.partner(k) * rows, rows)]
        from_f[k] = links.send(source, land_f.at[k], here.across[k - 1])
    own_c = links.move(cotg.at[own_rows], land_c.at[0], keep=False)
    if gather:
        arrived(wr_a)
        place = wr.at[:, here.line, here.core, rest]
        last = here.lines - 1
        up, down = here.along[0], here.along[last - 1]
        line_up = [links.send_when(here.line < last, place, place, up)]
        line_down = [links.send_when(here.line > 0, place, place, down)]
        wr_b = [links.send(place, place, here.sibling)]
        arrived(wr_z)
        place = wr.at[here.me, :, here.core, head]
        wr_g = [links.send(place, place, peer) for peer in here.across]
        wg_a = spread_out(wg, here.along)
        we_a0 = spread_out(we, here.across, lower)
        we_a1 = spread_out(we, here.along, upper)
    perm[...] = to_inner(rows, images)
    back[...] = to_outer(rows, images)
    m_ref[...] = spread_mask(valid_ref[...], images)
    wr_c = []

    def hand_on(steps):
        if gather:
            for k in steps:
                from_below, from_above = here.line >= k, here.line <= last - k
                pl.when(from_below)(line_up[k - 1].wait_recv)
                place = wr.at[:, here.next_line(here.lines - k), here.core, rest]
                if k < last:
                    line_up.append(links.send_when(jnp.logical_and(from_below, here.line < last), place, place, up))
                wr_c.append((from_below, links.send_when(from_below, place, place, here.sibling)))
                pl.when(from_above)(line_down[k - 1].wait_recv)
                place = wr.at[:, here.next_line(k), here.core, rest]
                if k < last:
                    line_down.append(links.send_when(jnp.logical_and(from_above, here.line > 0), place, place, down))
                wr_c.append((from_above, links.send_when(from_above, place, place, here.sibling)))

    def place_features(number):
        if number:
            from_f[number].wait_recv()
        span = aligned(here.partner(number) * own_in, own_in)
        inner[:, span] = dot(perm[...], land_f[number]).astype(BF16)

    own_f.wait()
    place_features(0)
    hand_on(range(1, here.lines - 1))
    for number in range(1, grp - 1):
        place_features(number)
    hand_on([here.lines - 1])
    place_features(grp - 1)
    if gather:
        arrived(wr_g)
        place = wr.at[:, :, here.core, head]
        wr_b.append(links.send(place, place, here.sibling))
        arrived(wg_a)
        place = wg.at[here.me, :, here.core]
        wg_b = [links.send(place, place, peer) for peer in here.across]
        arrived(we_a0)
        arrived(we_a1)
        we_z = Rounds(
            [
                [
                    links.send(
                        we.at[a, here.line, here.core, lower], we.at[a, here.line, here.core, lower], peer, start=False
                    )
                    for peer in here.along
                ]
                for a in range(grp)
            ]
        )
        we_g = Rounds(
            [
                [
                    links.send(we.at[here.me, b, here.core, upper], we.at[here.me, b, here.core, upper], peer, start=False)
                    for peer in here.across
                ]
                for b in range(here.lines)
            ]
        )
        we_z.go(1)
        we_g.go(1)
        arrived(wr_b)
        for condition, copy in wr_c:
            pl.when(condition)(copy.wait_recv)
    for copy in loads:
        copy.wait()
    links.move(inner, big["inner"])

    steps = width // BLK

    @pl.loop(0, steps)
    def _(number):
        span = aligned(number * BLK, BLK)
        z1[:, span] = dot(inner[...], wr[:, :, :, :, span].reshape(channels, BLK))
        block_stats(z1, number * BLK, BLK, m_ref, st1, step)

    links.move(wr, big["wr"])
    arrived(small)
    from_c = Rounds(
        partner_rounds(
            here,
            links,
            rows,
            step,
            lambda k, span: (cotg.at[rows_of(here.partner(k), rows, span)], land_c.at[k, span]),
        )
    )
    wg_c = []

    def groups_on():
        if gather:
            arrived(wg_b)
            place = wg.at[:, :, here.core]
            wg_c.append(links.send(place, place, here.sibling))
            we_g.go(1)
            we_z.go(2)

    def expand_on():
        if gather:
            we_g.go(1)

    n1[...] = norm_rows(over_devices(st1, ex1, merge_stats, (expand_on, groups_on)))
    arrived(wg_c)
    if gather:
        we_g.go()
    from_c.go(1)

    clear_edges(col, images, False)

    @pl.loop(0, steps)
    def _(number):
        span = aligned(number * BLK, BLK)
        block_weights(wg, number, blocks)
        centre, scale = n1[0:1, span], n1[1:2, span]
        gain, bias = norm_all[0:1, span], norm_all[1:2, span]
        for row in range(SIDE):
            at = row * step
            mask = wide(m_ref[at : at + step], BLK)
            normed = (z1[at : at + step, span] - centre) * scale
            value, slope = smooth(normed * gain + bias, mask)
            act = value.astype(BF16)
            x1[at : at + step, span] = normed.astype(BF16)
            act1[at : at + step, span] = act
            slope1[at : at + step, span] = slope.astype(BF16)
            spread_row(col, act, row, images, False)
        z1[:, span] = dot(col[...], blocks[...])
        block_stats(z1, number * BLK, BLK, m_ref, st2, step)

    for name in ("x1", "act1", "slope1", "wg"):
        links.move(held[name], big[name])
    if gather:
        arrived(we_g.copies())
        arrived(we_z.copies(0, 3))
        place = we.at[:, :, here.core, upper]
        we_c = [links.send(place, place, here.sibling)]
        place = we.at[0 : grp - 1, :, here.core, lower]
        we_c.append(links.send(place, place, here.sibling))

    def expand_last():
        if gather:
            we_z.go()
        from_c.go(2)

    n2[...] = norm_rows(over_devices(st2, ex2, merge_stats, (from_c.later(2), expand_last)))
    from_c.go(2)

    @pl.loop(0, steps)
    def _(number):
        span = aligned(number * BLK, BLK)
        for at in range(0, rows, step):
            mask = wide(m_ref[at : at + step], BLK)
            normed = (z1[at : at + step, span] - n2[0:1, span]) * n2[1:2, span]
            value, slope = smooth(normed * norm_all[2:3, span] + norm_all[3:4, span], mask)
            x2[at : at + step, span] = normed.astype(BF16)
            act2[at : at + step, span] = value.astype(BF16)
            slope2[at : at + step, span] = slope.astype(BF16)

    for name in ("x2", "act2", "slope2"):
        links.move(held[name], big[name])
    from_c.go(3)
    if gather:
        arrived(we_z.copies(3))
        place = we.at[grp - 1, :, here.core, lower]
        we_c.append(links.send(place, place, here.sibling))
        arrived(we_c)
    links.move(we, big["we"])

    @pl.loop(0, grp)
    def _(number):
        for part in range(0, own_in, BLK):
            span = pl.ds(pl.multiple_of(number * own_in + part, BLK), BLK)
            ze[:, span] = dot(act2[...], we[number, :, :, :, part : part + BLK].reshape(width, BLK))
        block_stats(ze, number * own_in, own_in, m_ref, st3, step)

    n3[...] = norm_rows(over_devices(st3, ex3, merge_stats, (from_c.later(1), from_c.later(1))))
    from_c.go()
    own_c.wait()
    to_near = Rounds(
        partner_rounds(
            here,
            links,
            rows,
            step,
            lambda k, span: (land_f.at[k, span], block_out.at[rows_of(here.me, rows, span)]),
            near=(0, NEAR_ROUNDS),
            far=(0, 0),
        )
    )
    parts = SIDE
    arrived(from_c.copies(0, parts))

    def output_block(slot):
        number = here.partner(slot)
        cot[...] = dot(perm[...], land_c[slot])
        for part in range(0, own_in, BLK):
            span = pl.ds(pl.multiple_of(number * own_in + part, BLK), BLK)
            local = slice(part, part + BLK)
            bias_grad = jnp.zeros((1, BLK), F32)
            gain_grad = jnp.zeros((1, BLK), F32)
            for at in range(0, rows, step):
                mask = wide(m_ref[at : at + step], BLK)
                normed = (ze[at : at + step, span] - n3[0:1, span]) * n3[1:2, span]
                summed = normed * out_all[0:1, span] + out_all[1:2, span] + inner[at : at + step, span].astype(F32)
                value, slope = smooth(summed, mask)
                grad = cot[at : at + step, local] * slope
                x3[at : at + step, span] = normed.astype(BF16)
                col[at : at + step, local] = value.astype(BF16)
                grads[at : at + step, span] = grad.astype(BF16)
                bias_grad += jnp.sum(grad, axis=0, keepdims=True)
                gain_grad += jnp.sum(grad * normed, axis=0, keepdims=True)
            st4[0:1, span] = bias_grad
            st4[1:2, span] = gain_grad
        land_f[slot] = dot(back[...], col[:, 0:own_in]).astype(BF16)

    pl.loop(0, grp - 1)(output_block)
    to_near.go(1)
    arrived(from_c.copies(parts))
    output_block(grp - 1)
    links.move(land_f.at[0], block_out.at[own_rows])
    links.move(land_f.at[1:], big["far"])
    for name in ("x3", "grads"):
        links.move(held[name], big[name])
    sums3[...] = over_devices(st4, ex4, add_rows, (to_near.later(1), to_near.later()))
    arrived(to_near.copies())
    links.close()


def forward(features, out_cotangent, valid, norm_params, out_params, reduce_w, expand_w, group_w, gather):
    grp = lax.axis_size("grp")
    rows = features.shape[0] // grp
    own_in = features.shape[1]
    channels = own_in * grp
    width = norm_params.shape[1] * grp
    lines, cores = (lax.axis_size("batch") // 2, 2) if gather else (1, 1)
    r_shape = (grp, lines, cores, own_in // (lines * cores), width)
    e_shape = (grp, lines, cores, width // (lines * cores), own_in)
    g_shape = (width // BLK, BLK // GW // 2, 2, 3 * GW, 128)
    across = (rows, width)
    shapes = {
        "inner": (rows, channels),
        "x1": across,
        "act1": across,
        "slope1": across,
        "x2": across,
        "act2": across,
        "slope2": across,
        "x3": (rows, channels),
        "grads": (rows, channels),
        "far": (grp - 1, rows, own_in),
        "wr": r_shape,
        "we": e_shape,
        "wg": g_shape,
    }
    small = [(rows, 128), (3, width), (3, width), (3, channels), (4, width), (2, channels), (2, channels)]
    vmem = pl.BlockSpec(memory_space=pltpu.VMEM)
    hbm = pl.BlockSpec(memory_space=pl.ANY)
    if gather:
        weights = (reduce_w, expand_w, group_w)
    else:
        weights = (reduce_w.reshape(r_shape), expand_w.reshape(e_shape), group_w.reshape(g_shape))
    results = pl.pallas_call(
        functools.partial(forward_kernel, images=rows // HW, gather=gather),
        out_shape=[jax.ShapeDtypeStruct(shapes[name], BF16) for name in FWD_OUTS]
        + [jax.ShapeDtypeStruct(features.shape, BF16)]
        + [jax.ShapeDtypeStruct(shape, F32) for shape in small],
        in_specs=[hbm, hbm, vmem, vmem, vmem, hbm, hbm, vmem if gather else hbm],
        out_specs=[hbm] * (len(FWD_OUTS) + 1) + [vmem] * len(small),
        scratch_shapes=[pltpu.VMEM(shapes[name], BF16) for name in FWD_OUTS[:-1]]
        + [
            pltpu.VMEM((grp, rows, own_in), BF16),
            pltpu.VMEM((grp, rows, own_in), BF16),
            pltpu.VMEM((rows, own_in), F32),
            pltpu.VMEM((rows, rows), BF16),
            pltpu.VMEM((rows, rows), BF16),
            pltpu.VMEM(across, F32),
            pltpu.VMEM((rows, channels), F32),
            pltpu.VMEM((rows, 9 * BLK), BF16),
            pltpu.VMEM((9 * BLK, BLK), BF16),
            pltpu.VMEM((3, width), F32),
            pltpu.VMEM((3, width), F32),
            pltpu.VMEM((3, channels), F32),
            pltpu.VMEM((2, channels), F32),
            pltpu.SemaphoreType.DMA((112,)),
            pltpu.SemaphoreType.DMA((112,)),
            pltpu.SemaphoreType.DMA((24,)),
        ]
        + sums_scratch(3, width)
        + sums_scratch(3, width)
        + sums_scratch(3, channels)
        + sums_scratch(2, channels)
        + ([pltpu.VMEM(reduce_w.shape, F32), pltpu.VMEM(expand_w.shape, F32)] if gather else []),
        compiler_params=params(collective_id=1, has_side_effects=True),
    )(features, out_cotangent, valid, norm_params, out_params, *weights)
    return dict(zip(FWD_OUTS, results)), results[len(FWD_OUTS)], results[len(FWD_OUTS) + 1 :]


def packed_groups(weight):
    groups = weight.shape[1] // GW
    taps = jnp.pad(weight.reshape(9, GW, groups, GW), ((0, 3), (0, 0), (0, 0), (0, 0)))
    return taps.reshape(3, 4, GW, groups, GW).transpose(3, 0, 2, 1, 4).reshape(groups, 3 * GW, 4 * GW)


BWD_INS = ("grads", "x3", "we", "act2", "slope2", "x2", "act1", "slope1", "x1", "wg", "wr")


def backward_kernel(*refs, images, owners):
    _, far_in, inner_in = refs[:3]
    given = dict(zip(BWD_INS, refs[3:14]))
    m_ref, n1, n2, n3, norm_all, out_all, sums3 = refs[14:21]
    refs = refs[21:]
    state, refs = (refs[:15], refs[15:]) if owners else ((), refs)
    block_out, input_grad, reduce_out, expand_out, group_out, sums1, sums2 = refs[:7]
    raws, refs = ((reduce_out, group_out, expand_out, *refs[7:9]), refs[9:]) if owners else ((), refs[7:])
    scalars, refs = (refs[0], refs[1:]) if owners else (None, refs)
    (grads, x3, we, act2, slope2, x2, act1, slope1, x1, wg, wr) = refs[:11]
    held = dict(zip(BWD_INS, (grads, x3, we, act2, slope2, x2, act1, slope1, x1, wg, wr)))
    (ge, dp, col, blocks, turned, grad_in, back, st1, st2, raw_e, raw_r, raw_g, send, recv, moves) = refs[11:26]
    ex1, ex2 = refs[26:33], refs[33:40]
    here = Place()
    me, grp, core, line, lines = here.me, here.grp, here.core, here.line, here.lines
    rows, width = dp.shape
    channels = grads.shape[1]
    own_in = channels // grp
    step = SIDE * images
    steps = width // BLK
    links = Links(send, recv, moves)
    if owners:
        e_slots, r_slots = refs[40:45], refs[45:50]
        (g1, g2, g3, g4, gs1, gs2, gs3) = refs[50:57]
        trust_scratch = refs[57:72]
        state_in, state = state, refs[72:]

    greet(everyone())
    loads = {name: links.move(given[name], held[name], keep=False) for name in BWD_INS[:4]}
    own_rows = aligned(me * rows, rows)
    back[...] = to_outer(rows, images)
    greeted(everyone())
    to_out = Rounds(
        partner_rounds(
            here,
            links,
            rows,
            step,
            lambda k, span: (far_in.at[k - 1, span], block_out.at[rows_of(me, rows, span)]),
            near=(NEAR_ROUNDS, None),
        )
    )
    to_out.go(7)

    def core_swap(raw, slots):
        return [
            links.send(raw.at[a, :, 1 - core], slots[0].at[a], here.sibling, start=False) for a in range(grp)
        ]

    def swap_now(copies, number):
        for a, copy in enumerate(copies):

            @pl.when(number == a)
            def _():
                copy.start()

    def add_core(raw, slots):
        @pl.loop(0, grp * lines)
        def _(at):
            a, b = at // lines, lax.rem(at, lines)
            slots[0][a, b] = (raw[a, b, core].astype(F32) + slots[0][a, b].astype(F32)).astype(BF16)

    def cuts(slots):
        cut, rest = slots[1].shape[2], slots[2].shape[2]
        return cut, pl.ds(0, cut), pl.ds(cut, rest)

    def spread_sums(slots):
        one, grp_slots, line_slots = slots[:3]
        _, lower, upper = cuts(slots)
        over = [
            links.send(one.at[here.partner(k), :, lower], grp_slots.at[k - 1], here.across[k - 1])
            for k in range(1, grp)
        ]
        along = [
            links.send(one.at[:, here.next_line(k), upper], line_slots.at[k - 1], here.along[k - 1])
            for k in range(1, lines)
        ]
        return over, along

    def add_over(slots):
        one, grp_slots = slots[:2]
        cut = cuts(slots)[0]

        @pl.loop(0, lines)
        def _(b):
            piece = one[me, b, 0:cut].astype(F32)
            for k in range(grp - 1):
                piece += grp_slots[k, b].astype(F32)
            grp_slots[0, b] = piece.astype(BF16)

        return [
            links.send(grp_slots.at[0, here.next_line(k)], slots[3].at[k - 1], here.along[k - 1])
            for k in range(1, lines)
        ]

    def add_along(slots):
        one, line_slots = slots[0], slots[2]
        cut = cuts(slots)[0]

        @pl.loop(0, grp)
        def _(a):
            piece = one[a, line, cut:].astype(F32)
            for k in range(lines - 1):
                piece += line_slots[k, a].astype(F32)
            line_slots[0, a] = piece.astype(BF16)

        return [
            links.send(line_slots.at[0, here.partner(k)], slots[4].at[k - 1], here.across[k - 1])
            for k in range(1, grp)
        ]

    def add_last(slots, out):
        cut = cuts(slots)[0]
        piece = slots[1][0, line].astype(F32)
        for k in range(lines - 1):
            piece += slots[3][k].astype(F32)
        out[0:cut] = piece
        piece = slots[2][0, me].astype(F32)
        for k in range(grp - 1):
            piece += slots[4][k].astype(F32)
        out[cut:] = piece

    for name in BWD_INS[:4]:
        loads[name].wait()
    loads.update({name: links.move(given[name], held[name], keep=False) for name in BWD_INS[4:]})
    if owners:
        state_loads = [links.move(source, target, keep=False) for source, target in zip(state_in, state)]
        e_core = core_swap(raw_e, e_slots)

    @pl.loop(0, grp)
    def _(number):
        for part in range(0, own_in, BLK):
            span = pl.ds(pl.multiple_of(number * own_in + part, BLK), BLK)
            inverse = 1.0 / n3[2:3, span]
            factor = out_all[0:1, span] * n3[1:2, span]
            for at in range(0, rows, step):
                mask = wide(m_ref[at : at + step], BLK)
                normed = x3[at : at + step, span].astype(F32)
                shift = (sums3[0:1, span] + normed * sums3[1:2, span]) * inverse
                value = mask * factor * (grads[at : at + step, span].astype(F32) - shift)
                ge[at : at + step, part : part + BLK] = value.astype(BF16)
        per = we.shape[3]
        taken = BLK // per if per < BLK else 1
        for left in range(0, width, BLK):
            if per < BLK:
                slots = [divmod(left // per + k, we.shape[2]) for k in range(taken)]
                weights = jnp.concatenate([we[number, b, c] for b, c in slots], axis=0)
            else:
                weights = we[number, 0, 0, left : left + BLK]
            part_sum = dot_right(ge[...], weights)
            block = dot_left(act2[:, left : left + BLK], ge[...]).astype(BF16)
            if per < BLK:
                for k, (b, c) in enumerate(slots):
                    raw_e[number, b, c] = block[k * per : (k + 1) * per]
            else:
                raw_e[number, 0, 0, left : left + BLK] = block

            @pl.when(number == 0)
            def _():
                dp[:, left : left + BLK] = part_sum

            @pl.when(number > 0)
            def _():
                dp[:, left : left + BLK] += part_sum

        if owners:
            swap_now(e_core, number)

    if not owners:
        links.move(raw_e, expand_out)
    for name in ("slope2", "x2"):
        loads[name].wait()

    def norm_sums(slope, normed, sums):
        @pl.loop(0, steps)
        def _(number):
            span = aligned(number * BLK, BLK)
            bias_grad = jnp.zeros((1, BLK), F32)
            gain_grad = jnp.zeros((1, BLK), F32)
            for at in range(0, rows, step):
                grad = dp[at : at + step, span] * slope[at : at + step, span].astype(F32)
                dp[at : at + step, span] = grad
                bias_grad += jnp.sum(grad, axis=0, keepdims=True)
                gain_grad += jnp.sum(grad * normed[at : at + step, span].astype(F32), axis=0, keepdims=True)
            sums[0:1, span] = bias_grad
            sums[1:2, span] = gain_grad

    norm_sums(slope2, x2, st2)
    sums2[...] = over_devices(st2, ex2, add_rows, (to_out.later(1), to_out.later(1)))
    if owners:
        arrived(e_core)
        add_core(raw_e, e_slots)
        e_over, e_along = spread_sums(e_slots)

    for name in ("act1", "slope1", "x1", "wg"):
        loads[name].wait()
    own = (
        lax.broadcasted_iota(jnp.int32, (BLK, BLK), 0) // GW == lax.broadcasted_iota(jnp.int32, (BLK, BLK), 1) // GW
    )

    @pl.loop(0, steps)
    def _(number):
        span = aligned(number * BLK, BLK)
        inverse = 1.0 / n2[2:3, span]
        factor = norm_all[2:3, span] * n2[1:2, span]
        clear_edges(col, images, False)
        for row in range(SIDE):
            at = row * step
            mask = wide(m_ref[at : at + step], BLK)
            normed = x2[at : at + step, span].astype(F32)
            shift = (sums2[0:1, span] + normed * sums2[1:2, span]) * inverse
            grad_in[at : at + step] = (mask * factor * (dp[at : at + step, span] - shift)).astype(BF16)
            spread_row(col, act1[at : at + step, span], row, images, False)
        for tap in range(9):
            product = dot_left(col[:, tap * BLK : (tap + 1) * BLK], grad_in[...])
            product = jnp.where(own, product, 0.0)
            piece = product[0:GW]
            for group in range(1, BLK // GW):
                piece += product[group * GW : (group + 1) * GW]
            raw_g[tap * GW : (tap + 1) * GW, span] = piece.astype(BF16)
        clear_edges(col, images, True)
        for row in range(SIDE):
            at = row * step
            spread_row(col, grad_in[at : at + step], row, images, True)
        block_weights(wg, number, blocks)
        for tap in range(9):
            turned[tap * BLK : (tap + 1) * BLK] = blocks[tap * BLK : (tap + 1) * BLK].astype(F32).T.astype(BF16)
        dp[:, span] = dot(col[...], turned[...])

    norm_sums(slope1, x1, st1)
    inner = col.at[:, 0:channels]
    load_inner = links.move(inner_in, inner, keep=False)
    g_grp = []

    def groups_on():
        if owners:
            g_grp.extend(
                links.send(raw_g.at[:, aligned(here.partner(k) * BLK, BLK)], g1.at[k - 1], here.across[k - 1])
                for k in range(1, grp)
            )

    if not owners:
        links.move(raw_g, group_out)
    sums1[...] = over_devices(st1, ex1, add_rows, (to_out.later(1), groups_on))
    if owners:
        arrived(e_over)
        e_last = add_over(e_slots)
        arrived(e_along)
        e_last += add_along(e_slots)
        r_core = core_swap(raw_r, r_slots)
    to_out.go()

    @pl.loop(0, steps)
    def _(number):
        span = aligned(number * BLK, BLK)
        inverse = 1.0 / n1[2:3, span]
        factor = norm_all[0:1, span] * n1[1:2, span]
        for at in range(0, rows, step):
            mask = wide(m_ref[at : at + step], BLK)
            normed = x1[at : at + step, span].astype(F32)
            shift = (sums1[0:1, span] + normed * sums1[1:2, span]) * inverse
            x1[at : at + step, span] = (mask * factor * (dp[at : at + step, span] - shift)).astype(BF16)

    grad_reduce = x1
    load_inner.wait()
    per_r = raw_r.shape[3]

    @pl.loop(0, grp)
    def _(number):
        for part in range(0, own_in, BLK):
            span = pl.ds(pl.multiple_of(number * own_in + part, BLK), BLK)
            block = dot_left(col[:, span], grad_reduce[...]).astype(BF16)
            if per_r < BLK:
                for k in range(BLK // per_r):
                    b, c = divmod(part // per_r + k, raw_r.shape[2])
                    raw_r[number, b, c] = block[k * per_r : (k + 1) * per_r]
            else:
                raw_r[number, 0, 0, part : part + BLK] = block
        if owners:
            swap_now(r_core, number)

    if owners:
        arrived(r_core)
        add_core(raw_r, r_slots)
        r_over, r_along = spread_sums(r_slots)
        arrived(g_grp)
        total = raw_g[:, aligned(me * BLK, BLK)].astype(F32)
        for k in range(grp - 1):
            total += g1[k].astype(F32)
        gs1[...] = total.astype(BF16)
        high = line // 2
        g_far = links.send(gs1.at[:, aligned((1 - high) * 128, 128)], g2, here.far)
    else:
        links.move(raw_r, reduce_out)
    loads["wr"].wait()

    @pl.loop(0, grp)
    def _(number):
        for part in range(0, own_in, BLK):
            span = pl.ds(pl.multiple_of(number * own_in + part, BLK), BLK)
            per = wr.shape[3]
            if per < BLK:
                slots = [divmod(part // per + k, wr.shape[2]) for k in range(BLK // per)]
                weights = jnp.concatenate([wr[number, b, c] for b, c in slots], axis=0)
            else:
                weights = wr[number, 0, 0, part : part + BLK]
            total = grads[:, span].astype(F32) + dot_right(grad_reduce[...], weights)
            ge[:, part : part + BLK] = total.astype(BF16)
        grads[:, aligned(number * own_in, own_in)] = dot(back[...], ge[...]).astype(BF16)

    to_in = Rounds(
        partner_rounds(
            here,
            links,
            rows,
            step,
            lambda k, span: (
                grads.at[span, aligned(here.partner(k) * own_in, own_in)],
                input_grad.at[rows_of(me, rows, span)],
            ),
        )
    )
    links.move(grads.at[:, aligned(me * own_in, own_in)], input_grad.at[own_rows])
    if owners:
        to_in.go(7)
        g_far.wait_recv()
        gs2[...] = (gs1[:, aligned(high * 128, 128)].astype(F32) + g2[...].astype(F32)).astype(BF16)
        g_near = links.send(gs2, g3, here.near)
        arrived(e_last)
        add_last(e_slots, expand_out)
        g_near.wait_recv()
        gs3[...] = (gs2[...].astype(F32) + g3[...].astype(F32)).astype(BF16)
        g_last = links.send(gs3, g4, here.sibling)
        own_width = width // grp
        span = aligned(me * own_width, own_width)
        raws[3][0:1], raws[3][1:2] = sums1[1:2, span], sums1[0:1, span]
        raws[3][2:3], raws[3][3:4] = sums2[1:2, span], sums2[0:1, span]
        span = aligned(me * own_in, own_in)
        raws[4][0:1], raws[4][1:2] = sums3[1:2, span], sums3[0:1, span]
        g_last.wait_recv()
        turned_sum = (gs3[...].astype(F32) + g4[...].astype(F32)).T
        quarter = lax.rem(here.mine, 4)
        piece = turned_sum[0:GW]
        for k in range(1, 4):
            piece = jnp.where(quarter == k, turned_sum[k * GW : (k + 1) * GW], piece)
        group_out[...] = piece
        arrived(r_over)
        r_last = add_over(r_slots)
        arrived(r_along)
        r_last += add_along(r_slots)
        to_in.go(2)
        arrived(r_last)
        add_last(r_slots, reduce_out)
        for copy in state_loads:
            copy.wait()
        beside = (to_in.later(1), to_in.later(2), to_in.later(1), to_in.later())
        trust(
            raws,
            state[:5],
            state[5:10],
            state[10:],
            scalars,
            trust_scratch[0],
            trust_scratch[1:8],
            trust_scratch[8:],
            beside,
        )
    else:
        to_in.go()
    arrived(to_out.copies())
    arrived(to_in.copies())
    links.close()


def backward(kept, block_out, mask, n1, n2, n3, norm_all, out_all, sums3, state, owners):
    grp = lax.axis_size("grp")
    rows, width = kept["act1"].shape
    channels = kept["x3"].shape[1]
    own_in = channels // grp
    r_shape, e_shape = kept["wr"].shape, kept["we"].shape
    lines = r_shape[1]
    vmem = pl.BlockSpec(memory_space=pltpu.VMEM)
    hbm = pl.BlockSpec(memory_space=pl.ANY)
    if owners:
        parts = [
            jax.ShapeDtypeStruct(r_shape[3:], F32),
            jax.ShapeDtypeStruct(e_shape[3:], F32),
            jax.ShapeDtypeStruct((GW, 9 * GW), F32),
        ]
        last = [
            jax.ShapeDtypeStruct((4, width // grp), F32),
            jax.ShapeDtypeStruct((2, own_in), F32),
            jax.ShapeDtypeStruct((8, 128), F32),
        ]
    else:
        last = []
        parts = [jax.ShapeDtypeStruct(shape, BF16) for shape in (r_shape, e_shape, (9 * GW, width))]
    sums = [jax.ShapeDtypeStruct((2, width), F32)] * 2
    scratch = [pltpu.VMEM(kept[name].shape, BF16) for name in BWD_INS] + [
        pltpu.VMEM((rows, own_in), BF16),
        pltpu.VMEM((rows, width), F32),
        pltpu.VMEM((rows, 9 * BLK), BF16),
        pltpu.VMEM((9 * BLK, BLK), BF16),
        pltpu.VMEM((9 * BLK, BLK), BF16),
        pltpu.VMEM((rows, BLK), BF16),
        pltpu.VMEM((rows, rows), BF16),
        pltpu.VMEM((2, width), F32),
        pltpu.VMEM((2, width), F32),
        pltpu.VMEM(e_shape, BF16),
        pltpu.VMEM(r_shape, BF16),
        pltpu.VMEM((9 * GW, width), BF16),
        pltpu.SemaphoreType.DMA((96,)),
        pltpu.SemaphoreType.DMA((96,)),
        pltpu.SemaphoreType.DMA((40,)),
    ]
    scratch += sums_scratch(2, width) + sums_scratch(2, width)
    if owners:
        for shape in (e_shape, r_shape):
            cut = shape[3] * 5 // 128 * 16 if shape[3] > 64 else shape[3] // 2
            scratch += [
                pltpu.VMEM((grp, lines, *shape[3:]), BF16),
                pltpu.VMEM((grp - 1, lines, cut, shape[4]), BF16),
                pltpu.VMEM((lines - 1, grp, shape[3] - cut, shape[4]), BF16),
                pltpu.VMEM((lines - 1, cut, shape[4]), BF16),
                pltpu.VMEM((grp - 1, shape[3] - cut, shape[4]), BF16),
            ]
        narrow = pltpu.VMEM((9 * GW, 128), BF16)
        scratch += [pltpu.VMEM((grp - 1, 9 * GW, BLK), BF16), narrow, narrow, narrow]
        scratch += [pltpu.VMEM((9 * GW, BLK), BF16), narrow, narrow]
        scratch += [pltpu.VMEM((2, 8, 128), F32)] + sums_scratch(8, 128) + sums_scratch(8, 128)
        scratch += [pltpu.VMEM(value.shape, F32) for value in state]
    whole = jax.ShapeDtypeStruct((grp * rows, own_in), BF16)
    return pl.pallas_call(
        functools.partial(backward_kernel, images=rows // HW, owners=owners),
        out_shape=[whole, whole, *parts, *sums, *last],
        in_specs=[hbm] * 14 + [vmem] * 7 + [hbm] * len(state),
        out_specs=[hbm, hbm] + [vmem if owners else hbm] * 3 + [vmem] * (2 + len(last)),
        scratch_shapes=scratch,
        input_output_aliases={0: 0},
        compiler_params=params(collective_id=2, has_side_effects=True),
    )(
        block_out,
        kept["far"],
        kept["inner"],
        *[kept[name] for name in BWD_INS],
        mask,
        n1,
        n2,
        n3,
        norm_all,
        out_all,
        sums3,
        *state,
    )


DECAYS = (0.01, 0.01, 0.01, 0.0, 0.0)


def whole_sum(value):
    return jnp.sum(jnp.sum(value, axis=0, keepdims=True), axis=1, keepdims=True)


def adam_direction(tensor, clipped, moment_one, moment_two, decay_rate):
    new_first = beta_one * moment_one + (1.0 - beta_one) * clipped
    new_second = beta_two * moment_two + (1.0 - beta_two) * clipped * clipped
    first_hat = new_first / (1.0 - beta_one**step_count)
    second_hat = new_second / (1.0 - beta_two**step_count)
    direction = first_hat / (jnp.sqrt(second_hat) + adam_eps) + decay_rate * tensor
    return (new_first, new_second, direction)


def trust(raws, tensors, firsts, seconds, out_ref, pay, one, two, beside=(None,) * 4):
    share = 1.0 / lax.axis_size("batch")
    shares = (1.0, 1.0, 1.0, share, share)
    square = jnp.zeros((1, 1), F32)
    pay[...] = jnp.zeros_like(pay)
    for number in range(5):
        square += shares[number] * whole_sum(raws[number][...] ** 2)
        weight = shares[number] * whole_sum(tensors[number][...] ** 2)
        pay[0, number + 1 : number + 2] = jnp.broadcast_to(weight, (1, 128))
    pay[0, 0:1] = jnp.broadcast_to(square, (1, 128))
    sums = over_devices(pay.at[0], one, add_rows, beside[:2])
    grad_norm = jnp.sqrt(sums[0:1])
    factor = jnp.minimum(1.0, clip_norm / grad_norm)
    for number in range(5):
        direction = adam_direction(
            tensors[number][...],
            factor[0:1, 0:1] * raws[number][...],
            firsts[number][...],
            seconds[number][...],
            DECAYS[number],
        )[2]
        step = shares[number] * whole_sum(direction * direction)
        pay[1, number + 1 : number + 2] = jnp.broadcast_to(step, (1, 128))
    steps = over_devices(pay.at[1], two, add_rows, beside[2:])
    out_ref[...] = jnp.zeros_like(out_ref)
    out_ref[0:1] = grad_norm
    out_ref[1:2] = factor
    out_ref[2:7] = jnp.sqrt(sums[1:6]) * lax.rsqrt(steps[1:6] + 1e-06)


def trust_kernel(*refs):
    raws, tensors, firsts, seconds = (refs[5 * k : 5 * k + 5] for k in range(4))
    greet(everyone())
    greeted(everyone())
    trust(raws, tensors, firsts, seconds, refs[20], refs[21], refs[22:29], refs[29:])


def update_kernel(*refs):
    scalars, results = refs[0], refs[1:3]
    raws, tensors, firsts, seconds = (refs[5 * k + 3 : 5 * k + 8] for k in range(4))
    norm_out, weight_out, rows_out, *refs = refs[23:]
    targets, refs = refs[:2], refs[2:]
    rooms, sems, out_sems = refs[-4:-2], refs[-2], refs[-1]
    outs, held = refs[: len(refs) // 2 - 2], refs[len(refs) // 2 - 2 : -4]
    copies, onward = [], []
    for number, (source, room, target) in enumerate(zip(results, rooms, targets)):
        part = source.shape[0] // 4
        for at in range(4):
            span = pl.ds(at * part, part)
            copies.append(pltpu.make_async_copy(source.at[span], room.at[span], sems.at[0, number, at]))
            onward.append(pltpu.make_async_copy(room.at[span], target.at[span], sems.at[1, number, at]))
            copies[-1].start()
    norm_out[0] = scalars[0, 0]
    at = 0
    for number in range(5):
        trust_ratio = scalars[2 + number, 0]
        if number < 3:
            weight_out[number] = trust_ratio
        else:
            rows_out[number - 3] = trust_ratio
        clipped = scalars[1, 0] * raws[number][...]
        tensor = tensors[number][...]
        new_first, new_second, direction = adam_direction(
            tensor, clipped, firsts[number][...], seconds[number][...], DECAYS[number]
        )
        updated = tensor - learn_rate * trust_ratio * direction
        values = [clipped, new_first, new_second, updated]
        if number < 3:
            values.append(updated.astype(BF16))
        for value in values:
            held[at][...] = value
            onward.append(pltpu.make_async_copy(held[at], outs[at], out_sems.at[at]))
            onward[-1].start()
            at += 1
        if number < 4:
            for copy, after in list(zip(copies, onward))[2 * number : 2 * number + 2]:
                copy.wait()
                after.start()
    for copy in onward:
        copy.wait()


def trust_alone(raws, state):
    vmem = pl.BlockSpec(memory_space=pltpu.VMEM)
    return pl.pallas_call(
        trust_kernel,
        out_shape=jax.ShapeDtypeStruct((8, 128), F32),
        in_specs=[vmem] * 20,
        out_specs=vmem,
        scratch_shapes=[pltpu.VMEM((2, 8, 128), F32)] + sums_scratch(8, 128) + sums_scratch(8, 128),
        compiler_params=params(collective_id=3, has_side_effects=True),
    )(*raws, *state)


def update(scalars, results, raws, state):
    vmem = pl.BlockSpec(memory_space=pltpu.VMEM)
    smem = pl.BlockSpec(memory_space=pltpu.SMEM)
    hbm = pl.BlockSpec(memory_space=pl.ANY)
    shapes = []
    for number, tensor in enumerate(state[:5]):
        shapes += [jax.ShapeDtypeStruct(tensor.shape, F32)] * 4
        if number < 3:
            shapes.append(jax.ShapeDtypeStruct(tensor.shape, BF16))
    outs = pl.pallas_call(
        update_kernel,
        out_shape=[jax.ShapeDtypeStruct((size,), F32) for size in (1, 3, 2)]
        + [jax.ShapeDtypeStruct(result.shape, result.dtype) for result in results]
        + shapes,
        in_specs=[smem, hbm, hbm] + [vmem] * 20,
        out_specs=[smem] * 3 + [hbm] * (2 + len(shapes)),
        scratch_shapes=[pltpu.VMEM(shape.shape, shape.dtype) for shape in shapes]
        + [pltpu.VMEM(result.shape, result.dtype) for result in results]
        + [pltpu.SemaphoreType.DMA((2, 2, 4)), pltpu.SemaphoreType.DMA((len(shapes),))],
        compiler_params=params(),
    )(scalars, *results, *raws, *state)
    return outs[:3], outs[3:5], list(outs[5:])


def local(
    features,
    pixel_mask,
    out_cotangent,
    reduce_master,
    group_master,
    expand_master,
    norm_params,
    out_params,
    reduce_first,
    reduce_second,
    group_first,
    group_second,
    expand_first,
    expand_second,
    norm_first,
    norm_second,
    out_first,
    out_second,
):
    grp, batch = lax.axis_size("grp"), lax.axis_size("batch")
    both = ("grp", "batch")
    me = lax.axis_index("grp")
    rows = features.shape[0] // grp
    images = rows // HW
    own_in = features.shape[1]
    own_width = norm_params.shape[1]
    inside = batch == 8 and own_width == 8 * GW
    valid = lax.dynamic_slice_in_dim(pixel_mask, me * rows, rows, 0).astype(F32).reshape(images, HW)
    state = (
        *(reduce_master, group_master.T, expand_master, norm_params, out_params),
        *(reduce_first, group_first.T, expand_first, norm_first, out_first),
        *(reduce_second, group_second.T, expand_second, norm_second, out_second),
    )
    if inside:
        reduce_w, expand_w, group_w = reduce_master, expand_master, group_master.T
    else:
        reduce_w = lax.all_gather(reduce_master.astype(BF16), both, axis=0, tiled=True)
        expand_w = lax.all_gather(expand_master.astype(BF16), both, axis=0, tiled=True)
        group_w = packed_groups(lax.all_gather(group_master.astype(BF16), both, axis=1, tiled=True))
    kept, block_out, (mask, n1, n2, n3, norm_all, out_all, sums_three) = forward(
        features, out_cotangent, valid, norm_params, out_params, reduce_w, expand_w, group_w, inside
    )
    block_out, input_grad, reduce_part, expand_part, group_part, sums_one, sums_two, *last = backward(
        kept, block_out, mask, n1, n2, n3, norm_all, out_all, sums_three, state if inside else (), inside
    )
    if inside:
        norm_raw, out_raw, scalars = last
        raws = (reduce_part, group_part, expand_part, norm_raw, out_raw)
    else:
        flat = group_part.reshape(9 * GW, grp * batch, -1).transpose(1, 2, 0)
        reduce_part, expand_part, group_part = (
            lax.psum_scatter(value, both, scatter_dimension=0).astype(F32)
            for value in (
                reduce_part.reshape(grp * batch, own_in // batch, -1),
                expand_part.reshape(grp * batch, -1, own_in),
                flat,
            )
        )
        norm_sums = jnp.concatenate([sums_one[1:2], sums_one[0:1], sums_two[1:2], sums_two[0:1]], axis=0)
        norm_raw = lax.dynamic_slice_in_dim(norm_sums, me * own_width, own_width, 1)
        out_sums = jnp.concatenate([sums_three[1:2], sums_three[0:1]], axis=0)
        out_raw = lax.dynamic_slice_in_dim(out_sums, me * own_in, own_in, 1)
        raws = (reduce_part, group_part, expand_part, norm_raw, out_raw)
        scalars = trust_alone(raws, state)
    (grad_norm, weight_trust, norm_trust), results, updates = update(scalars, (block_out, input_grad), raws, state)
    updates[5:10] = [value.T for value in updates[5:10]]
    return (*results, grad_norm.reshape(()), weight_trust, norm_trust, *updates)


def solution(mesh):
    in_specs = (
        P("batch", "grp"),
        P("batch"),
        P("batch", "grp"),
        P(("grp", "batch"), None),
        P(None, ("grp", "batch")),
        P("batch", "grp"),
        P(None, "grp"),
        P(None, "grp"),
        P(("grp", "batch"), None),
        P(("grp", "batch"), None),
        P(None, ("grp", "batch")),
        P(None, ("grp", "batch")),
        P("batch", "grp"),
        P("batch", "grp"),
        P(None, "grp"),
        P(None, "grp"),
        P(None, "grp"),
        P(None, "grp"),
    )
    out_specs = (
        P("batch", "grp"),
        P("batch", "grp"),
        P(),
        P(),
        P(),
        P(("grp", "batch"), None),
        P(("grp", "batch"), None),
        P(("grp", "batch"), None),
        P(("grp", "batch"), None),
        P(("grp", "batch"), None),
        P(None, ("grp", "batch")),
        P(None, ("grp", "batch")),
        P(None, ("grp", "batch")),
        P(None, ("grp", "batch")),
        P(None, ("grp", "batch")),
        P("batch", "grp"),
        P("batch", "grp"),
        P("batch", "grp"),
        P("batch", "grp"),
        P("batch", "grp"),
        P(None, "grp"),
        P(None, "grp"),
        P(None, "grp"),
        P(None, "grp"),
        P(None, "grp"),
        P(None, "grp"),
        P(None, "grp"),
        P(None, "grp"),
    )
    return jax.shard_map(local, mesh=mesh, in_specs=in_specs, out_specs=out_specs, check_vma=False)
```
